32 devices in a mesh: group: 2 (over y), res: 4 (over z), seq: 4 (over x, core).
Axes of the slice: x: 2, y: 2, z: 4, core: 2. Of those that a mesh axis runs over, the one named last changes fastest.
Arguments:
- alignment_features: bfloat16 [256, 64, 256], P(('group', 'seq'), 'res'), parts along dimension 0, may hold values from -6 to 6
- occupancy_flags: int32 [256, 64], P(('group', 'seq'), 'res'), parts along dimension 0, may hold values from 0 to 1
- standardize_scale: float32 [256], replicated, may hold values from 0.1 to 1.9
- standardize_shift: float32 [256], replicated, may hold values from -3 to 3
- first_factor_matrix: bfloat16 [256, 32], replicated, may hold values from -0.375 to 0.375
- first_factor_offset: float32 [32], replicated, may hold values from -3 to 3
- second_factor_matrix: bfloat16 [256, 32], replicated, may hold values from -0.375 to 0.375
- second_factor_offset: float32 [32], replicated, may hold values from -3 to 3
- final_matrix: bfloat16 [1024, 128], replicated, may hold values from -1.75 to 1.75
- final_offset: float32 [128], replicated, may hold values from -256 to 256
Outputs:
- pair: bfloat16 [128, 64, 128], P(('group', 'res'), 'seq'), parts along dimension 0
The draws below stay inside these ranges and needn't reach their ends.
There are 2 independent parts, one for each index of `group`. The reference program is written for one: setup_inputs(seed, part) draws one part's arguments, and reference() takes and returns one part's arrays. A program takes and returns all parts, laid end to end along the dimension named above; an argument that names none is the same for every part. Nothing has to cross between parts.
All inputs are finite; a program needn't handle non-finite values.
Results may differ from the reference program's by a relative error of at most 0.004.
Values may be sent and summed in bfloat16 or wider, within the bound.
No kernel may reach another device: no remote copies, remote signals or barrier semaphores. Data moves between devices by JAX's collectives and lax.ppermute only.
A program may use at most 64 MiB of HBM per device.

```python
import math
import jax
import jax.numpy as jnp
from jax import lax

FEATURE_DEPTH = 256
PROJ_WIDTH = 32
CO = 128
ALIGNED_ROWS = 128
CHAIN_LENGTH = 64


def draw_occupancy_flags(key, part):
    key = jax.random.fold_in(key, 7)
    averaged_products = jax.random.randint(key, (ALIGNED_ROWS, CHAIN_LENGTH), 0, 100)
    rows = jnp.arange(ALIGNED_ROWS, dtype=jnp.int32)
    limit = 90 - 65 * rows // ALIGNED_ROWS
    return (averaged_products < limit[:, None]).astype(jnp.int32)


def block_scale(rng, shape, cuts, low, high):
    def one(dim, blocks):
        steps = jax.random.uniform(jax.random.fold_in(jax.random.fold_in(rng, 6), dim), (blocks,), jnp.float32, low / len(cuts), high / len(cuts))
        return jnp.repeat(jnp.exp(steps), shape[dim] // blocks).reshape((-1,) + (1,) * (len(shape) - dim - 1))

    loudness = one(*cuts[0])
    for cut in cuts[1:]:
        loudness = loudness * one(*cut)
    return loudness


def normal_values(rng, extent, deviation, reach, shards=(), held_as=jnp.bfloat16):
    drawn = deviation * jax.random.normal(rng, extent, jnp.float32)
    if shards:
        drawn = drawn * block_scale(rng, extent, shards, -0.22, 0.18)
    return jnp.clip(drawn, -reach, reach).astype(held_as)


def setup_inputs(seed: int = 0, part: int = 0) -> dict:
    key_of = jax.random.split(jax.random.key(seed), 11)
    own_keys = jax.random.split(jax.random.fold_in(key_of[10], part), 11)
    return {
        "alignment_features": normal_values(own_keys[0], (ALIGNED_ROWS, CHAIN_LENGTH, FEATURE_DEPTH), 1.0, 6.0, ((0, 4), (1, 4))),
        "occupancy_flags": draw_occupancy_flags(jax.random.fold_in(jax.random.fold_in(key_of[10], part), 71), part),
        "standardize_scale": jnp.clip(1.0 + 0.18 * jax.random.normal(key_of[2], (FEATURE_DEPTH,), jnp.float32), 0.1, 1.9),
        "standardize_shift": normal_values(key_of[3], (FEATURE_DEPTH,), 0.5, 3.0, (), jnp.float32),
        "first_factor_matrix": normal_values(key_of[4], (FEATURE_DEPTH, PROJ_WIDTH), FEATURE_DEPTH ** -0.5, 0.375),
        "first_factor_offset": normal_values(key_of[5], (PROJ_WIDTH,), 0.5, 3.0, (), jnp.float32),
        "second_factor_matrix": normal_values(key_of[6], (FEATURE_DEPTH, PROJ_WIDTH), FEATURE_DEPTH ** -0.5, 0.375),
        "second_factor_offset": normal_values(key_of[7], (PROJ_WIDTH,), 0.5, 3.0, (), jnp.float32),
        "final_matrix": normal_values(key_of[8], (PROJ_WIDTH * PROJ_WIDTH, CO), 0.3, 1.75),
        "final_offset": normal_values(key_of[9], (CO,), 40.0, 256.0, (), jnp.float32),
    }


def standardize_features(alignment_features, standardize_scale, standardize_shift):
    averaged_products = alignment_features.astype(jnp.float32)
    center = lax.optimization_barrier(jnp.mean(averaged_products, axis=-1, keepdims=True))
    spread = lax.optimization_barrier(jnp.mean((averaged_products - center) ** 2, axis=-1, keepdims=True))
    return ((averaged_products - center) * lax.rsqrt(spread + 1e-05) * standardize_scale + standardize_shift).astype(jnp.bfloat16)

def reference(alignment_features, occupancy_flags, standardize_scale, standardize_shift, first_factor_matrix, first_factor_offset, second_factor_matrix, second_factor_offset, final_matrix, final_offset):
    valid_entries = occupancy_flags.astype(jnp.float32)
    standardized_alignment = standardize_features(alignment_features, standardize_scale, standardize_shift)
    first_factor = ((jnp.dot(standardized_alignment, first_factor_matrix, preferred_element_type=jnp.float32) + first_factor_offset) * valid_entries[:, :, None]).astype(jnp.bfloat16)
    second_factor = ((jnp.dot(standardized_alignment, second_factor_matrix, preferred_element_type=jnp.float32) + second_factor_offset) * valid_entries[:, :, None]).astype(jnp.bfloat16)
    count = jnp.dot(valid_entries.T, valid_entries, precision=lax.Precision.HIGHEST)
    w_full = final_matrix.astype(jnp.float32)
    width = math.gcd(CHAIN_LENGTH, 16)
    blocks = first_factor.reshape(ALIGNED_ROWS, CHAIN_LENGTH // width, width, PROJ_WIDTH).transpose(1, 0, 2, 3)
    right_full = second_factor.astype(jnp.float32)

    def one_block(block):
        outer = jnp.einsum('sic,sje->ijce', block.astype(jnp.float32), right_full, precision=lax.Precision.HIGHEST)
        flat = outer.reshape(width * CHAIN_LENGTH, PROJ_WIDTH * PROJ_WIDTH)
        return jnp.dot(flat, w_full, precision=lax.Precision.HIGHEST).reshape(width, CHAIN_LENGTH, CO)
    raw = lax.map(one_block, blocks).reshape(CHAIN_LENGTH, CHAIN_LENGTH, CO)
    return ((raw + final_offset) / (1.0 + count)[:, :, None]).astype(jnp.bfloat16)
```

```python
import functools

import jax
import jax.numpy as jnp
from jax import lax
from jax.experimental import pallas as pl
from jax.experimental.pallas import tpu as pltpu
from jax.sharding import PartitionSpec as P

LANES = 128
F32 = jnp.float32
BF16 = jnp.bfloat16
TN = (((0,), (0,)), ((), ()))
NT = (((1,), (1,)), ((), ()))
NN = (((1,), (0,)), ((), ()))


def dot(a, b, dims=NN):
    return lax.dot_general(a, b, dims, preferred_element_type=F32)


def iota(shape, dim):
    return lax.broadcasted_iota(jnp.int32, shape, dim)


def project_kernel(x_ref, flag_ref, scale_ref, shift_ref, wl_ref, bl_ref, wr_ref, br_ref,
                   left_ref, right_ref, proj_ref):
    seqs, rows, depth = x_ref.shape
    width = wl_ref.shape[0]
    fold = LANES // width
    lanes = rows * width

    x = x_ref[...].astype(F32).reshape(seqs * rows, depth)
    center = jnp.mean(x, axis=-1, keepdims=True)
    x = x - center
    spread = jnp.mean(x * x, axis=-1, keepdims=True)
    normed = x * lax.rsqrt(spread + 1e-05) * scale_ref[...].reshape(1, depth)
    normed = (normed + shift_ref[...].reshape(1, depth)).astype(BF16)
    weight = jnp.concatenate([wl_ref[...]] * fold + [wr_ref[...]] * fold, axis=0)
    bias = jnp.concatenate([bl_ref[...].reshape(1, width)] * fold + [br_ref[...].reshape(1, width)] * fold, axis=1)
    both = dot(normed, weight, NT) + bias
    proj_ref[0] = both[:, :LANES]
    proj_ref[1] = both[:, LANES:]

    lane = iota((rows, lanes + LANES), 1)
    residue = jnp.where(lane < lanes, lane // width, lane - lanes)
    spreader = (residue == iota((rows, lanes + LANES), 0)).astype(BF16)
    mask = dot(flag_ref[...].astype(BF16), spreader, TN)

    place = iota((seqs, LANES), 1) // width
    for half, out_ref in ((0, left_ref), (1, right_ref)):
        for tile in range(rows // fold):
            merged = proj_ref[half, pl.ds(tile * fold, seqs, stride=rows), :]
            for k in range(1, fold):
                part = proj_ref[half, pl.ds(tile * fold + k, seqs, stride=rows), :]
                merged = jnp.where(place == k, part, merged)
            where = slice(tile * LANES, (tile + 1) * LANES)
            out_ref[:, where] = (merged * mask[:, where]).astype(BF16)
        out_ref[:, lanes:] = mask[:, lanes:].astype(BF16)


def pair_kernel(count_of, rows, columns, width, *refs):
    lefts, rights = refs[:count_of], refs[count_of:2 * count_of]
    w_ref, bias_ref, out_ref, left_ref, right_ref, outer_ref, flat_ref, raw_ref = refs[2 * count_of:]
    seqs = lefts[0].shape[0]
    fold = LANES // width
    lanes = rows * width

    me_res, me_seq = lax.axis_index("res"), lax.axis_index("seq")
    for k in range(count_of):
        at = pl.multiple_of(lax.rem(me_seq + count_of - k, count_of) * seqs, seqs)
        left_ref[pl.ds(at, seqs), :] = lefts[k][...]
        at = pl.multiple_of(lax.rem(me_res + count_of - k, count_of) * seqs, seqs)
        right_ref[pl.ds(at, seqs), :] = rights[k][...]

    outer = dot(left_ref[:, :lanes], right_ref[:, :lanes], TN)
    for tile in range(columns // fold):
        outer_ref[tile] = outer[:, tile * LANES:(tile + 1) * LANES]

    place = iota((rows, LANES), 1) // width
    for tile in range(columns // fold):
        for quad in range(width // fold):
            part = [
                outer_ref[tile, pl.ds(quad * fold + k, rows, stride=width), :]
                for k in range(fold)
            ]
            step = fold // 2
            while step:
                keep = (place // step) % 2 == 0
                new = list(part)
                for k in range(fold):
                    if (k // step) % 2 == 0:
                        a, b = part[k], part[k + step]
                        new[k] = jnp.where(keep, a, pltpu.roll(b, step * width, 1))
                        new[k + step] = jnp.where(keep, pltpu.roll(a, LANES - step * width, 1), b)
                part = new
                step //= 2
            for k in range(fold):
                j = tile * fold + k
                flat_ref[j * rows:(j + 1) * rows, quad * LANES:(quad + 1) * LANES] = part[k].astype(BF16)

    raw = dot(flat_ref[...], w_ref[...]) + bias_ref[...].reshape(1, -1)

    pair = rows * columns
    lane, sub = iota((LANES, pair), 1), iota((LANES, pair), 0)
    live_left = dot(left_ref[:, lanes:], (lane % rows == sub).astype(BF16))
    live_right = dot(right_ref[:, lanes:], (lane // rows == sub).astype(BF16))
    both = (live_left * live_right).astype(BF16)
    count = dot(both, jnp.ones((both.shape[0], raw.shape[1]), BF16), TN)
    raw_ref[...] = raw / (1.0 + count)
    for i in range(rows):
        out_ref[i] = raw_ref[pl.ds(i, columns, stride=rows), :].astype(BF16)


def local(n, x, flags, scale, shift, wl, bl, wr, br, w, bias):
    seqs, rows, depth = x.shape
    width = wl.shape[1]
    outs = w.shape[1]
    lanes = rows * width
    wire = jax.ShapeDtypeStruct((seqs, lanes + LANES), BF16)
    left, right = pl.pallas_call(
        project_kernel,
        out_shape=(wire, wire),
        scratch_shapes=[pltpu.VMEM((2, seqs * rows, LANES), F32)],
        compiler_params=pltpu.CompilerParams(vmem_limit_bytes=16 << 20),
        name="project",
    )(x, flags.T, scale, shift, wl.T, bl, wr.T, br)

    lefts = [left] + [
        lax.ppermute(left, "seq", [(p, (p + k) % n) for p in range(n)]) for k in range(1, n)
    ]
    rights = [
        lax.ppermute(
            right, ("res", "seq"),
            [(a * n + p, (p + k) % n * n + a) for a in range(n) for p in range(n)],
        )
        for k in range(n)
    ]
    return pl.pallas_call(
        functools.partial(pair_kernel, n, rows, rows, width),
        out_shape=jax.ShapeDtypeStruct((rows, rows, outs), BF16),
        scratch_shapes=[
            pltpu.VMEM((n * seqs, lanes + LANES), BF16),
            pltpu.VMEM((n * seqs, lanes + LANES), BF16),
            pltpu.VMEM((lanes // LANES, lanes, LANES), F32),
            pltpu.VMEM((rows * rows, width * width), BF16),
            pltpu.VMEM((rows * rows, outs), F32),
        ],
        compiler_params=pltpu.CompilerParams(vmem_limit_bytes=24 << 20),
        name="pair",
    )(*lefts, *rights, w, bias)


def solution(mesh):
    n = mesh.shape["res"]
    assert n == mesh.shape["seq"]
    in_specs = (P(("group", "seq"), "res", None), P(("group", "seq"), "res")) + (P(),) * 8
    return jax.shard_map(
        functools.partial(local, n), mesh=mesh, in_specs=in_specs,
        out_specs=P(("group", "res"), "seq", None), check_vma=False,
    )
```

```python
import functools

import jax
import jax.numpy as jnp
from jax import lax
from jax.experimental import pallas as pl
from jax.experimental.pallas import tpu as pltpu
from jax.sharding import PartitionSpec as P

LANES = 128
F32 = jnp.float32
BF16 = jnp.bfloat16
TN = (((0,), (0,)), ((), ()))
NT = (((1,), (1,)), ((), ()))
NN = (((1,), (0,)), ((), ()))


def dot(a, b, dims=NN):
    return lax.dot_general(a, b, dims, preferred_element_type=F32)


def iota(shape, dim):
    return lax.broadcasted_iota(jnp.int32, shape, dim)


def project_kernel(x_hbm, flag_hbm, scale_hbm, shift_hbm, wl_hbm, bl_hbm, wr_hbm, br_hbm,
                   left_ref, right_ref,
                   x_ref, flag_ref, scale_ref, shift_ref, wl_ref, bl_ref, wr_ref, br_ref, proj_ref, sems):
    copies = [
        pltpu.make_async_copy(src, dst, sems.at[k])
        for k, (src, dst) in enumerate((
            (x_hbm, x_ref), (flag_hbm, flag_ref), (scale_hbm, scale_ref), (shift_hbm, shift_ref),
            (wl_hbm, wl_ref), (bl_hbm, bl_ref), (wr_hbm, wr_ref), (br_hbm, br_ref),
        ))
    ]
    for copy in copies:
        copy.start()
    seqs, rows, depth = x_ref.shape
    width = wl_ref.shape[0]
    fold = LANES // width
    lanes = rows * width
    data = lanes // LANES * seqs
    for copy in copies:
        copy.wait()

    x = x_ref[...].astype(F32).reshape(seqs * rows, depth)
    center = jnp.mean(x, axis=-1, keepdims=True)
    x = x - center
    spread = jnp.mean(x * x, axis=-1, keepdims=True)
    normed = x * lax.rsqrt(spread + 1e-05) * scale_ref[...].reshape(1, depth)
    normed = (normed + shift_ref[...].reshape(1, depth)).astype(BF16)
    weight = jnp.concatenate([wl_ref[...]] * fold + [wr_ref[...]] * fold, axis=0)
    bias = jnp.concatenate([bl_ref[...].reshape(1, width)] * fold + [br_ref[...].reshape(1, width)] * fold, axis=1)
    both = dot(normed, weight, NT) + bias
    proj_ref[0] = both[:, :LANES]
    proj_ref[1] = both[:, LANES:]

    flags = flag_ref[...].astype(F32)
    spreader = (iota((rows, lanes), 1) // width == iota((rows, lanes), 0)).astype(BF16)
    mask = dot(flags.astype(BF16), spreader, TN)
    flags = jnp.concatenate([flags, jnp.zeros((rows, LANES - seqs), F32)], axis=1).astype(BF16)

    place = iota((seqs, LANES), 1) // width
    for half, out_ref in ((0, left_ref), (1, right_ref)):
        for tile in range(rows // fold):
            merged = proj_ref[half, pl.ds(tile * fold, seqs, stride=rows), :]
            for k in range(1, fold):
                part = proj_ref[half, pl.ds(tile * fold + k, seqs, stride=rows), :]
                merged = jnp.where(place == k, part, merged)
            merged = merged * mask[:, tile * LANES:(tile + 1) * LANES]
            out_ref[tile * seqs:(tile + 1) * seqs, :] = merged.astype(BF16)
        out_ref[data:, :] = flags


def whole_factor(pieces, seqs, data):
    return jnp.concatenate(
        [
            jnp.concatenate([p[t * seqs:(t + 1) * seqs, :] for t in range(data // seqs)], axis=1)
            for p in pieces
        ],
        axis=0,
    )


def whole_mask(pieces, seqs, data):
    each = LANES // seqs
    tiles = []
    for first in range(0, len(pieces), each):
        total = pieces[first][data:, :].astype(F32)
        for k in range(1, min(each, len(pieces) - first)):
            total = total + pltpu.roll(pieces[first + k][data:, :].astype(F32), k * seqs, 1)
        tiles.append(total)
    return jnp.concatenate(tiles, axis=1).astype(BF16)


def pair_kernel(pieces, seqs, rows, columns, width, *refs):
    lefts, rights = refs[:pieces], refs[pieces:2 * pieces]
    w_ref, bias_ref, out_ref, outer_ref, flat_ref, raw_ref = refs[2 * pieces:]
    fold = LANES // width
    data = rows * width // LANES * seqs

    outer = dot(whole_factor(lefts, seqs, data), whole_factor(rights, seqs, data), TN)
    for tile in range(columns // fold):
        outer_ref[tile] = outer[:, tile * LANES:(tile + 1) * LANES]

    place = iota((rows, LANES), 1) // width
    for tile in range(columns // fold):
        for quad in range(width // fold):
            part = [
                outer_ref[tile, pl.ds(quad * fold + k, rows, stride=width), :]
                for k in range(fold)
            ]
            step = fold // 2
            while step:
                keep = (place // step) % 2 == 0
                new = list(part)
                for k in range(fold):
                    if (k // step) % 2 == 0:
                        a, b = part[k], part[k + step]
                        new[k] = jnp.where(keep, a, pltpu.roll(b, step * width, 1))
                        new[k + step] = jnp.where(keep, pltpu.roll(a, LANES - step * width, 1), b)
                part = new
                step //= 2
            for k in range(fold):
                j = tile * fold + k
                flat_ref[j * rows:(j + 1) * rows, quad * LANES:(quad + 1) * LANES] = part[k].astype(BF16)

    raw = dot(flat_ref[...], w_ref[...]) + bias_ref[...].reshape(1, -1)

    pair = rows * columns
    row = iota((pair, rows), 0)
    live_left = dot((row % rows == iota((pair, rows), 1)).astype(BF16), whole_mask(lefts, seqs, data))
    row = iota((pair, columns), 0)
    live_right = dot((row // rows == iota((pair, columns), 1)).astype(BF16), whole_mask(rights, seqs, data))
    count = jnp.sum(live_left * live_right, axis=1, keepdims=True)
    raw_ref[...] = raw / (1.0 + count)
    for i in range(rows):
        out_ref[i] = raw_ref[pl.ds(i, columns, stride=rows), :].astype(BF16)


def local(n, x, flags, scale, shift, wl, bl, wr, br, w, bias):
    seqs, rows, depth = x.shape
    width = wl.shape[1]
    outs = w.shape[1]
    lanes = rows * width
    data = lanes // LANES * seqs
    operands = (x, flags.T, scale, shift, wl.T, bl, wr.T, br)
    wire = jax.ShapeDtypeStruct((data + rows, LANES), BF16)
    left, right = pl.pallas_call(
        project_kernel,
        out_shape=(wire, wire),
        in_specs=[pl.BlockSpec(memory_space=pltpu.HBM)] * len(operands),
        scratch_shapes=[pltpu.VMEM(o.shape, o.dtype) for o in operands] + [
            pltpu.VMEM((2, seqs * rows, LANES), F32),
            pltpu.SemaphoreType.DMA((len(operands),)),
        ],
        compiler_params=pltpu.CompilerParams(vmem_limit_bytes=16 << 20),
        name="project",
    )(*operands)

    other = (lambda a, b, m: a ^ b ^ m) if n & (n - 1) == 0 else (lambda a, b, m: (m - a - b) % n)
    both = [(a, b) for a in range(n) for b in range(n)]
    along_res = [[(a * n + b, other(a, b, m) * n + b) for a, b in both] for m in range(n)]
    along_seq = [[(a * n + b, a * n + other(a, b, m)) for a, b in both] for m in range(n)]
    axes = ("res", "seq")
    brought = [lax.ppermute(right, axes, pairs) for pairs in along_res]
    lefts = [lax.ppermute(left, axes, pairs) for pairs in along_seq]
    rights = [lax.ppermute(block, axes, pairs) for block, pairs in zip(brought, along_seq)]
    return pl.pallas_call(
        functools.partial(pair_kernel, n, seqs, rows, rows, width),
        out_shape=jax.ShapeDtypeStruct((rows, rows, outs), BF16),
        scratch_shapes=[
            pltpu.VMEM((lanes // LANES, lanes, LANES), F32),
            pltpu.VMEM((rows * rows, width * width), BF16),
            pltpu.VMEM((rows * rows, outs), F32),
        ],
        compiler_params=pltpu.CompilerParams(vmem_limit_bytes=24 << 20),
        name="pair",
    )(*lefts, *rights, w, bias)


def solution(mesh):
    n = mesh.shape["res"]
    assert n == mesh.shape["seq"]
    in_specs = (P(("group", "seq"), "res", None), P(("group", "seq"), "res")) + (P(),) * 8
    return jax.shard_map(
        functools.partial(local, n), mesh=mesh, in_specs=in_specs,
        out_specs=P(("group", "res"), "seq", None), check_vma=False,
    )
```

```python
import functools

import jax
import jax.numpy as jnp
from jax import lax
from jax.experimental import pallas as pl
from jax.experimental.pallas import tpu as pltpu
from jax.sharding import PartitionSpec as P

LANES = 128
F32 = jnp.float32
BF16 = jnp.bfloat16
TN = (((0,), (0,)), ((), ()))
NT = (((1,), (1,)), ((), ()))
NN = (((1,), (0,)), ((), ()))


def dot(a, b, dims=NN):
    return lax.dot_general(a, b, dims, preferred_element_type=F32)


def iota(shape, dim):
    return lax.broadcasted_iota(jnp.int32, shape, dim)


def project_kernel(x_hbm, flag_hbm, scale_hbm, shift_hbm, wl_hbm, bl_hbm, wr_hbm, br_hbm,
                   left_ref, right_ref,
                   x_ref, flag_ref, scale_ref, shift_ref, wl_ref, bl_ref, wr_ref, br_ref, proj_ref, sems):
    copies = [
        pltpu.make_async_copy(src, dst, sems.at[k])
        for k, (src, dst) in enumerate((
            (x_hbm, x_ref), (flag_hbm, flag_ref), (scale_hbm, scale_ref), (shift_hbm, shift_ref),
            (wl_hbm, wl_ref), (bl_hbm, bl_ref), (wr_hbm, wr_ref), (br_hbm, br_ref),
        ))
    ]
    for copy in copies:
        copy.start()
    seqs, rows, depth = x_ref.shape
    width = wl_ref.shape[0]
    fold = LANES // width
    lanes = rows * width
    data = lanes // LANES * seqs
    for copy in copies:
        copy.wait()

    x = x_ref[...].astype(F32).reshape(seqs * rows, depth)
    center = jnp.mean(x, axis=-1, keepdims=True)
    x = x - center
    spread = jnp.mean(x * x, axis=-1, keepdims=True)
    normed = x * lax.rsqrt(spread + 1e-05) * scale_ref[...].reshape(1, depth)
    normed = (normed + shift_ref[...].reshape(1, depth)).astype(BF16)
    weight = jnp.concatenate([wl_ref[...]] * fold + [wr_ref[...]] * fold, axis=0)
    bias = jnp.concatenate([bl_ref[...].reshape(1, width)] * fold + [br_ref[...].reshape(1, width)] * fold, axis=1)
    both = dot(normed, weight, NT) + bias
    proj_ref[0] = both[:, :LANES]
    proj_ref[1] = both[:, LANES:]

    flags = flag_ref[...].astype(F32)
    spreader = (iota((rows, lanes), 1) // width == iota((rows, lanes), 0)).astype(BF16)
    mask = dot(flags.astype(BF16), spreader, TN)
    flags = jnp.concatenate([flags] * (LANES // seqs), axis=1)
    block = iota((rows, LANES), 1) // seqs
    me = lax.axis_index("seq")

    place = iota((seqs, LANES), 1) // width
    for half, out_ref in ((0, left_ref), (1, right_ref)):
        for tile in range(rows // fold):
            merged = proj_ref[half, pl.ds(tile * fold, seqs, stride=rows), :]
            for k in range(1, fold):
                part = proj_ref[half, pl.ds(tile * fold + k, seqs, stride=rows), :]
                merged = jnp.where(place == k, part, merged)
            merged = merged * mask[:, tile * LANES:(tile + 1) * LANES]
            out_ref[tile * seqs:(tile + 1) * seqs, :] = merged.astype(BF16)
        for tile in range((out_ref.shape[0] - data) // rows):
            mine = jnp.where(block + tile * (LANES // seqs) == me, flags, 0.0)
            out_ref[data + tile * rows:data + (tile + 1) * rows, :] = mine.astype(BF16)


def whole_mask(pieces, rows, data):
    total = functools.reduce(jnp.add, [p[data:, :] for p in pieces])
    return jnp.concatenate([total[k:k + rows] for k in range(0, total.shape[0], rows)], axis=1)


def pair_kernel(n, seqs, rows, columns, width, *refs):
    lefts, rights, own_ref = refs[:n], refs[n:2 * n], refs[2 * n]
    w_ref, bias_ref, out_ref, left_ref, right_ref, outer_ref, flat_ref, raw_ref = refs[2 * n + 1:]
    fold = LANES // width
    data = rows * width // LANES * seqs

    me_res, me_seq = lax.axis_index("res"), lax.axis_index("seq")
    rights = [jnp.where(me_res == me_seq, own_ref[...], rights[0][...])] + list(rights[1:])
    for k in range(n):
        for pieces, me, whole_ref in ((lefts, me_seq, left_ref), (rights, me_res, right_ref)):
            at = pl.multiple_of((me ^ k) * seqs, seqs)
            for tile in range(data // seqs):
                whole_ref[pl.ds(at, seqs), tile * LANES:(tile + 1) * LANES] = pieces[k][tile * seqs:(tile + 1) * seqs, :]

    outer = dot(left_ref[...], right_ref[...], TN)
    for tile in range(columns // fold):
        outer_ref[tile] = outer[:, tile * LANES:(tile + 1) * LANES]

    place = iota((rows, LANES), 1) // width
    for tile in range(columns // fold):
        for quad in range(width // fold):
            part = [
                outer_ref[tile, pl.ds(quad * fold + k, rows, stride=width), :]
                for k in range(fold)
            ]
            step = fold // 2
            while step:
                keep = (place // step) % 2 == 0
                new = list(part)
                for k in range(fold):
                    if (k // step) % 2 == 0:
                        a, b = part[k], part[k + step]
                        new[k] = jnp.where(keep, a, pltpu.roll(b, step * width, 1))
                        new[k + step] = jnp.where(keep, pltpu.roll(a, LANES - step * width, 1), b)
                part = new
                step //= 2
            for k in range(fold):
                j = tile * fold + k
                flat_ref[j * rows:(j + 1) * rows, quad * LANES:(quad + 1) * LANES] = part[k].astype(BF16)

    raw = dot(flat_ref[...], w_ref[...]) + bias_ref[...].reshape(1, -1)

    pair = rows * columns
    row = iota((pair, rows), 0)
    live_left = dot((row % rows == iota((pair, rows), 1)).astype(BF16), whole_mask(lefts, rows, data))
    row = iota((pair, columns), 0)
    live_right = dot((row // rows == iota((pair, columns), 1)).astype(BF16), whole_mask(rights, rows, data))
    count = jnp.sum(live_left * live_right, axis=1, keepdims=True)
    raw_ref[...] = raw / (1.0 + count)
    for i in range(rows):
        out_ref[i] = raw_ref[pl.ds(i, columns, stride=rows), :].astype(BF16)


def local(n, x, flags, scale, shift, wl, bl, wr, br, w, bias):
    seqs, rows, depth = x.shape
    width = wl.shape[1]
    outs = w.shape[1]
    lanes = rows * width
    data = lanes // LANES * seqs
    operands = [
        pltpu.with_memory_space_constraint(o, pltpu.HBM)
        for o in (x, flags.T, scale, shift, wl.T, bl, wr.T, br)
    ]
    wire = jax.ShapeDtypeStruct((data + rows * pl.cdiv(n * seqs, LANES), LANES), BF16)
    left, right = pl.pallas_call(
        project_kernel,
        out_shape=(wire, wire),
        in_specs=[pl.BlockSpec(memory_space=pltpu.HBM)] * len(operands),
        scratch_shapes=[pltpu.VMEM(o.shape, o.dtype) for o in operands] + [
            pltpu.VMEM((2, seqs * rows, LANES), F32),
            pltpu.SemaphoreType.DMA((len(operands),)),
        ],
        compiler_params=pltpu.CompilerParams(vmem_limit_bytes=16 << 20),
        name="project",
    )(*operands)

    axes = ("res", "seq")
    rights = []
    for k in range(n):
        pairs = []
        for a in range(n):
            for p in range(n):
                r = p ^ k
                to = ((a + 1) % n, (a + 1) % n) if (r, a) == (a, p) else (r, a)
                pairs.append((a * n + p, to[0] * n + to[1]))
        rights.append(lax.ppermute(right, axes, pairs))
    lefts = [left] + [lax.ppermute(left, "seq", [(p, p ^ k) for p in range(n)]) for k in range(1, n)]
    return pl.pallas_call(
        functools.partial(pair_kernel, n, seqs, rows, rows, width),
        out_shape=jax.ShapeDtypeStruct((rows, rows, outs), BF16),
        scratch_shapes=[
            pltpu.VMEM((n * seqs, lanes), BF16),
            pltpu.VMEM((n * seqs, lanes), BF16),
            pltpu.VMEM((lanes // LANES, lanes, LANES), F32),
            pltpu.VMEM((rows * rows, width * width), BF16),
            pltpu.VMEM((rows * rows, outs), F32),
        ],
        compiler_params=pltpu.CompilerParams(vmem_limit_bytes=24 << 20),
        name="pair",
    )(*lefts, *rights, right, w, bias)


def solution(mesh):
    n = mesh.shape["res"]
    assert n == mesh.shape["seq"] and n & (n - 1) == 0
    in_specs = (P(("group", "seq"), "res", None), P(("group", "seq"), "res")) + (P(),) * 8
    return jax.shard_map(
        functools.partial(local, n), mesh=mesh, in_specs=in_specs,
        out_specs=P(("group", "res"), "seq", None), check_vma=False,
    )
```

```python
import functools

import jax
import jax.numpy as jnp
from jax import lax
from jax.experimental import pallas as pl
from jax.experimental.pallas import tpu as pltpu
from jax.sharding import PartitionSpec as P

LANES = 128
F32 = jnp.float32
BF16 = jnp.bfloat16
TN = (((0,), (0,)), ((), ()))
NT = (((1,), (1,)), ((), ()))
NN = (((1,), (0,)), ((), ()))


def dot(a, b, dims=NN):
    return lax.dot_general(a, b, dims, preferred_element_type=F32)


def iota(shape, dim):
    return lax.broadcasted_iota(jnp.int32, shape, dim)


def project_kernel(x_hbm, flag_hbm, scale_hbm, shift_hbm, wl_hbm, bl_hbm, wr_hbm, br_hbm,
                   both_ref,
                   x_ref, flag_ref, scale_ref, shift_ref, wl_ref, bl_ref, wr_ref, br_ref, proj_ref, sems):
    copies = [
        pltpu.make_async_copy(src, dst, sems.at[k])
        for k, (src, dst) in enumerate((
            (x_hbm, x_ref), (flag_hbm, flag_ref), (scale_hbm, scale_ref), (shift_hbm, shift_ref),
            (wl_hbm, wl_ref), (bl_hbm, bl_ref), (wr_hbm, wr_ref), (br_hbm, br_ref),
        ))
    ]
    for copy in copies:
        copy.start()
    seqs, rows, depth = x_ref.shape
    width = wl_ref.shape[0]
    fold = LANES // width
    lanes = rows * width
    data = lanes // LANES * seqs
    for copy in copies:
        copy.wait()

    x = x_ref[...].astype(F32).reshape(seqs * rows, depth)
    center = jnp.mean(x, axis=-1, keepdims=True)
    x = x - center
    spread = jnp.mean(x * x, axis=-1, keepdims=True)
    normed = x * lax.rsqrt(spread + 1e-05) * scale_ref[...].reshape(1, depth)
    normed = (normed + shift_ref[...].reshape(1, depth)).astype(BF16)
    weight = jnp.concatenate([wl_ref[...]] * fold + [wr_ref[...]] * fold, axis=0)
    bias = jnp.concatenate([bl_ref[...].reshape(1, width)] * fold + [br_ref[...].reshape(1, width)] * fold, axis=1)
    both = dot(normed, weight, NT) + bias
    proj_ref[0] = both[:, :LANES]
    proj_ref[1] = both[:, LANES:]

    flags = flag_ref[...].astype(F32)
    spreader = (iota((rows, lanes), 1) // width == iota((rows, lanes), 0)).astype(BF16)
    mask = dot(flags.astype(BF16), spreader, TN)
    flags = jnp.concatenate([flags] * (LANES // seqs), axis=1)
    block = iota((rows, LANES), 1) // seqs
    me = lax.axis_index("seq")

    place = iota((seqs, LANES), 1) // width
    size = both_ref.shape[0] // 2
    for half in range(2):
        out_ref = both_ref.at[half * size:(half + 1) * size]
        for tile in range(rows // fold):
            merged = proj_ref[half, pl.ds(tile * fold, seqs, stride=rows), :]
            for k in range(1, fold):
                part = proj_ref[half, pl.ds(tile * fold + k, seqs, stride=rows), :]
                merged = jnp.where(place == k, part, merged)
            merged = merged * mask[:, tile * LANES:(tile + 1) * LANES]
            out_ref[tile * seqs:(tile + 1) * seqs, :] = merged.astype(BF16)
        for tile in range((out_ref.shape[0] - data) // rows):
            mine = jnp.where(block + tile * (LANES // seqs) == me, flags, 0.0)
            out_ref[data + tile * rows:data + (tile + 1) * rows, :] = mine.astype(BF16)


def whole_mask(pieces, rows, data):
    total = functools.reduce(jnp.add, [p[data:, :] for p in pieces])
    return jnp.concatenate([total[k:k + rows] for k in range(0, total.shape[0], rows)], axis=1)


def pair_kernel(n, seqs, rows, columns, width, all_ref, w_ref, bias_ref, out_ref, outer_ref, flat_ref, raw_ref):
    fold = LANES // width
    data = rows * width // LANES * seqs
    size = all_ref.shape[0] // (2 * n * n)

    def pieces(block, half):
        at = [pl.multiple_of(((block * n + p) * 2 + half) * size, size) for p in range(n)]
        return [all_ref[pl.ds(k, size), :] for k in at]

    def factor(pieces):
        return jnp.concatenate(
            [
                jnp.concatenate([p[t * seqs:(t + 1) * seqs] for t in range(data // seqs)], axis=1)
                for p in pieces
            ],
            axis=0,
        )

    lefts, rights = pieces(lax.axis_index("res"), 0), pieces(lax.axis_index("seq"), 1)
    outer = dot(factor(lefts), factor(rights), TN)
    for tile in range(columns // fold):
        outer_ref[tile] = outer[:, tile * LANES:(tile + 1) * LANES]

    place = iota((rows, LANES), 1) // width
    for tile in range(columns // fold):
        for quad in range(width // fold):
            part = [
                outer_ref[tile, pl.ds(quad * fold + k, rows, stride=width), :]
                for k in range(fold)
            ]
            step = fold // 2
            while step:
                keep = (place // step) % 2 == 0
                new = list(part)
                for k in range(fold):
                    if (k // step) % 2 == 0:
                        a, b = part[k], part[k + step]
                        new[k] = jnp.where(keep, a, pltpu.roll(b, step * width, 1))
                        new[k + step] = jnp.where(keep, pltpu.roll(a, LANES - step * width, 1), b)
                part = new
                step //= 2
            for k in range(fold):
                j = tile * fold + k
                flat_ref[j * rows:(j + 1) * rows, quad * LANES:(quad + 1) * LANES] = part[k].astype(BF16)

    raw = dot(flat_ref[...], w_ref[...]) + bias_ref[...].reshape(1, -1)

    pair = rows * columns
    row = iota((pair, rows), 0)
    live_left = dot((row % rows == iota((pair, rows), 1)).astype(BF16), whole_mask(lefts, rows, data))
    row = iota((pair, columns), 0)
    live_right = dot((row // rows == iota((pair, columns), 1)).astype(BF16), whole_mask(rights, rows, data))
    count = jnp.sum(live_left * live_right, axis=1, keepdims=True)
    raw_ref[...] = raw / (1.0 + count)
    for i in range(rows):
        out_ref[i] = raw_ref[pl.ds(i, columns, stride=rows), :].astype(BF16)


def local(n, x, flags, scale, shift, wl, bl, wr, br, w, bias):
    seqs, rows, depth = x.shape
    width = wl.shape[1]
    outs = w.shape[1]
    lanes = rows * width
    data = lanes // LANES * seqs
    operands = [
        pltpu.with_memory_space_constraint(o, pltpu.HBM)
        for o in (x, flags.T, scale, shift, wl.T, bl, wr.T, br)
    ]
    wire = jax.ShapeDtypeStruct((2 * (data + rows * pl.cdiv(n * seqs, LANES)), LANES), BF16)
    both = pl.pallas_call(
        project_kernel,
        out_shape=wire,
        in_specs=[pl.BlockSpec(memory_space=pltpu.HBM)] * len(operands),
        scratch_shapes=[pltpu.VMEM(o.shape, o.dtype) for o in operands] + [
            pltpu.VMEM((2, seqs * rows, LANES), F32),
            pltpu.SemaphoreType.DMA((len(operands),)),
        ],
        compiler_params=pltpu.CompilerParams(vmem_limit_bytes=16 << 20),
        name="project",
    )(*operands)

    gathered = lax.all_gather(both, ("res", "seq"), axis=0, tiled=True)
    return pl.pallas_call(
        functools.partial(pair_kernel, n, seqs, rows, rows, width),
        out_shape=jax.ShapeDtypeStruct((rows, rows, outs), BF16),
        scratch_shapes=[
            pltpu.VMEM((lanes // LANES, lanes, LANES), F32),
            pltpu.VMEM((rows * rows, width * width), BF16),
            pltpu.VMEM((rows * rows, outs), F32),
        ],
        compiler_params=pltpu.CompilerParams(vmem_limit_bytes=24 << 20),
        name="pair",
    )(gathered, w, bias)


def solution(mesh):
    n = mesh.shape["res"]
    assert n == mesh.shape["seq"] and n & (n - 1) == 0
    in_specs = (P(("group", "seq"), "res", None), P(("group", "seq"), "res")) + (P(),) * 8
    return jax.shard_map(
        functools.partial(local, n), mesh=mesh, in_specs=in_specs,
        out_specs=P(("group", "res"), "seq", None), check_vma=False,
    )
```

```python
import functools

import jax
import jax.numpy as jnp
from jax import lax
from jax.experimental import pallas as pl
from jax.experimental.pallas import tpu as pltpu
from jax.sharding import PartitionSpec as P

LANES = 128
CORES = 2
F32 = jnp.float32
BF16 = jnp.bfloat16
TN = (((0,), (0,)), ((), ()))
NT = (((1,), (1,)), ((), ()))
NN = (((1,), (0,)), ((), ()))


def dot(a, b, dims=NN):
    return lax.dot_general(a, b, dims, preferred_element_type=F32)


def iota(shape, dim):
    return lax.broadcasted_iota(jnp.int32, shape, dim)


def project_block(width, x_ref, flag_ref, weight, vectors, block, left_ref, right_ref, proj_ref):
    seqs, rows, depth = x_ref.shape
    fold = LANES // width
    lanes = rows * width
    data = lanes // LANES * seqs
    x = x_ref[...].astype(F32).reshape(seqs * rows, depth)
    center = jnp.mean(x, axis=-1, keepdims=True)
    x = x - center
    spread = jnp.mean(x * x, axis=-1, keepdims=True)
    normed = x * lax.rsqrt(spread + 1e-05) * vectors[0:1] + vectors[1:2]
    both = dot(normed.astype(BF16), weight, NT) + vectors[2:3]
    proj_ref[0] = both[:, :LANES]
    proj_ref[1] = both[:, LANES:]

    flags = flag_ref[...].astype(F32)
    spreader = (iota((rows, lanes), 1) // width == iota((rows, lanes), 0)).astype(BF16)
    mask = dot(flags.astype(BF16), spreader, TN)
    flags = jnp.concatenate([flags] * (LANES // seqs), axis=1)
    lane_block = iota((rows, LANES), 1) // seqs

    place = iota((seqs, LANES), 1) // width
    for half, out_ref in ((0, left_ref), (1, right_ref)):
        for tile in range(rows // fold):
            merged = proj_ref[half, pl.ds(tile * fold, seqs, stride=rows), :]
            for k in range(1, fold):
                part = proj_ref[half, pl.ds(tile * fold + k, seqs, stride=rows), :]
                merged = jnp.where(place == k, part, merged)
            merged = merged * mask[:, tile * LANES:(tile + 1) * LANES]
            out_ref[tile * seqs:(tile + 1) * seqs, :] = merged.astype(BF16)
        for tile in range((out_ref.shape[0] - data) // rows):
            mine = jnp.where(lane_block + tile * (LANES // seqs) == block, flags, 0.0)
            out_ref[data + tile * rows:data + (tile + 1) * rows, :] = mine.astype(BF16)


def own_kernel(x_hbm, flag_hbm, scale_hbm, shift_hbm, wl_hbm, bl_hbm, wr_hbm, br_hbm,
               left_ref, right_ref, weight_ref, vector_ref,
               x_ref, flag_ref, scale_ref, shift_ref, wl_ref, bl_ref, wr_ref, br_ref, proj_ref, sems):
    copies = [
        pltpu.make_async_copy(src, dst, sems.at[k])
        for k, (src, dst) in enumerate((
            (x_hbm, x_ref), (flag_hbm, flag_ref), (scale_hbm, scale_ref), (shift_hbm, shift_ref),
            (wl_hbm, wl_ref), (bl_hbm, bl_ref), (wr_hbm, wr_ref), (br_hbm, br_ref),
        ))
    ]
    for copy in copies:
        copy.start()
    for copy in copies:
        copy.wait()
    width, depth = wl_ref.shape
    fold = LANES // width
    weight = jnp.concatenate([wl_ref[...]] * fold + [wr_ref[...]] * fold, axis=0)
    bias = [bl_ref[...].reshape(1, width)] * fold + [br_ref[...].reshape(1, width)] * fold
    vectors = jnp.concatenate(
        [
            scale_ref[...].reshape(1, depth),
            shift_ref[...].reshape(1, depth),
            jnp.concatenate(bias, axis=1),
            jnp.zeros((5, depth), F32),
        ],
        axis=0,
    )
    weight_ref[...] = weight
    vector_ref[...] = vectors
    project_block(width, x_ref, flag_ref, weight, vectors, lax.axis_index("seq"), left_ref, right_ref, proj_ref)


def both_kernel(width, x_ref, flag_ref, weight_ref, vector_ref, own_left_ref, own_right_ref, left_ref, right_ref, proj_ref):
    block = lax.axis_index("seq")
    core = block % CORES
    left_ref[core] = own_left_ref[...]
    right_ref[core] = own_right_ref[...]
    other = 1 - core
    project_block(
        width, x_ref, flag_ref, weight_ref[...], vector_ref[...], block + other - core,
        left_ref.at[other], right_ref.at[other], proj_ref,
    )


def whole_mask(pieces, rows, data):
    total = functools.reduce(jnp.add, [p[k, data:, :] for p in pieces for k in range(CORES)])
    return jnp.concatenate([total[k:k + rows] for k in range(0, total.shape[0], rows)], axis=1)


def pair_kernel(steps, seqs, rows, columns, width, *refs):
    n = len(steps)
    lefts, rights, own_ref = refs[:n], refs[n:2 * n], refs[2 * n]
    w_ref, bias_ref, out_ref, left_ref, right_ref, outer_ref, flat_ref, raw_ref = refs[2 * n + 1:]
    fold = LANES // width
    data = rows * width // LANES * seqs

    me_res, me_seq = lax.axis_index("res"), lax.axis_index("seq")
    rights = [jnp.where(me_res == me_seq, own_ref[...], rights[0][...])] + list(rights[1:])
    for k in range(n):
        for pieces, chip, whole_ref in ((lefts, me_seq // CORES ^ k, left_ref), (rights, (me_res ^ steps[k]) // CORES, right_ref)):
            for core in range(CORES):
                at = pl.multiple_of((chip * CORES + core) * seqs, seqs)
                for tile in range(data // seqs):
                    whole_ref[pl.ds(at, seqs), tile * LANES:(tile + 1) * LANES] = (
                        pieces[k][core, tile * seqs:(tile + 1) * seqs, :]
                    )

    outer = dot(left_ref[...], right_ref[...], TN)
    for tile in range(columns // fold):
        outer_ref[tile] = outer[:, tile * LANES:(tile + 1) * LANES]

    place = iota((rows, LANES), 1) // width
    for tile in range(columns // fold):
        for quad in range(width // fold):
            part = [
                outer_ref[tile, pl.ds(quad * fold + k, rows, stride=width), :]
                for k in range(fold)
            ]
            step = fold // 2
            while step:
                keep = (place // step) % 2 == 0
                new = list(part)
                for k in range(fold):
                    if (k // step) % 2 == 0:
                        a, b = part[k], part[k + step]
                        new[k] = jnp.where(keep, a, pltpu.roll(b, step * width, 1))
                        new[k + step] = jnp.where(keep, pltpu.roll(a, LANES - step * width, 1), b)
                part = new
                step //= 2
            for k in range(fold):
                j = tile * fold + k
                flat_ref[j * rows:(j + 1) * rows, quad * LANES:(quad + 1) * LANES] = part[k].astype(BF16)

    raw = dot(flat_ref[...], w_ref[...]) + bias_ref[...].reshape(1, -1)

    pair = rows * columns
    row = iota((pair, rows), 0)
    live_left = dot((row % rows == iota((pair, rows), 1)).astype(BF16), whole_mask(lefts, rows, data))
    row = iota((pair, columns), 0)
    live_right = dot((row // rows == iota((pair, columns), 1)).astype(BF16), whole_mask(rights, rows, data))
    count = jnp.sum(live_left * live_right, axis=1, keepdims=True)
    raw_ref[...] = raw / (1.0 + count)
    for i in range(rows):
        out_ref[i] = raw_ref[pl.ds(i, columns, stride=rows), :].astype(BF16)


def local(n, x, flags, scale, shift, wl, bl, wr, br, w, bias):
    seqs, rows, depth = x.shape
    width = wl.shape[1]
    outs = w.shape[1]
    lanes = rows * width
    size = lanes // LANES * seqs + rows * pl.cdiv(n * seqs, LANES)
    axes = ("res", "seq")
    flags = flags.T

    swap = [(p, p ^ 1) for p in range(n)]
    other_x, other_flags = lax.ppermute(x, "seq", swap), lax.ppermute(flags, "seq", swap)

    operands = [
        pltpu.with_memory_space_constraint(o, pltpu.HBM) for o in (x, flags, scale, shift, wl.T, bl, wr.T, br)
    ]
    wire = jax.ShapeDtypeStruct((size, LANES), BF16)
    left, right, weight, vectors = pl.pallas_call(
        own_kernel,
        out_shape=(
            wire, wire,
            jax.ShapeDtypeStruct((2 * LANES, depth), BF16),
            jax.ShapeDtypeStruct((8, 2 * LANES), F32),
        ),
        in_specs=[pl.BlockSpec(memory_space=pltpu.HBM)] * len(operands),
        scratch_shapes=[pltpu.VMEM(o.shape, o.dtype) for o in operands] + [
            pltpu.VMEM((2, seqs * rows, LANES), F32),
            pltpu.SemaphoreType.DMA((len(operands),)),
        ],
        compiler_params=pltpu.CompilerParams(vmem_limit_bytes=16 << 20),
        cost_estimate=pl.CostEstimate(flops=1 << 25, bytes_accessed=x.size * 8, transcendentals=0),
        name="project_own",
    )(*operands)
    wire = jax.ShapeDtypeStruct((CORES, size, LANES), BF16)
    left, right = pl.pallas_call(
        functools.partial(both_kernel, width),
        out_shape=(wire, wire),
        scratch_shapes=[pltpu.VMEM((2, seqs * rows, LANES), F32)],
        compiler_params=pltpu.CompilerParams(vmem_limit_bytes=16 << 20),
        name="project_other",
    )(other_x, other_flags, weight, vectors, left, right)

    steps = [m for m in range(n) if bin(m).count("1") % 2 == 0]
    lefts = [left] + [
        lax.ppermute(left, "seq", [(p, p ^ k * CORES) for p in range(n)]) for k in range(1, n // CORES)
    ]
    rights = []
    for m in steps:
        pairs = []
        for a in range(n):
            for p in range(n):
                to = (a ^ 1, a ^ 1) if (p ^ m, a) == (a, p) else (p ^ m, a)
                pairs.append((a * n + p, to[0] * n + to[1]))
        rights.append(lax.ppermute(right, axes, pairs))
    return pl.pallas_call(
        functools.partial(pair_kernel, steps, seqs, rows, rows, width),
        out_shape=jax.ShapeDtypeStruct((rows, rows, outs), BF16),
        scratch_shapes=[
            pltpu.VMEM((n * seqs, lanes), BF16),
            pltpu.VMEM((n * seqs, lanes), BF16),
            pltpu.VMEM((lanes // LANES, lanes, LANES), F32),
            pltpu.VMEM((rows * rows, width * width), BF16),
            pltpu.VMEM((rows * rows, outs), F32),
        ],
        compiler_params=pltpu.CompilerParams(vmem_limit_bytes=24 << 20),
        name="pair",
    )(*lefts, *rights, right, w, bias)


def solution(mesh):
    n = mesh.shape["res"]
    assert n == mesh.shape["seq"] and n & (n - 1) == 0 and n % CORES == 0
    in_specs = (P(("group", "seq"), "res", None), P(("group", "seq"), "res")) + (P(),) * 8
    return jax.shard_map(
        functools.partial(local, n), mesh=mesh, in_specs=in_specs,
        out_specs=P(("group", "res"), "seq", None), check_vma=False,
    )
```

```python
import functools

import jax
import jax.numpy as jnp
from jax import lax
from jax.experimental import pallas as pl
from jax.experimental.pallas import tpu as pltpu
from jax.sharding import PartitionSpec as P

LANES = 128
CORES = 2
F32 = jnp.float32
BF16 = jnp.bfloat16
TN = (((0,), (0,)), ((), ()))
NT = (((1,), (1,)), ((), ()))
NN = (((1,), (0,)), ((), ()))


def dot(a, b, dims=NN):
    return lax.dot_general(a, b, dims, preferred_element_type=F32)


def iota(shape, dim):
    return lax.broadcasted_iota(jnp.int32, shape, dim)


def project_block(width, x_ref, flag_ref, weight, vectors, block, left_ref, right_ref, proj_ref):
    seqs, rows, depth = x_ref.shape
    fold = LANES // width
    lanes = rows * width
    data = lanes // LANES * seqs
    x = x_ref[...].astype(F32).reshape(seqs * rows, depth)
    center = jnp.mean(x, axis=-1, keepdims=True)
    x = x - center
    spread = jnp.mean(x * x, axis=-1, keepdims=True)
    normed = x * lax.rsqrt(spread + 1e-05) * vectors[0:1] + vectors[1:2]
    both = dot(normed.astype(BF16), weight, NT) + vectors[2:3]
    proj_ref[0] = both[:, :LANES]
    proj_ref[1] = both[:, LANES:]

    flags = flag_ref[...].astype(F32)
    spreader = (iota((rows, lanes), 1) // width == iota((rows, lanes), 0)).astype(BF16)
    mask = dot(flags.astype(BF16), spreader, TN)
    flags = jnp.concatenate([flags] * (LANES // seqs), axis=1)
    lane_block = iota((rows, LANES), 1) // seqs

    place = iota((seqs, LANES), 1) // width
    for half, out_ref in ((0, left_ref), (1, right_ref)):
        for tile in range(rows // fold):
            merged = proj_ref[half, pl.ds(tile * fold, seqs, stride=rows), :]
            for k in range(1, fold):
                part = proj_ref[half, pl.ds(tile * fold + k, seqs, stride=rows), :]
                merged = jnp.where(place == k, part, merged)
            merged = merged * mask[:, tile * LANES:(tile + 1) * LANES]
            out_ref[tile * seqs:(tile + 1) * seqs, :] = merged.astype(BF16)
        for tile in range((out_ref.shape[0] - data) // rows):
            mine = jnp.where(lane_block + tile * (LANES // seqs) == block, flags, 0.0)
            out_ref[data + tile * rows:data + (tile + 1) * rows, :] = mine.astype(BF16)


def own_kernel(x_hbm, flag_hbm, scale_hbm, shift_hbm, wl_hbm, bl_hbm, wr_hbm, br_hbm,
               left_ref, right_ref, weight_ref, vector_ref,
               x_ref, flag_ref, scale_ref, shift_ref, wl_ref, bl_ref, wr_ref, br_ref, proj_ref, sems):
    copies = [
        pltpu.make_async_copy(src, dst, sems.at[k])
        for k, (src, dst) in enumerate((
            (x_hbm, x_ref), (flag_hbm, flag_ref), (scale_hbm, scale_ref), (shift_hbm, shift_ref),
            (wl_hbm, wl_ref), (bl_hbm, bl_ref), (wr_hbm, wr_ref), (br_hbm, br_ref),
        ))
    ]
    for copy in copies:
        copy.start()
    for copy in copies:
        copy.wait()
    width, depth = wl_ref.shape
    fold = LANES // width
    weight = jnp.concatenate([wl_ref[...]] * fold + [wr_ref[...]] * fold, axis=0)
    bias = [bl_ref[...].reshape(1, width)] * fold + [br_ref[...].reshape(1, width)] * fold
    vectors = jnp.concatenate(
        [
            scale_ref[...].reshape(1, depth),
            shift_ref[...].reshape(1, depth),
            jnp.concatenate(bias, axis=1),
            jnp.zeros((5, depth), F32),
        ],
        axis=0,
    )
    weight_ref[...] = weight
    vector_ref[...] = vectors
    project_block(width, x_ref, flag_ref, weight, vectors, lax.axis_index("seq"), left_ref, right_ref, proj_ref)


def both_kernel(width, x_ref, flag_ref, weight_ref, vector_ref, own_left_ref, own_right_ref, left_ref, right_ref, proj_ref):
    block = lax.axis_index("seq")
    core = block % CORES
    left_ref[core] = own_left_ref[...]
    right_ref[core] = own_right_ref[...]
    other = 1 - core
    project_block(
        width, x_ref, flag_ref, weight_ref[...], vector_ref[...], block + other - core,
        left_ref.at[other], right_ref.at[other], proj_ref,
    )


def whole_mask(pieces, rows, data):
    total = functools.reduce(jnp.add, [p[k, data:, :] for p in pieces for k in range(CORES)])
    return jnp.concatenate([total[k:k + rows] for k in range(0, total.shape[0], rows)], axis=1)


def pair_kernel(steps, seqs, rows, columns, width, *refs):
    n = len(steps)
    lefts, rights = refs[:n], refs[n:2 * n]
    w_ref, bias_ref, out_ref, left_ref, right_ref, outer_ref, flat_ref, raw_ref = refs[2 * n:]
    fold = LANES // width
    data = rows * width // LANES * seqs

    me_res, me_seq = lax.axis_index("res"), lax.axis_index("seq")
    for k in range(n):
        for pieces, chip, whole_ref in ((lefts, me_seq // CORES ^ k, left_ref), (rights, (me_res ^ steps[k]) // CORES, right_ref)):
            for core in range(CORES):
                at = pl.multiple_of((chip * CORES + core) * seqs, seqs)
                for tile in range(data // seqs):
                    whole_ref[pl.ds(at, seqs), tile * LANES:(tile + 1) * LANES] = (
                        pieces[k][core, tile * seqs:(tile + 1) * seqs, :]
                    )

    outer = dot(left_ref[...], right_ref[...], TN)
    for tile in range(columns // fold):
        outer_ref[tile] = outer[:, tile * LANES:(tile + 1) * LANES]

    place = iota((rows, LANES), 1) // width
    for tile in range(columns // fold):
        for quad in range(width // fold):
            part = [
                outer_ref[tile, pl.ds(quad * fold + k, rows, stride=width), :]
                for k in range(fold)
            ]
            step = fold // 2
            while step:
                keep = (place // step) % 2 == 0
                new = list(part)
                for k in range(fold):
                    if (k // step) % 2 == 0:
                        a, b = part[k], part[k + step]
                        new[k] = jnp.where(keep, a, pltpu.roll(b, step * width, 1))
                        new[k + step] = jnp.where(keep, pltpu.roll(a, LANES - step * width, 1), b)
                part = new
                step //= 2
            for k in range(fold):
                j = tile * fold + k
                flat_ref[j * rows:(j + 1) * rows, quad * LANES:(quad + 1) * LANES] = part[k].astype(BF16)

    raw = dot(flat_ref[...], w_ref[...]) + bias_ref[...].reshape(1, -1)

    pair = rows * columns
    row = iota((pair, rows), 0)
    live_left = dot((row % rows == iota((pair, rows), 1)).astype(BF16), whole_mask(lefts, rows, data))
    row = iota((pair, columns), 0)
    live_right = dot((row // rows == iota((pair, columns), 1)).astype(BF16), whole_mask(rights, rows, data))
    count = jnp.sum(live_left * live_right, axis=1, keepdims=True)
    raw_ref[...] = raw / (1.0 + count)
    for i in range(rows):
        out_ref[i] = raw_ref[pl.ds(i, columns, stride=rows), :].astype(BF16)


def local(n, x, flags, scale, shift, wl, bl, wr, br, w, bias):
    seqs, rows, depth = x.shape
    width = wl.shape[1]
    outs = w.shape[1]
    lanes = rows * width
    size = lanes // LANES * seqs + rows * pl.cdiv(n * seqs, LANES)
    axes = ("res", "seq")
    flags = flags.T

    swap = [(p, p ^ 1) for p in range(n)]
    other_x, other_flags = lax.ppermute(x, "seq", swap), lax.ppermute(flags, "seq", swap)

    operands = [
        pltpu.with_memory_space_constraint(o, pltpu.HBM) for o in (x, flags, scale, shift, wl.T, bl, wr.T, br)
    ]
    wire = jax.ShapeDtypeStruct((size, LANES), BF16)
    left, right, weight, vectors = pl.pallas_call(
        own_kernel,
        out_shape=(
            wire, wire,
            jax.ShapeDtypeStruct((2 * LANES, depth), BF16),
            jax.ShapeDtypeStruct((8, 2 * LANES), F32),
        ),
        in_specs=[pl.BlockSpec(memory_space=pltpu.HBM)] * len(operands),
        scratch_shapes=[pltpu.VMEM(o.shape, o.dtype) for o in operands] + [
            pltpu.VMEM((2, seqs * rows, LANES), F32),
            pltpu.SemaphoreType.DMA((len(operands),)),
        ],
        compiler_params=pltpu.CompilerParams(vmem_limit_bytes=16 << 20),
        cost_estimate=pl.CostEstimate(flops=1 << 25, bytes_accessed=x.size * 8, transcendentals=0),
        name="project_own",
    )(*operands)
    wire = jax.ShapeDtypeStruct((CORES, size, LANES), BF16)
    left, right = pl.pallas_call(
        functools.partial(both_kernel, width),
        out_shape=(wire, wire),
        scratch_shapes=[pltpu.VMEM((2, seqs * rows, LANES), F32)],
        compiler_params=pltpu.CompilerParams(vmem_limit_bytes=16 << 20),
        name="project_other",
    )(other_x, other_flags, weight, vectors, left, right)

    steps = [m for m in reversed(range(n)) if bin(m).count("1") % 2 == 1]
    lefts = [left] + [
        lax.ppermute(left, "seq", [(p, p ^ k * CORES) for p in range(n)]) for k in range(1, n // CORES)
    ]
    rights = []
    for m in steps:
        pairs = [(a * n + p, (p ^ m) * n + a) for a in range(n) for p in range(n)]
        rights.append(lax.ppermute(right, axes, pairs))
    return pl.pallas_call(
        functools.partial(pair_kernel, steps, seqs, rows, rows, width),
        out_shape=jax.ShapeDtypeStruct((rows, rows, outs), BF16),
        scratch_shapes=[
            pltpu.VMEM((n * seqs, lanes), BF16),
            pltpu.VMEM((n * seqs, lanes), BF16),
            pltpu.VMEM((lanes // LANES, lanes, LANES), F32),
            pltpu.VMEM((rows * rows, width * width), BF16),
            pltpu.VMEM((rows * rows, outs), F32),
        ],
        compiler_params=pltpu.CompilerParams(vmem_limit_bytes=24 << 20),
        name="pair",
    )(*lefts, *rights, w, bias)


def solution(mesh):
    n = mesh.shape["res"]
    assert n == mesh.shape["seq"] and n & (n - 1) == 0 and n % CORES == 0
    in_specs = (P(("group", "seq"), "res", None), P(("group", "seq"), "res")) + (P(),) * 8
    return jax.shard_map(
        functools.partial(local, n), mesh=mesh, in_specs=in_specs,
        out_specs=P(("group", "res"), "seq", None), check_vma=False,
    )
```

```python
import functools

import jax
import jax.numpy as jnp
from jax import lax
from jax.experimental import pallas as pl
from jax.experimental.pallas import tpu as pltpu
from jax.sharding import PartitionSpec as P

LANES = 128
CORES = 2
F32 = jnp.float32
BF16 = jnp.bfloat16
TN = (((0,), (0,)), ((), ()))
NT = (((1,), (1,)), ((), ()))
NN = (((1,), (0,)), ((), ()))


def dot(a, b, dims=NN):
    return lax.dot_general(a, b, dims, preferred_element_type=F32)


def iota(shape, dim):
    return lax.broadcasted_iota(jnp.int32, shape, dim)


ROUTES = (
    ((2, 0, 3, 1), (1, 0, 2, 3), (1, 3, 0, 2), (1, 3, 0, 2)),
    ((3, 1, 2, 0), (2, 3, 1, 0), (2, 0, 3, 1), (2, 0, 3, 1)),
)


def routes(n):
    if n == 4:
        return ROUTES
    steps = [m for m in range(n) if bin(m).count("1") % 2 == 1]
    return tuple(tuple(tuple(p ^ m for p in range(n)) for a in range(n)) for m in steps)


def sending_chip(step, r, q):
    n = len(step)
    chip = 0
    for bit in range((n // CORES - 1).bit_length()):
        for a in range(n):
            word = sum((step[a].index(to) // CORES >> bit & 1) << to for to in range(n))
            chip = chip | jnp.where(q == a, (jnp.int32(word) >> r & 1) << bit, 0)
    return chip


def project_block(width, x_ref, flag_ref, weight, vectors, block, left_ref, right_ref, proj_ref):
    seqs, rows, depth = x_ref.shape
    fold = LANES // width
    lanes = rows * width
    data = lanes // LANES * seqs
    x = x_ref[...].astype(F32).reshape(seqs * rows, depth)
    center = jnp.mean(x, axis=-1, keepdims=True)
    x = x - center
    spread = jnp.mean(x * x, axis=-1, keepdims=True)
    normed = x * lax.rsqrt(spread + 1e-05) * vectors[0:1] + vectors[1:2]
    both = dot(normed.astype(BF16), weight, NT) + vectors[2:3]
    proj_ref[0] = both[:, :LANES]
    proj_ref[1] = both[:, LANES:]

    flags = flag_ref[...].astype(F32)
    spreader = (iota((rows, lanes), 1) // width == iota((rows, lanes), 0)).astype(BF16)
    mask = dot(flags.astype(BF16), spreader, TN)
    flags = jnp.concatenate([flags] * (LANES // seqs), axis=1)
    lane_block = iota((rows, LANES), 1) // seqs

    place = iota((seqs, LANES), 1) // width
    for half, out_ref in ((0, left_ref), (1, right_ref)):
        for tile in range(rows // fold):
            merged = proj_ref[half, pl.ds(tile * fold, seqs, stride=rows), :]
            for k in range(1, fold):
                part = proj_ref[half, pl.ds(tile * fold + k, seqs, stride=rows), :]
                merged = jnp.where(place == k, part, merged)
            merged = merged * mask[:, tile * LANES:(tile + 1) * LANES]
            out_ref[tile * seqs:(tile + 1) * seqs, :] = merged.astype(BF16)
        for tile in range((out_ref.shape[0] - data) // rows):
            mine = jnp.where(lane_block + tile * (LANES // seqs) == block, flags, 0.0)
            out_ref[data + tile * rows:data + (tile + 1) * rows, :] = mine.astype(BF16)


def own_kernel(x_hbm, flag_hbm, scale_hbm, shift_hbm, wl_hbm, bl_hbm, wr_hbm, br_hbm,
               left_ref, right_ref, weight_ref, vector_ref,
               x_ref, flag_ref, scale_ref, shift_ref, wl_ref, bl_ref, wr_ref, br_ref, proj_ref, sems):
    copies = [
        pltpu.make_async_copy(src, dst, sems.at[k])
        for k, (src, dst) in enumerate((
            (x_hbm, x_ref), (flag_hbm, flag_ref), (scale_hbm, scale_ref), (shift_hbm, shift_ref),
            (wl_hbm, wl_ref), (bl_hbm, bl_ref), (wr_hbm, wr_ref), (br_hbm, br_ref),
        ))
    ]
    for copy in copies:
        copy.start()
    for copy in copies:
        copy.wait()
    width, depth = wl_ref.shape
    fold = LANES // width
    weight = jnp.concatenate([wl_ref[...]] * fold + [wr_ref[...]] * fold, axis=0)
    bias = [bl_ref[...].reshape(1, width)] * fold + [br_ref[...].reshape(1, width)] * fold
    vectors = jnp.concatenate(
        [
            scale_ref[...].reshape(1, depth),
            shift_ref[...].reshape(1, depth),
            jnp.concatenate(bias, axis=1),
            jnp.zeros((5, depth), F32),
        ],
        axis=0,
    )
    weight_ref[...] = weight
    vector_ref[...] = vectors
    project_block(width, x_ref, flag_ref, weight, vectors, lax.axis_index("seq"), left_ref, right_ref, proj_ref)


def both_kernel(width, x_ref, flag_ref, weight_ref, vector_ref, own_left_ref, own_right_ref, left_ref, right_ref, proj_ref):
    block = lax.axis_index("seq")
    core = block % CORES
    left_ref[core] = own_left_ref[...]
    right_ref[core] = own_right_ref[...]
    other = 1 - core
    project_block(
        width, x_ref, flag_ref, weight_ref[...], vector_ref[...], block + other - core,
        left_ref.at[other], right_ref.at[other], proj_ref,
    )


def whole_mask(pieces, rows, data):
    total = functools.reduce(jnp.add, [p[k, data:, :] for p in pieces for k in range(CORES)])
    return jnp.concatenate([total[k:k + rows] for k in range(0, total.shape[0], rows)], axis=1)


def pair_kernel(steps, seqs, rows, columns, width, *refs):
    n = len(steps)
    lefts, rights = refs[:n], refs[n:2 * n]
    w_ref, bias_ref, out_ref, left_ref, right_ref, outer_ref, flat_ref, raw_ref = refs[2 * n:]
    fold = LANES // width
    data = rows * width // LANES * seqs

    me_res, me_seq = lax.axis_index("res"), lax.axis_index("seq")
    for k in range(n):
        for pieces, chip, whole_ref in ((lefts, me_seq // CORES ^ k, left_ref), (rights, sending_chip(steps[k], me_res, me_seq), right_ref)):
            for core in range(CORES):
                at = pl.multiple_of((chip * CORES + core) * seqs, seqs)
                for tile in range(data // seqs):
                    whole_ref[pl.ds(at, seqs), tile * LANES:(tile + 1) * LANES] = (
                        pieces[k][core, tile * seqs:(tile + 1) * seqs, :]
                    )

    outer = dot(left_ref[...], right_ref[...], TN)
    for tile in range(columns // fold):
        outer_ref[tile] = outer[:, tile * LANES:(tile + 1) * LANES]

    place = iota((rows, LANES), 1) // width
    for tile in range(columns // fold):
        for quad in range(width // fold):
            part = [
                outer_ref[tile, pl.ds(quad * fold + k, rows, stride=width), :]
                for k in range(fold)
            ]
            step = fold // 2
            while step:
                keep = (place // step) % 2 == 0
                new = list(part)
                for k in range(fold):
                    if (k // step) % 2 == 0:
                        a, b = part[k], part[k + step]
                        new[k] = jnp.where(keep, a, pltpu.roll(b, step * width, 1))
                        new[k + step] = jnp.where(keep, pltpu.roll(a, LANES - step * width, 1), b)
                part = new
                step //= 2
            for k in range(fold):
                j = tile * fold + k
                flat_ref[j * rows:(j + 1) * rows, quad * LANES:(quad + 1) * LANES] = part[k].astype(BF16)

    raw = dot(flat_ref[...], w_ref[...]) + bias_ref[...].reshape(1, -1)

    pair = rows * columns
    row = iota((pair, rows), 0)
    live_left = dot((row % rows == iota((pair, rows), 1)).astype(BF16), whole_mask(lefts, rows, data))
    row = iota((pair, columns), 0)
    live_right = dot((row // rows == iota((pair, columns), 1)).astype(BF16), whole_mask(rights, rows, data))
    count = jnp.sum(live_left * live_right, axis=1, keepdims=True)
    raw_ref[...] = raw / (1.0 + count)
    for i in range(rows):
        out_ref[i] = raw_ref[pl.ds(i, columns, stride=rows), :].astype(BF16)


def local(n, x, flags, scale, shift, wl, bl, wr, br, w, bias):
    seqs, rows, depth = x.shape
    width = wl.shape[1]
    outs = w.shape[1]
    lanes = rows * width
    size = lanes // LANES * seqs + rows * pl.cdiv(n * seqs, LANES)
    axes = ("res", "seq")
    flags = flags.T

    swap = [(p, p ^ 1) for p in range(n)]
    other_x, other_flags = lax.ppermute(x, "seq", swap), lax.ppermute(flags, "seq", swap)

    operands = [
        pltpu.with_memory_space_constraint(o, pltpu.HBM) for o in (x, flags, scale, shift, wl.T, bl, wr.T, br)
    ]
    wire = jax.ShapeDtypeStruct((size, LANES), BF16)
    left, right, weight, vectors = pl.pallas_call(
        own_kernel,
        out_shape=(
            wire, wire,
            jax.ShapeDtypeStruct((2 * LANES, depth), BF16),
            jax.ShapeDtypeStruct((8, 2 * LANES), F32),
        ),
        in_specs=[pl.BlockSpec(memory_space=pltpu.HBM)] * len(operands),
        scratch_shapes=[pltpu.VMEM(o.shape, o.dtype) for o in operands] + [
            pltpu.VMEM((2, seqs * rows, LANES), F32),
            pltpu.SemaphoreType.DMA((len(operands),)),
        ],
        compiler_params=pltpu.CompilerParams(vmem_limit_bytes=16 << 20),
        cost_estimate=pl.CostEstimate(flops=1 << 25, bytes_accessed=x.size * 8, transcendentals=0),
        name="project_own",
    )(*operands)
    wire = jax.ShapeDtypeStruct((CORES, size, LANES), BF16)
    left, right = pl.pallas_call(
        functools.partial(both_kernel, width),
        out_shape=(wire, wire),
        scratch_shapes=[pltpu.VMEM((2, seqs * rows, LANES), F32)],
        compiler_params=pltpu.CompilerParams(vmem_limit_bytes=16 << 20),
        name="project_other",
    )(other_x, other_flags, weight, vectors, left, right)

    steps = routes(n)
    lefts = [left] + [
        lax.ppermute(left, "seq", [(p, p ^ k * CORES) for p in range(n)]) for k in range(1, n // CORES)
    ]
    rights = [
        lax.ppermute(right, axes, [(a * n + p, step[a][p] * n + a) for a in range(n) for p in range(n)])
        for step in steps
    ]
    return pl.pallas_call(
        functools.partial(pair_kernel, steps, seqs, rows, rows, width),
        out_shape=jax.ShapeDtypeStruct((rows, rows, outs), BF16),
        scratch_shapes=[
            pltpu.VMEM((n * seqs, lanes), BF16),
            pltpu.VMEM((n * seqs, lanes), BF16),
            pltpu.VMEM((lanes // LANES, lanes, LANES), F32),
            pltpu.VMEM((rows * rows, width * width), BF16),
            pltpu.VMEM((rows * rows, outs), F32),
        ],
        compiler_params=pltpu.CompilerParams(vmem_limit_bytes=24 << 20),
        name="pair",
    )(*lefts, *rights, w, bias)


def solution(mesh):
    n = mesh.shape["res"]
    assert n == mesh.shape["seq"] and n & (n - 1) == 0 and n % CORES == 0
    in_specs = (P(("group", "seq"), "res", None), P(("group", "seq"), "res")) + (P(),) * 8
    return jax.shard_map(
        functools.partial(local, n), mesh=mesh, in_specs=in_specs,
        out_specs=P(("group", "res"), "seq", None), check_vma=False,
    )
```

```python
import functools

import jax
import jax.numpy as jnp
from jax import lax
from jax.experimental import pallas as pl
from jax.experimental.pallas import tpu as pltpu
from jax.sharding import PartitionSpec as P

LANES = 128
CORES = 2
F32 = jnp.float32
BF16 = jnp.bfloat16
TN = (((0,), (0,)), ((), ()))
NT = (((1,), (1,)), ((), ()))
NN = (((1,), (0,)), ((), ()))


def dot(a, b, dims=NN):
    return lax.dot_general(a, b, dims, preferred_element_type=F32)


def iota(shape, dim):
    return lax.broadcasted_iota(jnp.int32, shape, dim)


ROUTES = (
    ((2, 0, 3, 1), (1, 0, 2, 3), (1, 3, 0, 2), (1, 3, 0, 2)),
    ((3, 1, 2, 0), (2, 3, 1, 0), (2, 0, 3, 1), (2, 0, 3, 1)),
)


def routes(n):
    if n == 4:
        return ROUTES
    steps = [m for m in range(n) if bin(m).count("1") % 2 == 1]
    return tuple(tuple(tuple(p ^ m for p in range(n)) for a in range(n)) for m in steps)


def sending_chip(step, r, q):
    n = len(step)
    chip = 0
    for bit in range((n // CORES - 1).bit_length()):
        for a in range(n):
            word = sum((step[a].index(to) // CORES >> bit & 1) << to for to in range(n))
            chip = chip | jnp.where(q == a, (jnp.int32(word) >> r & 1) << bit, 0)
    return chip


def project_block(width, x_ref, flag_ref, weight, vectors, block, left_ref, right_ref, proj_ref):
    seqs, rows, depth = x_ref.shape
    fold = LANES // width
    lanes = rows * width
    data = lanes // LANES * seqs
    x = x_ref[...].astype(F32).reshape(seqs * rows, depth)
    center = jnp.mean(x, axis=-1, keepdims=True)
    x = x - center
    spread = jnp.mean(x * x, axis=-1, keepdims=True)
    normed = x * lax.rsqrt(spread + 1e-05) * vectors[0:1] + vectors[1:2]
    both = dot(normed.astype(BF16), weight, NT) + vectors[2:3]
    proj_ref[0] = both[:, :LANES]
    proj_ref[1] = both[:, LANES:]

    flags = flag_ref[...].astype(F32)
    spreader = (iota((rows, lanes), 1) // width == iota((rows, lanes), 0)).astype(BF16)
    mask = dot(flags.astype(BF16), spreader, TN)
    flags = jnp.concatenate([flags] * (LANES // seqs), axis=1)
    lane_block = iota((rows, LANES), 1) // seqs

    place = iota((seqs, LANES), 1) // width
    for half, out_ref in ((0, left_ref), (1, right_ref)):
        for tile in range(rows // fold):
            merged = proj_ref[half, pl.ds(tile * fold, seqs, stride=rows), :]
            for k in range(1, fold):
                part = proj_ref[half, pl.ds(tile * fold + k, seqs, stride=rows), :]
                merged = jnp.where(place == k, part, merged)
            merged = merged * mask[:, tile * LANES:(tile + 1) * LANES]
            out_ref[tile * seqs:(tile + 1) * seqs, :] = merged.astype(BF16)
        for tile in range((out_ref.shape[0] - data) // rows):
            mine = jnp.where(lane_block + tile * (LANES // seqs) == block, flags, 0.0)
            out_ref[data + tile * rows:data + (tile + 1) * rows, :] = mine.astype(BF16)


def own_kernel(x_hbm, flag_hbm, scale_hbm, shift_hbm, wl_hbm, bl_hbm, wr_hbm, br_hbm,
               left_ref, right_ref, weight_ref, vector_ref,
               x_ref, flag_ref, scale_ref, shift_ref, wl_ref, bl_ref, wr_ref, br_ref, proj_ref, sems):
    copies = [
        pltpu.make_async_copy(src, dst, sems.at[k])
        for k, (src, dst) in enumerate((
            (x_hbm, x_ref), (flag_hbm, flag_ref), (scale_hbm, scale_ref), (shift_hbm, shift_ref),
            (wl_hbm, wl_ref), (bl_hbm, bl_ref), (wr_hbm, wr_ref), (br_hbm, br_ref),
        ))
    ]
    for copy in copies:
        copy.start()
    for copy in copies:
        copy.wait()
    width, depth = wl_ref.shape
    fold = LANES // width
    weight = jnp.concatenate([wl_ref[...]] * fold + [wr_ref[...]] * fold, axis=0)
    bias = [bl_ref[...].reshape(1, width)] * fold + [br_ref[...].reshape(1, width)] * fold
    vectors = jnp.concatenate(
        [
            scale_ref[...].reshape(1, depth),
            shift_ref[...].reshape(1, depth),
            jnp.concatenate(bias, axis=1),
            jnp.zeros((5, depth), F32),
        ],
        axis=0,
    )
    weight_ref[...] = weight
    vector_ref[...] = vectors
    project_block(width, x_ref, flag_ref, weight, vectors, lax.axis_index("seq"), left_ref, right_ref, proj_ref)


def both_kernel(width, x_ref, flag_ref, weight_ref, vector_ref, own_left_ref, own_right_ref, left_ref, right_ref, proj_ref):
    block = lax.axis_index("seq")
    core = block % CORES
    left_ref[core] = own_left_ref[...]
    right_ref[core] = own_right_ref[...]
    other = 1 - core
    project_block(
        width, x_ref, flag_ref, weight_ref[...], vector_ref[...], block + other - core,
        left_ref.at[other], right_ref.at[other], proj_ref,
    )


def whole_mask(pieces, rows, data):
    total = functools.reduce(jnp.add, [p[k, data:, :] for p in pieces for k in range(CORES)])
    return jnp.concatenate([total[k:k + rows] for k in range(0, total.shape[0], rows)], axis=1)


def pair_kernel(steps, seqs, rows, columns, width, *refs):
    n = len(steps)
    lefts, rights = refs[:n], refs[n:2 * n]
    w_ref, bias_ref, out_ref, left_ref, right_ref, turned_ref, flat_ref, raw_ref = refs[2 * n:]
    fold = LANES // width
    assert fold == 4
    data = rows * width // LANES * seqs

    me_res, me_seq = lax.axis_index("res"), lax.axis_index("seq")
    for k in range(n):
        for pieces, chip, whole_ref in ((lefts, me_seq // CORES ^ k, left_ref), (rights, sending_chip(steps[k], me_res, me_seq), right_ref)):
            for core in range(CORES):
                at = pl.multiple_of((chip * CORES + core) * seqs, seqs)
                for tile in range(data // seqs):
                    whole_ref[pl.ds(at, seqs), tile * LANES:(tile + 1) * LANES] = (
                        pieces[k][core, tile * seqs:(tile + 1) * seqs, :]
                    )

    for tile in range(turned_ref.shape[0]):
        turned_ref[tile] = left_ref[tile * LANES:(tile + 1) * LANES, :].astype(F32).T
    turned = jnp.concatenate(
        [
            jnp.concatenate(
                [turned_ref[tile, pl.ds(c, rows, stride=width), :].astype(BF16) for c in range(width)], axis=0
            )
            for tile in range(turned_ref.shape[0])
        ],
        axis=1,
    )
    outer = dot(turned, right_ref[...]).astype(BF16)

    place = (iota((rows, LANES), 1) // width).astype(BF16)
    even = [None] * fold
    even[1] = (place == 0.0) | (place == 2.0)
    even[2] = (place == 0.0) | (place == 1.0)
    for tile in range(columns // fold):
        for quad in range(width // fold):
            part = [
                outer[(quad * fold + k) * rows:(quad * fold + k + 1) * rows, tile * LANES:(tile + 1) * LANES]
                for k in range(fold)
            ]
            for step in (2, 1):
                new = list(part)
                for k in range(fold):
                    if k & step == 0:
                        x, y = part[k], part[k + step]
                        new[k] = jnp.where(even[step], x, pltpu.roll(y, step * width, 1))
                        new[k + step] = jnp.where(even[step], pltpu.roll(x, LANES - step * width, 1), y)
                part = new
            for k in range(fold):
                j = tile * fold + k
                flat_ref[j * rows:(j + 1) * rows, quad * LANES:(quad + 1) * LANES] = part[k]

    raw = dot(flat_ref[...], w_ref[...]) + bias_ref[...].reshape(1, -1)
    count = dot(whole_mask(lefts, rows, data), whole_mask(rights, rows, data), NT)
    scale = 1.0 / (1.0 + count)
    for j in range(columns):
        raw_ref[j * rows:(j + 1) * rows, :] = raw[j * rows:(j + 1) * rows, :] * scale[:, j:j + 1]
    for i in range(rows):
        out_ref[i] = raw_ref[pl.ds(i, columns, stride=rows), :].astype(BF16)


def local(n, x, flags, scale, shift, wl, bl, wr, br, w, bias):
    seqs, rows, depth = x.shape
    width = wl.shape[1]
    outs = w.shape[1]
    lanes = rows * width
    size = lanes // LANES * seqs + rows * pl.cdiv(n * seqs, LANES)
    axes = ("res", "seq")
    flags = flags.T

    swap = [(p, p ^ 1) for p in range(n)]
    other_x, other_flags = lax.ppermute(x, "seq", swap), lax.ppermute(flags, "seq", swap)

    operands = [
        pltpu.with_memory_space_constraint(o, pltpu.HBM) for o in (x, flags, scale, shift, wl.T, bl, wr.T, br)
    ]
    wire = jax.ShapeDtypeStruct((size, LANES), BF16)
    left, right, weight, vectors = pl.pallas_call(
        own_kernel,
        out_shape=(
            wire, wire,
            jax.ShapeDtypeStruct((2 * LANES, depth), BF16),
            jax.ShapeDtypeStruct((8, 2 * LANES), F32),
        ),
        in_specs=[pl.BlockSpec(memory_space=pltpu.HBM)] * len(operands),
        scratch_shapes=[pltpu.VMEM(o.shape, o.dtype) for o in operands] + [
            pltpu.VMEM((2, seqs * rows, LANES), F32),
            pltpu.SemaphoreType.DMA((len(operands),)),
        ],
        compiler_params=pltpu.CompilerParams(vmem_limit_bytes=16 << 20),
        cost_estimate=pl.CostEstimate(flops=1 << 25, bytes_accessed=x.size * 8, transcendentals=0),
        name="project_own",
    )(*operands)
    wire = jax.ShapeDtypeStruct((CORES, size, LANES), BF16)
    left, right = pl.pallas_call(
        functools.partial(both_kernel, width),
        out_shape=(wire, wire),
        scratch_shapes=[pltpu.VMEM((2, seqs * rows, LANES), F32)],
        compiler_params=pltpu.CompilerParams(vmem_limit_bytes=16 << 20),
        name="project_other",
    )(other_x, other_flags, weight, vectors, left, right)

    steps = routes(n)
    lefts = [left] + [
        lax.ppermute(left, "seq", [(p, p ^ k * CORES) for p in range(n)]) for k in range(1, n // CORES)
    ]
    rights = [
        lax.ppermute(right, axes, [(a * n + p, step[a][p] * n + a) for a in range(n) for p in range(n)])
        for step in steps
    ]
    return pl.pallas_call(
        functools.partial(pair_kernel, steps, seqs, rows, rows, width),
        out_shape=jax.ShapeDtypeStruct((rows, rows, outs), BF16),
        scratch_shapes=[
            pltpu.VMEM((n * seqs, lanes), BF16),
            pltpu.VMEM((n * seqs, lanes), BF16),
            pltpu.VMEM((n * seqs // LANES, lanes, LANES), F32),
            pltpu.VMEM((rows * rows, width * width), BF16),
            pltpu.VMEM((rows * rows, outs), F32),
        ],
        compiler_params=pltpu.CompilerParams(vmem_limit_bytes=24 << 20),
        name="pair",
    )(*lefts, *rights, w, bias)


def solution(mesh):
    n = mesh.shape["res"]
    assert n == mesh.shape["seq"] and n & (n - 1) == 0 and n % CORES == 0
    in_specs = (P(("group", "seq"), "res", None), P(("group", "seq"), "res")) + (P(),) * 8
    return jax.shard_map(
        functools.partial(local, n), mesh=mesh, in_specs=in_specs,
        out_specs=P(("group", "res"), "seq", None), check_vma=False,
    )
```

```python
import functools

import jax
import jax.numpy as jnp
from jax import lax
from jax.experimental import pallas as pl
from jax.experimental.pallas import tpu as pltpu
from jax.sharding import PartitionSpec as P

LANES = 128
CORES = 2
F32 = jnp.float32
BF16 = jnp.bfloat16
TN = (((0,), (0,)), ((), ()))
NT = (((1,), (1,)), ((), ()))
NN = (((1,), (0,)), ((), ()))


def dot(a, b, dims=NN):
    return lax.dot_general(a, b, dims, preferred_element_type=F32)


def iota(shape, dim):
    return lax.broadcasted_iota(jnp.int32, shape, dim)


ROUTES = (
    ((2, 0, 3, 1), (1, 0, 2, 3), (1, 3, 0, 2), (1, 3, 0, 2)),
    ((3, 1, 2, 0), (2, 3, 1, 0), (2, 0, 3, 1), (2, 0, 3, 1)),
)


def routes(n):
    if n == 4:
        return ROUTES
    steps = [m for m in range(n) if bin(m).count("1") % 2 == 1]
    return tuple(tuple(tuple(p ^ m for p in range(n)) for a in range(n)) for m in steps)


def sending_chip(step, r, q):
    n = len(step)
    chip = 0
    for bit in range((n // CORES - 1).bit_length()):
        for a in range(n):
            word = sum((step[a].index(to) // CORES >> bit & 1) << to for to in range(n))
            chip = chip | jnp.where(q == a, (jnp.int32(word) >> r & 1) << bit, 0)
    return chip


def project_block(width, x_ref, flag_ref, weight, vectors, block, left_ref, right_ref, proj_ref):
    seqs, rows, depth = x_ref.shape
    fold = LANES // width
    lanes = rows * width
    data = lanes // LANES * seqs
    x = x_ref[...].astype(F32).reshape(seqs * rows, depth)
    center = jnp.mean(x, axis=-1, keepdims=True)
    x = x - center
    spread = jnp.mean(x * x, axis=-1, keepdims=True)
    normed = x * lax.rsqrt(spread + 1e-05) * vectors[0:1] + vectors[1:2]
    both = dot(normed.astype(BF16), weight, NT) + vectors[2:3]
    proj_ref[0] = both[:, :LANES]
    proj_ref[1] = both[:, LANES:]

    flags = flag_ref[...].astype(F32)
    spreader = (iota((rows, lanes), 1) // width == iota((rows, lanes), 0)).astype(BF16)
    mask = dot(flags.astype(BF16), spreader, TN)
    flags = jnp.concatenate([flags] * (LANES // seqs), axis=1)
    lane_block = iota((rows, LANES), 1) // seqs

    place = iota((seqs, LANES), 1) // width
    for half, out_ref in ((0, left_ref), (1, right_ref)):
        for tile in range(rows // fold):
            merged = proj_ref[half, pl.ds(tile * fold, seqs, stride=rows), :]
            for k in range(1, fold):
                part = proj_ref[half, pl.ds(tile * fold + k, seqs, stride=rows), :]
                merged = jnp.where(place == k, part, merged)
            merged = merged * mask[:, tile * LANES:(tile + 1) * LANES]
            out_ref[tile * seqs:(tile + 1) * seqs, :] = merged.astype(BF16)
        for tile in range((out_ref.shape[0] - data) // rows):
            mine = jnp.where(lane_block + tile * (LANES // seqs) == block, flags, 0.0)
            out_ref[data + tile * rows:data + (tile + 1) * rows, :] = mine.astype(BF16)


def own_kernel(x_hbm, flag_hbm, scale_hbm, shift_hbm, wl_hbm, bl_hbm, wr_hbm, br_hbm, last_hbm,
               left_ref, right_ref, weight_ref, vector_ref,
               x_ref, flag_ref, scale_ref, shift_ref, wl_ref, bl_ref, wr_ref, br_ref, last_ref, proj_ref, sems):
    copies = [
        pltpu.make_async_copy(src, dst, sems.at[k])
        for k, (src, dst) in enumerate((
            (x_hbm, x_ref), (flag_hbm, flag_ref), (scale_hbm, scale_ref), (shift_hbm, shift_ref),
            (wl_hbm, wl_ref), (bl_hbm, bl_ref), (wr_hbm, wr_ref), (br_hbm, br_ref), (last_hbm, last_ref),
        ))
    ]
    for copy in copies:
        copy.start()
    for copy in copies:
        copy.wait()
    width, depth = wl_ref.shape
    fold = LANES // width
    weight = jnp.concatenate([wl_ref[...]] * fold + [wr_ref[...]] * fold, axis=0)
    bias = [bl_ref[...].reshape(1, width)] * fold + [br_ref[...].reshape(1, width)] * fold
    vectors = jnp.concatenate(
        [
            scale_ref[...].reshape(1, depth),
            shift_ref[...].reshape(1, depth),
            jnp.concatenate(bias, axis=1),
            jnp.concatenate([last_ref[...].reshape(1, LANES)] * (depth // LANES), axis=1),
            jnp.zeros((4, depth), F32),
        ],
        axis=0,
    )
    weight_ref[...] = weight
    vector_ref[...] = vectors
    project_block(width, x_ref, flag_ref, weight, vectors, lax.axis_index("seq"), left_ref, right_ref, proj_ref)


def both_kernel(width, x_ref, flag_ref, weight_ref, vector_ref, own_left_ref, own_right_ref, left_ref, right_ref, proj_ref):
    block = lax.axis_index("seq")
    core = block % CORES
    left_ref[core] = own_left_ref[...]
    right_ref[core] = own_right_ref[...]
    other = 1 - core
    project_block(
        width, x_ref, flag_ref, weight_ref[...], vector_ref[...], block + other - core,
        left_ref.at[other], right_ref.at[other], proj_ref,
    )


def whole_mask(pieces, rows, data):
    total = functools.reduce(jnp.add, [p[k, data:, :] for p in pieces for k in range(CORES)])
    return jnp.concatenate([total[k:k + rows] for k in range(0, total.shape[0], rows)], axis=1)


def gather_factor(pieces, chips, seqs, data, whole_ref):
    for piece, chip in zip(pieces, chips):
        for core in range(CORES):
            at = pl.multiple_of((chip * CORES + core) * seqs, seqs)
            for tile in range(data // seqs):
                whole_ref[pl.ds(at, seqs), tile * LANES:(tile + 1) * LANES] = (
                    piece[core, tile * seqs:(tile + 1) * seqs, :]
                )


def left_kernel(seqs, rows, width, *refs):
    lefts, (out_ref, mask_ref, left_ref, turned_ref) = refs[:-4], refs[-4:]
    data = rows * width // LANES * seqs
    me = lax.axis_index("seq") // CORES
    gather_factor(lefts, [me ^ k for k in range(len(lefts))], seqs, data, left_ref)
    mask_ref[...] = whole_mask(lefts, rows, data)
    for tile in range(turned_ref.shape[0]):
        turned_ref[tile] = left_ref[tile * LANES:(tile + 1) * LANES, :].astype(F32).T
        for c in range(width):
            out_ref[c * rows:(c + 1) * rows, tile * LANES:(tile + 1) * LANES] = (
                turned_ref[tile, pl.ds(c, rows, stride=width), :].astype(BF16)
            )


def pair_kernel(steps, seqs, rows, columns, width, *refs):
    n = len(steps)
    rights = refs[:n]
    turned_ref, live_ref, w_ref, vector_ref, out_ref, right_ref, flat_ref, raw_ref = refs[n:]
    fold = LANES // width
    assert fold == 4
    data = rows * width // LANES * seqs

    me_res, me_seq = lax.axis_index("res"), lax.axis_index("seq")
    gather_factor(rights, [sending_chip(step, me_res, me_seq) for step in steps], seqs, data, right_ref)
    outer = dot(turned_ref[...], right_ref[...]).astype(BF16)

    place = (iota((rows, LANES), 1) // width).astype(BF16)
    even = [None] * fold
    even[1] = (place == 0.0) | (place == 2.0)
    even[2] = (place == 0.0) | (place == 1.0)
    for tile in range(columns // fold):
        for quad in range(width // fold):
            part = [
                outer[(quad * fold + k) * rows:(quad * fold + k + 1) * rows, tile * LANES:(tile + 1) * LANES]
                for k in range(fold)
            ]
            for step in (2, 1):
                new = list(part)
                for k in range(fold):
                    if k & step == 0:
                        x, y = part[k], part[k + step]
                        new[k] = jnp.where(even[step], x, pltpu.roll(y, step * width, 1))
                        new[k + step] = jnp.where(even[step], pltpu.roll(x, LANES - step * width, 1), y)
                part = new
            for k in range(fold):
                j = tile * fold + k
                flat_ref[j * rows:(j + 1) * rows, quad * LANES:(quad + 1) * LANES] = part[k]

    raw = dot(flat_ref[...], w_ref[...]) + vector_ref[3:4, :LANES]
    count = dot(live_ref[...], whole_mask(rights, rows, data), NT)
    scale = 1.0 / (1.0 + count)
    for j in range(columns):
        raw_ref[j * rows:(j + 1) * rows, :] = raw[j * rows:(j + 1) * rows, :] * scale[:, j:j + 1]
    for i in range(rows):
        out_ref[i] = raw_ref[pl.ds(i, columns, stride=rows), :].astype(BF16)


def local(n, x, flags, scale, shift, wl, bl, wr, br, w, bias):
    seqs, rows, depth = x.shape
    width = wl.shape[1]
    outs = w.shape[1]
    lanes = rows * width
    size = lanes // LANES * seqs + rows * pl.cdiv(n * seqs, LANES)
    axes = ("res", "seq")
    flags = flags.T

    swap = [(p, p ^ 1) for p in range(n)]
    other_x, other_flags = lax.ppermute(x, "seq", swap), lax.ppermute(flags, "seq", swap)

    operands = [
        pltpu.with_memory_space_constraint(o, pltpu.HBM) for o in (x, flags, scale, shift, wl.T, bl, wr.T, br, bias)
    ]
    wire = jax.ShapeDtypeStruct((size, LANES), BF16)
    left, right, weight, vectors = pl.pallas_call(
        own_kernel,
        out_shape=(
            wire, wire,
            jax.ShapeDtypeStruct((2 * LANES, depth), BF16),
            jax.ShapeDtypeStruct((8, 2 * LANES), F32),
        ),
        in_specs=[pl.BlockSpec(memory_space=pltpu.HBM)] * len(operands),
        scratch_shapes=[pltpu.VMEM(o.shape, o.dtype) for o in operands] + [
            pltpu.VMEM((2, seqs * rows, LANES), F32),
            pltpu.SemaphoreType.DMA((len(operands),)),
        ],
        compiler_params=pltpu.CompilerParams(vmem_limit_bytes=16 << 20),
        cost_estimate=pl.CostEstimate(flops=1 << 25, bytes_accessed=x.size * 8, transcendentals=0),
        name="project_own",
    )(*operands)
    wire = jax.ShapeDtypeStruct((CORES, size, LANES), BF16)
    left, right = pl.pallas_call(
        functools.partial(both_kernel, width),
        out_shape=(wire, wire),
        scratch_shapes=[pltpu.VMEM((2, seqs * rows, LANES), F32)],
        compiler_params=pltpu.CompilerParams(vmem_limit_bytes=16 << 20),
        name="project_other",
    )(other_x, other_flags, weight, vectors, left, right)

    steps = routes(n)
    lefts = [left] + [
        lax.ppermute(left, "seq", [(p, p ^ k * CORES) for p in range(n)]) for k in range(1, n // CORES)
    ]
    rights = [
        lax.ppermute(right, axes, [(a * n + p, step[a][p] * n + a) for a in range(n) for p in range(n)])
        for step in steps
    ]
    turned, live = pl.pallas_call(
        functools.partial(left_kernel, seqs, rows, width),
        out_shape=(jax.ShapeDtypeStruct((lanes, n * seqs), BF16), jax.ShapeDtypeStruct((rows, n * seqs), BF16)),
        scratch_shapes=[
            pltpu.VMEM((n * seqs, lanes), BF16),
            pltpu.VMEM((n * seqs // LANES, lanes, LANES), F32),
        ],
        compiler_params=pltpu.CompilerParams(vmem_limit_bytes=16 << 20),
        name="turn_left",
    )(*lefts)
    return pl.pallas_call(
        functools.partial(pair_kernel, steps, seqs, rows, rows, width),
        out_shape=jax.ShapeDtypeStruct((rows, rows, outs), BF16),
        scratch_shapes=[
            pltpu.VMEM((n * seqs, lanes), BF16),
            pltpu.VMEM((rows * rows, width * width), BF16),
            pltpu.VMEM((rows * rows, outs), F32),
        ],
        compiler_params=pltpu.CompilerParams(vmem_limit_bytes=16 << 20),
        name="pair",
    )(*rights, turned, live, w, vectors)


def solution(mesh):
    n = mesh.shape["res"]
    assert n == mesh.shape["seq"] and n & (n - 1) == 0 and n % CORES == 0
    in_specs = (P(("group", "seq"), "res", None), P(("group", "seq"), "res")) + (P(),) * 8
    return jax.shard_map(
        functools.partial(local, n), mesh=mesh, in_specs=in_specs,
        out_specs=P(("group", "res"), "seq", None), check_vma=False,
    )
```

```python
import functools

import jax
import jax.numpy as jnp
from jax import lax
from jax.experimental import pallas as pl
from jax.experimental.pallas import tpu as pltpu
from jax.sharding import PartitionSpec as P

LANES = 128
CORES = 2
F32 = jnp.float32
BF16 = jnp.bfloat16
TN = (((0,), (0,)), ((), ()))
NT = (((1,), (1,)), ((), ()))
NN = (((1,), (0,)), ((), ()))


def dot(a, b, dims=NN):
    return lax.dot_general(a, b, dims, preferred_element_type=F32)


def iota(shape, dim):
    return lax.broadcasted_iota(jnp.int32, shape, dim)


ROUTES = (
    ((2, 0, 3, 1), (1, 0, 2, 3), (1, 3, 0, 2), (1, 3, 0, 2)),
    ((3, 1, 2, 0), (2, 3, 1, 0), (2, 0, 3, 1), (2, 0, 3, 1)),
)


def routes(n):
    if n == 4:
        return ROUTES
    steps = [m for m in range(n) if bin(m).count("1") % 2 == 1]
    return tuple(tuple(tuple(p ^ m for p in range(n)) for a in range(n)) for m in steps)


def sending_chip(step, r, q):
    n = len(step)
    chip = 0
    for bit in range((n // CORES - 1).bit_length()):
        for a in range(n):
            word = sum((step[a].index(to) // CORES >> bit & 1) << to for to in range(n))
            chip = chip | jnp.where(q == a, (jnp.int32(word) >> r & 1) << bit, 0)
    return chip


def project_constants(seqs, rows, width, block, copies):
    lanes = rows * width
    spreader = (iota((rows, lanes), 1) // width == iota((rows, lanes), 0)).astype(BF16)
    place = iota((seqs, LANES), 1) // width
    mine = [iota((rows, LANES), 1) // seqs + tile * (LANES // seqs) == block for tile in range(copies)]
    return spreader, place, mine


def project_block(width, x_ref, flag_ref, weight, vectors, constants, chunks, left_ref, right_ref, proj_ref):
    seqs, rows, depth = x_ref.shape
    fold = LANES // width
    assert fold == 4
    lanes = rows * width
    data = lanes // LANES * seqs
    spreader, place, mine = constants
    part = seqs // len(chunks)
    for k, wait in enumerate(chunks):
        wait()
        x = x_ref[k * part:(k + 1) * part].astype(F32).reshape(part * rows, depth)
        center = jnp.mean(x, axis=-1, keepdims=True)
        x = x - center
        spread = jnp.mean(x * x, axis=-1, keepdims=True)
        normed = x * lax.rsqrt(spread + 1e-05) * vectors[0:1] + vectors[1:2]
        proj_ref[k * part * rows:(k + 1) * part * rows, :] = dot(normed.astype(BF16), weight, NT) + vectors[2:3, :LANES]

    flags = flag_ref[...].astype(F32)
    mask = dot(flags.astype(BF16), spreader, TN)
    flags = jnp.concatenate([flags] * (LANES // seqs), axis=1)
    for tile in range(rows // fold):
        own = [proj_ref[pl.ds(tile * fold + k, seqs, stride=rows), :] for k in range(fold)]
        moved = [pltpu.roll(p, width, 1) for p in own]
        where = slice(tile * LANES, (tile + 1) * LANES)
        for out_ref, (g0, g1, g2, g3) in (
            (left_ref, (own[0], moved[1], own[2], moved[3])),
            (right_ref, (moved[0], own[1], moved[2], own[3])),
        ):
            merged = jnp.where(place < 2, jnp.where(place == 0, g0, g1), jnp.where(place == 2, g2, g3))
            out_ref[tile * seqs:(tile + 1) * seqs, :] = (merged * mask[:, where]).astype(BF16)
    for tile, here in enumerate(mine):
        placed = jnp.where(here, flags, 0.0).astype(BF16)
        for out_ref in (left_ref, right_ref):
            out_ref[data + tile * rows:data + (tile + 1) * rows, :] = placed


def own_kernel(chunks, x_hbm, flag_hbm, scale_hbm, shift_hbm, wl_hbm, bl_hbm, wr_hbm, br_hbm, last_hbm,
               left_ref, right_ref, weight_ref, vector_ref,
               x_ref, flag_ref, scale_ref, shift_ref, wl_ref, bl_ref, wr_ref, br_ref, last_ref, proj_ref, sems):
    seqs, rows, depth = x_ref.shape
    part = seqs // chunks
    copies = [
        pltpu.make_async_copy(src, dst, sems.at[k])
        for k, (src, dst) in enumerate((
            (wl_hbm, wl_ref), (wr_hbm, wr_ref), (scale_hbm, scale_ref), (shift_hbm, shift_ref),
            (bl_hbm, bl_ref), (br_hbm, br_ref),
            *((x_hbm.at[k * part:(k + 1) * part], x_ref.at[k * part:(k + 1) * part]) for k in range(chunks)),
            (flag_hbm, flag_ref), (last_hbm, last_ref),
        ))
    ]
    for copy in copies:
        copy.start()
    width = wl_ref.shape[0]
    fold = LANES // width
    data = rows * width // LANES * seqs
    constants = project_constants(seqs, rows, width, lax.axis_index("seq"), (left_ref.shape[0] - data) // rows)
    for copy in copies[:6]:
        copy.wait()
    weight = jnp.concatenate([wl_ref[...], wr_ref[...]] * (fold // 2), axis=0)
    bias = [bl_ref[...].reshape(1, width), br_ref[...].reshape(1, width)] * (fold // 2)
    bias = jnp.concatenate(bias + [jnp.zeros((1, depth - LANES), F32)], axis=1)
    vectors = jnp.concatenate([scale_ref[...].reshape(1, depth), shift_ref[...].reshape(1, depth), bias], axis=0)

    def last_chunk():
        for copy in copies[5 + chunks:]:
            copy.wait()

    waits = [copy.wait for copy in copies[6:5 + chunks]] + [last_chunk]
    project_block(width, x_ref, flag_ref, weight, vectors, constants, waits, left_ref, right_ref, proj_ref)
    weight_ref[...] = weight
    last = jnp.concatenate([last_ref[...].reshape(1, LANES)] * (depth // LANES), axis=1)
    vector_ref[...] = jnp.concatenate([vectors, last, jnp.zeros((4, depth), F32)], axis=0)


def both_kernel(width, x_ref, flag_ref, weight_ref, vector_ref, own_left_ref, own_right_ref, left_ref, right_ref, proj_ref):
    seqs, rows, _ = x_ref.shape
    block = lax.axis_index("seq")
    core = block % CORES
    left_ref[core] = own_left_ref[...]
    right_ref[core] = own_right_ref[...]
    other = 1 - core
    data = rows * width // LANES * seqs
    constants = project_constants(seqs, rows, width, block + other - core, (left_ref.shape[1] - data) // rows)
    project_block(
        width, x_ref, flag_ref, weight_ref[...], vector_ref[...], constants, [lambda: None],
        left_ref.at[other], right_ref.at[other], proj_ref,
    )


def whole_mask(pieces, rows, data):
    total = functools.reduce(jnp.add, [p[k, data:, :] for p in pieces for k in range(CORES)])
    return jnp.concatenate([total[k:k + rows] for k in range(0, total.shape[0], rows)], axis=1)


def gather_factor(pieces, chips, seqs, data, whole_ref):
    for piece, chip in zip(pieces, chips):
        for core in range(CORES):
            at = pl.multiple_of((chip * CORES + core) * seqs, seqs)
            for tile in range(data // seqs):
                whole_ref[pl.ds(at, seqs), tile * LANES:(tile + 1) * LANES] = (
                    piece[core, tile * seqs:(tile + 1) * seqs, :]
                )


def left_kernel(seqs, rows, width, *refs):
    lefts, (out_ref, mask_ref, left_ref, turned_ref) = refs[:-4], refs[-4:]
    data = rows * width // LANES * seqs
    me = lax.axis_index("seq") // CORES
    gather_factor(lefts, [me ^ k for k in range(len(lefts))], seqs, data, left_ref)
    mask_ref[...] = whole_mask(lefts, rows, data)
    for tile in range(turned_ref.shape[0]):
        turned_ref[tile] = left_ref[tile * LANES:(tile + 1) * LANES, :].astype(F32).T
        for c in range(width):
            out_ref[c * rows:(c + 1) * rows, tile * LANES:(tile + 1) * LANES] = (
                turned_ref[tile, pl.ds(c, rows, stride=width), :].astype(BF16)
            )


def pair_kernel(steps, seqs, rows, columns, width, *refs):
    n = len(steps)
    rights = refs[:n]
    turned_ref, live_ref, w_ref, vector_ref, out_ref, right_ref, flat_ref, raw_ref = refs[n:]
    fold = LANES // width
    assert fold == 4
    data = rows * width // LANES * seqs

    me_res, me_seq = lax.axis_index("res"), lax.axis_index("seq")
    gather_factor(rights, [sending_chip(step, me_res, me_seq) for step in steps], seqs, data, right_ref)
    outer = dot(turned_ref[...], right_ref[...]).astype(BF16)

    place = (iota((rows, LANES), 1) // width).astype(BF16)
    even = [None] * fold
    even[1] = (place == 0.0) | (place == 2.0)
    even[2] = (place == 0.0) | (place == 1.0)
    for tile in range(columns // fold):
        for quad in range(width // fold):
            part = [
                outer[(quad * fold + k) * rows:(quad * fold + k + 1) * rows, tile * LANES:(tile + 1) * LANES]
                for k in range(fold)
            ]
            for step in (2, 1):
                new = list(part)
                for k in range(fold):
                    if k & step == 0:
                        x, y = part[k], part[k + step]
                        new[k] = jnp.where(even[step], x, pltpu.roll(y, step * width, 1))
                        new[k + step] = jnp.where(even[step], pltpu.roll(x, LANES - step * width, 1), y)
                part = new
            for k in range(fold):
                j = tile * fold + k
                flat_ref[j * rows:(j + 1) * rows, quad * LANES:(quad + 1) * LANES] = part[k]

    raw = dot(flat_ref[...], w_ref[...]) + vector_ref[3:4, :LANES]
    count = dot(live_ref[...], whole_mask(rights, rows, data), NT)
    scale = 1.0 / (1.0 + count)
    for j in range(columns):
        raw_ref[j * rows:(j + 1) * rows, :] = raw[j * rows:(j + 1) * rows, :] * scale[:, j:j + 1]
    for i in range(rows):
        out_ref[i] = raw_ref[pl.ds(i, columns, stride=rows), :].astype(BF16)


def local(n, x, flags, scale, shift, wl, bl, wr, br, w, bias):
    seqs, rows, depth = x.shape
    width = wl.shape[1]
    outs = w.shape[1]
    lanes = rows * width
    size = lanes // LANES * seqs + rows * pl.cdiv(n * seqs, LANES)
    axes = ("res", "seq")
    flags = flags.T

    swap = [(p, p ^ 1) for p in range(n)]
    other_x, other_flags = lax.ppermute(x, "seq", swap), lax.ppermute(flags, "seq", swap)

    chunks = 4
    operands = [
        pltpu.with_memory_space_constraint(o, pltpu.HBM) for o in (x, flags, scale, shift, wl.T, bl, wr.T, br, bias)
    ]
    wire = jax.ShapeDtypeStruct((size, LANES), BF16)
    left, right, weight, vectors = pl.pallas_call(
        functools.partial(own_kernel, chunks),
        out_shape=(
            wire, wire,
            jax.ShapeDtypeStruct((LANES, depth), BF16),
            jax.ShapeDtypeStruct((8, depth), F32),
        ),
        in_specs=[pl.BlockSpec(memory_space=pltpu.HBM)] * len(operands),
        scratch_shapes=[pltpu.VMEM(o.shape, o.dtype) for o in operands] + [
            pltpu.VMEM((seqs * rows, LANES), F32),
            pltpu.SemaphoreType.DMA((len(operands) - 1 + chunks,)),
        ],
        compiler_params=pltpu.CompilerParams(vmem_limit_bytes=16 << 20),
        cost_estimate=pl.CostEstimate(flops=1 << 25, bytes_accessed=x.size * 8, transcendentals=0),
        name="project_own",
    )(*operands)
    wire = jax.ShapeDtypeStruct((CORES, size, LANES), BF16)
    left, right = pl.pallas_call(
        functools.partial(both_kernel, width),
        out_shape=(wire, wire),
        scratch_shapes=[pltpu.VMEM((seqs * rows, LANES), F32)],
        compiler_params=pltpu.CompilerParams(vmem_limit_bytes=16 << 20),
        name="project_other",
    )(other_x, other_flags, weight, vectors, left, right)

    steps = routes(n)
    lefts = [left] + [
        lax.ppermute(left, "seq", [(p, p ^ k * CORES) for p in range(n)]) for k in range(1, n // CORES)
    ]
    rights = [
        lax.ppermute(right, axes, [(a * n + p, step[a][p] * n + a) for a in range(n) for p in range(n)])
        for step in steps
    ]
    turned, live = pl.pallas_call(
        functools.partial(left_kernel, seqs, rows, width),
        out_shape=(jax.ShapeDtypeStruct((lanes, n * seqs), BF16), jax.ShapeDtypeStruct((rows, n * seqs), BF16)),
        scratch_shapes=[
            pltpu.VMEM((n * seqs, lanes), BF16),
            pltpu.VMEM((n * seqs // LANES, lanes, LANES), F32),
        ],
        compiler_params=pltpu.CompilerParams(vmem_limit_bytes=16 << 20),
        name="turn_left",
    )(*lefts)
    return pl.pallas_call(
        functools.partial(pair_kernel, steps, seqs, rows, rows, width),
        out_shape=jax.ShapeDtypeStruct((rows, rows, outs), BF16),
        scratch_shapes=[
            pltpu.VMEM((n * seqs, lanes), BF16),
            pltpu.VMEM((rows * rows, width * width), BF16),
            pltpu.VMEM((rows * rows, outs), F32),
        ],
        compiler_params=pltpu.CompilerParams(vmem_limit_bytes=16 << 20),
        name="pair",
    )(*rights, turned, live, w, vectors)


def solution(mesh):
    n = mesh.shape["res"]
    assert n == mesh.shape["seq"] and n & (n - 1) == 0 and n % CORES == 0
    in_specs = (P(("group", "seq"), "res", None), P(("group", "seq"), "res")) + (P(),) * 8
    return jax.shard_map(
        functools.partial(local, n), mesh=mesh, in_specs=in_specs,
        out_specs=P(("group", "res"), "seq", None), check_vma=False,
    )
```

```python
import functools

import jax
import jax.numpy as jnp
from jax import lax
from jax.experimental import pallas as pl
from jax.experimental.pallas import tpu as pltpu
from jax.sharding import PartitionSpec as P

LANES = 128
CORES = 2
F32 = jnp.float32
BF16 = jnp.bfloat16
TN = (((0,), (0,)), ((), ()))
NT = (((1,), (1,)), ((), ()))
NN = (((1,), (0,)), ((), ()))


def dot(a, b, dims=NN):
    return lax.dot_general(a, b, dims, preferred_element_type=F32)


def iota(shape, dim):
    return lax.broadcasted_iota(jnp.int32, shape, dim)


ROUTES = (
    ((2, 0, 3, 1), (1, 0, 2, 3), (1, 3, 0, 2), (1, 3, 0, 2)),
    ((3, 1, 2, 0), (2, 3, 1, 0), (2, 0, 3, 1), (2, 0, 3, 1)),
)


def routes(n):
    if n == 4:
        return ROUTES
    steps = [m for m in range(n) if bin(m).count("1") % 2 == 1]
    return tuple(tuple(tuple(p ^ m for p in range(n)) for a in range(n)) for m in steps)


def sending_chip(step, r, q):
    n = len(step)
    chip = 0
    for bit in range((n // CORES - 1).bit_length()):
        for a in range(n):
            word = sum((step[a].index(to) // CORES >> bit & 1) << to for to in range(n))
            chip = chip | jnp.where(q == a, (jnp.int32(word) >> r & 1) << bit, 0)
    return chip


def project_constants(seqs, rows, width, block, tiles):
    lanes = rows * width
    spreader = (iota((rows, lanes), 1) // width == iota((rows, lanes), 0)).astype(BF16)
    place = iota((seqs, LANES), 1) // width
    mine = [iota((rows, LANES), 1) // seqs + tile * (LANES // seqs) == block for tile in range(tiles)]
    return spreader, place, mine


def project_block(width, x_ref, flag_ref, weight, vectors, constants, left_ref, right_ref, proj_ref):
    seqs, rows, depth = x_ref.shape
    fold = LANES // width
    lanes = rows * width
    data = lanes // LANES * seqs
    spreader, place, mine = constants
    x = x_ref[...].astype(F32).reshape(seqs * rows, depth)
    center = jnp.mean(x, axis=-1, keepdims=True)
    x = x - center
    spread = jnp.mean(x * x, axis=-1, keepdims=True)
    normed = x * lax.rsqrt(spread + 1e-05) * vectors[0:1] + vectors[1:2]
    both = dot(normed.astype(BF16), weight, NT) + vectors[2:3]
    proj_ref[0] = both[:, :LANES]
    proj_ref[1] = both[:, LANES:]

    flags = flag_ref[...].astype(F32)
    mask = dot(flags.astype(BF16), spreader, TN)
    flags = jnp.concatenate([flags] * (LANES // seqs), axis=1)

    for half, out_ref in ((0, left_ref), (1, right_ref)):
        for tile in range(rows // fold):
            merged = proj_ref[half, pl.ds(tile * fold, seqs, stride=rows), :]
            for k in range(1, fold):
                part = proj_ref[half, pl.ds(tile * fold + k, seqs, stride=rows), :]
                merged = jnp.where(place == k, part, merged)
            merged = merged * mask[:, tile * LANES:(tile + 1) * LANES]
            out_ref[tile * seqs:(tile + 1) * seqs, :] = merged.astype(BF16)
        for tile, here in enumerate(mine):
            out_ref[data + tile * rows:data + (tile + 1) * rows, :] = jnp.where(here, flags, 0.0).astype(BF16)


def own_kernel(chunks, x_hbm, flag_hbm, scale_hbm, shift_hbm, wl_hbm, bl_hbm, wr_hbm, br_hbm, last_hbm,
               left_ref, right_ref, weight_ref, vector_ref,
               x_ref, flag_ref, scale_ref, shift_ref, wl_ref, bl_ref, wr_ref, br_ref, last_ref, proj_ref, sems):
    seqs, rows, depth = x_ref.shape
    part = seqs // chunks
    copies = [
        pltpu.make_async_copy(src, dst, sems.at[k])
        for k, (src, dst) in enumerate((
            *((x_hbm.at[k * part:(k + 1) * part], x_ref.at[k * part:(k + 1) * part]) for k in range(chunks)),
            (flag_hbm, flag_ref), (scale_hbm, scale_ref), (shift_hbm, shift_ref),
            (wl_hbm, wl_ref), (bl_hbm, bl_ref), (wr_hbm, wr_ref), (br_hbm, br_ref), (last_hbm, last_ref),
        ))
    ]
    for copy in copies:
        copy.start()
    width = wl_ref.shape[0]
    data = rows * width // LANES * seqs
    constants = project_constants(seqs, rows, width, lax.axis_index("seq"), (left_ref.shape[0] - data) // rows)
    for copy in copies:
        copy.wait()
    fold = LANES // width
    weight = jnp.concatenate([wl_ref[...]] * fold + [wr_ref[...]] * fold, axis=0)
    bias = [bl_ref[...].reshape(1, width)] * fold + [br_ref[...].reshape(1, width)] * fold
    vectors = jnp.concatenate(
        [
            scale_ref[...].reshape(1, depth),
            shift_ref[...].reshape(1, depth),
            jnp.concatenate(bias, axis=1),
            jnp.concatenate([last_ref[...].reshape(1, LANES)] * (depth // LANES), axis=1),
            jnp.zeros((4, depth), F32),
        ],
        axis=0,
    )
    weight_ref[...] = weight
    vector_ref[...] = vectors
    project_block(width, x_ref, flag_ref, weight, vectors, constants, left_ref, right_ref, proj_ref)


def both_kernel(width, x_ref, flag_ref, weight_ref, vector_ref, own_left_ref, own_right_ref, left_ref, right_ref, proj_ref):
    block = lax.axis_index("seq")
    core = block % CORES
    left_ref[core] = own_left_ref[...]
    right_ref[core] = own_right_ref[...]
    other = 1 - core
    seqs, rows, _ = x_ref.shape
    data = rows * width // LANES * seqs
    constants = project_constants(seqs, rows, width, block + other - core, (left_ref.shape[1] - data) // rows)
    project_block(
        width, x_ref, flag_ref, weight_ref[...], vector_ref[...], constants,
        left_ref.at[other], right_ref.at[other], proj_ref,
    )


def whole_mask(pieces, rows, data):
    total = functools.reduce(jnp.add, [p[k, data:, :] for p in pieces for k in range(CORES)])
    return jnp.concatenate([total[k:k + rows] for k in range(0, total.shape[0], rows)], axis=1)


def gather_factor(pieces, chips, seqs, data, whole_ref):
    for piece, chip in zip(pieces, chips):
        for core in range(CORES):
            at = pl.multiple_of((chip * CORES + core) * seqs, seqs)
            for tile in range(data // seqs):
                whole_ref[pl.ds(at, seqs), tile * LANES:(tile + 1) * LANES] = (
                    piece[core, tile * seqs:(tile + 1) * seqs, :]
                )


def left_kernel(seqs, rows, width, *refs):
    lefts, (out_ref, mask_ref, left_ref, turned_ref) = refs[:-4], refs[-4:]
    data = rows * width // LANES * seqs
    me = lax.axis_index("seq") // CORES
    gather_factor(lefts, [me ^ k for k in range(len(lefts))], seqs, data, left_ref)
    mask_ref[...] = whole_mask(lefts, rows, data)
    for tile in range(turned_ref.shape[0]):
        turned_ref[tile] = left_ref[tile * LANES:(tile + 1) * LANES, :].astype(F32).T
        for c in range(width):
            out_ref[c * rows:(c + 1) * rows, tile * LANES:(tile + 1) * LANES] = (
                turned_ref[tile, pl.ds(c, rows, stride=width), :].astype(BF16)
            )


def pair_kernel(steps, seqs, rows, columns, width, *refs):
    n = len(steps)
    rights = refs[:n]
    turned_ref, live_ref, w_ref, vector_ref, out_ref, right_ref, flat_ref, raw_ref = refs[n:]
    fold = LANES // width
    assert fold == 4
    data = rows * width // LANES * seqs

    me_res, me_seq = lax.axis_index("res"), lax.axis_index("seq")
    gather_factor(rights, [sending_chip(step, me_res, me_seq) for step in steps], seqs, data, right_ref)
    outer = dot(turned_ref[...], right_ref[...]).astype(BF16)

    place = (iota((rows, LANES), 1) // width).astype(BF16)
    even = [None] * fold
    even[1] = (place == 0.0) | (place == 2.0)
    even[2] = (place == 0.0) | (place == 1.0)
    for tile in range(columns // fold):
        for quad in range(width // fold):
            part = [
                outer[(quad * fold + k) * rows:(quad * fold + k + 1) * rows, tile * LANES:(tile + 1) * LANES]
                for k in range(fold)
            ]
            for step in (2, 1):
                new = list(part)
                for k in range(fold):
                    if k & step == 0:
                        x, y = part[k], part[k + step]
                        new[k] = jnp.where(even[step], x, pltpu.roll(y, step * width, 1))
                        new[k + step] = jnp.where(even[step], pltpu.roll(x, LANES - step * width, 1), y)
                part = new
            for k in range(fold):
                j = tile * fold + k
                flat_ref[j * rows:(j + 1) * rows, quad * LANES:(quad + 1) * LANES] = part[k]

    raw = dot(flat_ref[...], w_ref[...]) + vector_ref[3:4, :LANES]
    count = dot(live_ref[...], whole_mask(rights, rows, data), NT)
    scale = 1.0 / (1.0 + count)
    for j in range(columns):
        raw_ref[j * rows:(j + 1) * rows, :] = raw[j * rows:(j + 1) * rows, :] * scale[:, j:j + 1]
    for i in range(rows):
        out_ref[i] = raw_ref[pl.ds(i, columns, stride=rows), :].astype(BF16)


def local(n, x, flags, scale, shift, wl, bl, wr, br, w, bias):
    seqs, rows, depth = x.shape
    width = wl.shape[1]
    outs = w.shape[1]
    lanes = rows * width
    size = lanes // LANES * seqs + rows * pl.cdiv(n * seqs, LANES)
    axes = ("res", "seq")
    flags = flags.T

    swap = [(p, p ^ 1) for p in range(n)]
    other_x, other_flags = lax.ppermute(x, "seq", swap), lax.ppermute(flags, "seq", swap)

    chunks = 4
    operands = [
        pltpu.with_memory_space_constraint(o, pltpu.HBM) for o in (x, flags, scale, shift, wl.T, bl, wr.T, br, bias)
    ]
    wire = jax.ShapeDtypeStruct((size, LANES), BF16)
    left, right, weight, vectors = pl.pallas_call(
        functools.partial(own_kernel, chunks),
        out_shape=(
            wire, wire,
            jax.ShapeDtypeStruct((2 * LANES, depth), BF16),
            jax.ShapeDtypeStruct((8, 2 * LANES), F32),
        ),
        in_specs=[pl.BlockSpec(memory_space=pltpu.HBM)] * len(operands),
        scratch_shapes=[pltpu.VMEM(o.shape, o.dtype) for o in operands] + [
            pltpu.VMEM((2, seqs * rows, LANES), F32),
            pltpu.SemaphoreType.DMA((len(operands) - 1 + chunks,)),
        ],
        compiler_params=pltpu.CompilerParams(vmem_limit_bytes=16 << 20),
        cost_estimate=pl.CostEstimate(flops=1 << 25, bytes_accessed=x.size * 8, transcendentals=0),
        name="project_own",
    )(*operands)
    wire = jax.ShapeDtypeStruct((CORES, size, LANES), BF16)
    left, right = pl.pallas_call(
        functools.partial(both_kernel, width),
        out_shape=(wire, wire),
        scratch_shapes=[pltpu.VMEM((2, seqs * rows, LANES), F32)],
        compiler_params=pltpu.CompilerParams(vmem_limit_bytes=16 << 20),
        name="project_other",
    )(other_x, other_flags, weight, vectors, left, right)

    steps = routes(n)
    lefts = [left] + [
        lax.ppermute(left, "seq", [(p, p ^ k * CORES) for p in range(n)]) for k in range(1, n // CORES)
    ]
    rights = [
        lax.ppermute(right, axes, [(a * n + p, step[a][p] * n + a) for a in range(n) for p in range(n)])
        for step in steps
    ]
    turned, live = pl.pallas_call(
        functools.partial(left_kernel, seqs, rows, width),
        out_shape=(jax.ShapeDtypeStruct((lanes, n * seqs), BF16), jax.ShapeDtypeStruct((rows, n * seqs), BF16)),
        scratch_shapes=[
            pltpu.VMEM((n * seqs, lanes), BF16),
            pltpu.VMEM((n * seqs // LANES, lanes, LANES), F32),
        ],
        compiler_params=pltpu.CompilerParams(vmem_limit_bytes=16 << 20),
        name="turn_left",
    )(*lefts)
    return pl.pallas_call(
        functools.partial(pair_kernel, steps, seqs, rows, rows, width),
        out_shape=jax.ShapeDtypeStruct((rows, rows, outs), BF16),
        scratch_shapes=[
            pltpu.VMEM((n * seqs, lanes), BF16),
            pltpu.VMEM((rows * rows, width * width), BF16),
            pltpu.VMEM((rows * rows, outs), F32),
        ],
        compiler_params=pltpu.CompilerParams(vmem_limit_bytes=16 << 20),
        name="pair",
    )(*rights, turned, live, w, vectors)


def solution(mesh):
    n = mesh.shape["res"]
    assert n == mesh.shape["seq"] and n & (n - 1) == 0 and n % CORES == 0
    in_specs = (P(("group", "seq"), "res", None), P(("group", "seq"), "res")) + (P(),) * 8
    return jax.shard_map(
        functools.partial(local, n), mesh=mesh, in_specs=in_specs,
        out_specs=P(("group", "res"), "seq", None), check_vma=False,
    )
```

```python
import functools

import jax
import jax.numpy as jnp
from jax import lax
from jax.experimental import pallas as pl
from jax.experimental.pallas import tpu as pltpu
from jax.sharding import PartitionSpec as P

LANES = 128
CORES = 2
F32 = jnp.float32
BF16 = jnp.bfloat16
TN = (((0,), (0,)), ((), ()))
NT = (((1,), (1,)), ((), ()))
NN = (((1,), (0,)), ((), ()))


def dot(a, b, dims=NN):
    return lax.dot_general(a, b, dims, preferred_element_type=F32)


def iota(shape, dim):
    return lax.broadcasted_iota(jnp.int32, shape, dim)


ROUTES = (
    ((2, 0, 3, 1), (1, 0, 2, 3), (1, 3, 0, 2), (1, 3, 0, 2)),
    ((3, 1, 2, 0), (2, 3, 1, 0), (2, 0, 3, 1), (2, 0, 3, 1)),
)


def routes(n):
    if n == 4:
        return ROUTES
    steps = [m for m in range(n) if bin(m).count("1") % 2 == 1]
    return tuple(tuple(tuple(p ^ m for p in range(n)) for a in range(n)) for m in steps)


def sending_chip(step, r, q):
    n = len(step)
    chip = 0
    for bit in range((n // CORES - 1).bit_length()):
        for a in range(n):
            word = sum((step[a].index(to) // CORES >> bit & 1) << to for to in range(n))
            chip = chip | jnp.where(q == a, (jnp.int32(word) >> r & 1) << bit, 0)
    return chip


def project_constants(seqs, rows, width, block, tiles):
    lanes = rows * width
    spreader = (iota((rows, lanes), 1) // width == iota((rows, lanes), 0)).astype(BF16)
    place = iota((seqs, LANES), 1) // width
    mine = [iota((rows, LANES), 1) // seqs + tile * (LANES // seqs) == block for tile in range(tiles)]
    return spreader, place, mine


def project_block(width, x_ref, flag_ref, weight, vectors, constants, left_ref, right_ref, proj_ref):
    seqs, rows, depth = x_ref.shape
    fold = LANES // width
    lanes = rows * width
    data = lanes // LANES * seqs
    spreader, place, mine = constants
    x = x_ref[...].astype(F32).reshape(seqs * rows, depth)
    center = jnp.mean(x, axis=-1, keepdims=True)
    x = x - center
    spread = jnp.mean(x * x, axis=-1, keepdims=True)
    normed = x * lax.rsqrt(spread + 1e-05) * vectors[0:1] + vectors[1:2]
    both = dot(normed.astype(BF16), weight, NT) + vectors[2:3]
    proj_ref[0] = both[:, :LANES]
    proj_ref[1] = both[:, LANES:]

    flags = flag_ref[...].astype(F32)
    mask = dot(flags.astype(BF16), spreader, TN)
    flags = jnp.concatenate([flags] * (LANES // seqs), axis=1)

    for half, out_ref in ((0, left_ref), (1, right_ref)):
        for tile in range(rows // fold):
            merged = proj_ref[half, pl.ds(tile * fold, seqs, stride=rows), :]
            for k in range(1, fold):
                part = proj_ref[half, pl.ds(tile * fold + k, seqs, stride=rows), :]
                merged = jnp.where(place == k, part, merged)
            merged = merged * mask[:, tile * LANES:(tile + 1) * LANES]
            out_ref[tile * seqs:(tile + 1) * seqs, :] = merged.astype(BF16)
        for tile, here in enumerate(mine):
            out_ref[data + tile * rows:data + (tile + 1) * rows, :] = jnp.where(here, flags, 0.0).astype(BF16)


def load_kernel(x_hbm, flag_hbm, scale_hbm, shift_hbm, wl_hbm, bl_hbm, wr_hbm, br_hbm, last_hbm,
                x_ref, flag_ref, weight_ref, vector_ref,
                scale_ref, shift_ref, wl_ref, bl_ref, wr_ref, br_ref, last_ref, sems):
    copies = [
        pltpu.make_async_copy(src, dst, sems.at[k])
        for k, (src, dst) in enumerate((
            (x_hbm, x_ref), (flag_hbm, flag_ref), (scale_hbm, scale_ref), (shift_hbm, shift_ref),
            (wl_hbm, wl_ref), (bl_hbm, bl_ref), (wr_hbm, wr_ref), (br_hbm, br_ref), (last_hbm, last_ref),
        ))
    ]
    for copy in copies:
        copy.start()
    for copy in copies[1:]:
        copy.wait()
    width, depth = wl_ref.shape
    fold = LANES // width
    weight_ref[...] = jnp.concatenate([wl_ref[...]] * fold + [wr_ref[...]] * fold, axis=0)
    bias = [bl_ref[...].reshape(1, width)] * fold + [br_ref[...].reshape(1, width)] * fold
    vector_ref[...] = jnp.concatenate(
        [
            scale_ref[...].reshape(1, depth),
            shift_ref[...].reshape(1, depth),
            jnp.concatenate(bias, axis=1),
            jnp.concatenate([last_ref[...].reshape(1, LANES)] * (depth // LANES), axis=1),
            jnp.zeros((4, depth), F32),
        ],
        axis=0,
    )
    copies[0].wait()


def project_kernel(width, own_x_ref, own_flag_ref, other_x_ref, other_flag_ref, weight_ref, vector_ref,
                   left_ref, right_ref, own_proj_ref, other_proj_ref):
    seqs, rows, _ = own_x_ref.shape
    block = lax.axis_index("seq")
    core = block % CORES
    other = 1 - core
    tiles = (left_ref.shape[1] - rows * width // LANES * seqs) // rows
    for x_ref, flag_ref, proj_ref, at in (
        (own_x_ref, own_flag_ref, own_proj_ref, core),
        (other_x_ref, other_flag_ref, other_proj_ref, other),
    ):
        project_block(
            width, x_ref, flag_ref, weight_ref[...], vector_ref[...],
            project_constants(seqs, rows, width, block - core + at, tiles),
            left_ref.at[at], right_ref.at[at], proj_ref,
        )


def whole_mask(pieces, rows, data):
    total = functools.reduce(jnp.add, [p[k, data:, :] for p in pieces for k in range(CORES)])
    return jnp.concatenate([total[k:k + rows] for k in range(0, total.shape[0], rows)], axis=1)


def left_kernel(steps, seqs, rows, width, *refs):
    lefts, (out_ref, mask_ref, left_ref, turned_ref) = refs[:-4], refs[-4:]
    data = rows * width // LANES * seqs
    me_res, me_seq = lax.axis_index("res"), lax.axis_index("seq")
    order = [sending_chip(step, me_res, me_seq) for step in steps]
    for k, piece in enumerate(lefts):
        chip = me_seq // CORES ^ k
        slot = sum(jnp.where(there == chip, place, 0) for place, there in enumerate(order))
        for core in range(CORES):
            at = pl.multiple_of((slot * CORES + core) * seqs, seqs)
            for tile in range(data // seqs):
                left_ref[pl.ds(at, seqs), tile * LANES:(tile + 1) * LANES] = (
                    piece[core, tile * seqs:(tile + 1) * seqs, :]
                )
    mask_ref[...] = whole_mask(lefts, rows, data)
    for tile in range(turned_ref.shape[0]):
        turned_ref[tile] = left_ref[tile * LANES:(tile + 1) * LANES, :].astype(F32).T
        for c in range(width):
            out_ref[c * rows:(c + 1) * rows, tile * LANES:(tile + 1) * LANES] = (
                turned_ref[tile, pl.ds(c, rows, stride=width), :].astype(BF16)
            )


def pair_kernel(seqs, rows, columns, width, *refs):
    rights = refs[:-7]
    turned_ref, live_ref, w_ref, vector_ref, out_ref, flat_ref, raw_ref = refs[-7:]
    fold = LANES // width
    assert fold == 4
    data = rows * width // LANES * seqs

    right = jnp.concatenate(
        [
            jnp.concatenate([p[core, t * seqs:(t + 1) * seqs, :] for t in range(data // seqs)], axis=1)
            for p in rights
            for core in range(CORES)
        ],
        axis=0,
    )
    outer = dot(turned_ref[...], right).astype(BF16)

    place = (iota((rows, LANES), 1) // width).astype(BF16)
    even = [None] * fold
    even[1] = (place == 0.0) | (place == 2.0)
    even[2] = (place == 0.0) | (place == 1.0)
    for tile in range(columns // fold):
        for quad in range(width // fold):
            part = [
                outer[(quad * fold + k) * rows:(quad * fold + k + 1) * rows, tile * LANES:(tile + 1) * LANES]
                for k in range(fold)
            ]
            for step in (2, 1):
                new = list(part)
                for k in range(fold):
                    if k & step == 0:
                        x, y = part[k], part[k + step]
                        new[k] = jnp.where(even[step], x, pltpu.roll(y, step * width, 1))
                        new[k + step] = jnp.where(even[step], pltpu.roll(x, LANES - step * width, 1), y)
                part = new
            for k in range(fold):
                j = tile * fold + k
                flat_ref[j * rows:(j + 1) * rows, quad * LANES:(quad + 1) * LANES] = part[k]

    raw = dot(flat_ref[...], w_ref[...]) + vector_ref[3:4, :LANES]
    count = dot(live_ref[...], whole_mask(rights, rows, data), NT)
    scale = 1.0 / (1.0 + count)
    for j in range(columns):
        raw_ref[j * rows:(j + 1) * rows, :] = raw[j * rows:(j + 1) * rows, :] * scale[:, j:j + 1]
    for i in range(rows):
        out_ref[i] = raw_ref[pl.ds(i, columns, stride=rows), :].astype(BF16)


def local(n, x, flags, scale, shift, wl, bl, wr, br, w, bias):
    seqs, rows, depth = x.shape
    width = wl.shape[1]
    outs = w.shape[1]
    lanes = rows * width
    size = lanes // LANES * seqs + rows * pl.cdiv(n * seqs, LANES)
    axes = ("res", "seq")
    flags = flags.T

    swap = [(p, p ^ 1) for p in range(n)]
    other_x, other_flags = lax.ppermute(x, "seq", swap), lax.ppermute(flags, "seq", swap)

    operands = [
        pltpu.with_memory_space_constraint(o, pltpu.HBM) for o in (x, flags, scale, shift, wl.T, bl, wr.T, br, bias)
    ]
    own_x, own_flags, weight, vectors = pl.pallas_call(
        load_kernel,
        out_shape=(
            jax.ShapeDtypeStruct(x.shape, x.dtype),
            jax.ShapeDtypeStruct(flags.shape, flags.dtype),
            jax.ShapeDtypeStruct((2 * LANES, depth), BF16),
            jax.ShapeDtypeStruct((8, 2 * LANES), F32),
        ),
        in_specs=[pl.BlockSpec(memory_space=pltpu.HBM)] * len(operands),
        scratch_shapes=[pltpu.VMEM(o.shape, o.dtype) for o in operands[2:]]
        + [pltpu.SemaphoreType.DMA((len(operands),))],
        compiler_params=pltpu.CompilerParams(vmem_limit_bytes=16 << 20),
        cost_estimate=pl.CostEstimate(flops=1 << 25, bytes_accessed=x.size * 8, transcendentals=0),
        name="load",
    )(*operands)
    wire = jax.ShapeDtypeStruct((CORES, size, LANES), BF16)
    left, right = pl.pallas_call(
        functools.partial(project_kernel, width),
        out_shape=(wire, wire),
        scratch_shapes=[pltpu.VMEM((2, seqs * rows, LANES), F32)] * 2,
        compiler_params=pltpu.CompilerParams(vmem_limit_bytes=16 << 20),
        name="project",
    )(own_x, own_flags, other_x, other_flags, weight, vectors)

    steps = routes(n)
    lefts = [left] + [
        lax.ppermute(left, "seq", [(p, p ^ k * CORES) for p in range(n)]) for k in range(1, n // CORES)
    ]
    rights = [
        lax.ppermute(right, axes, [(a * n + p, step[a][p] * n + a) for a in range(n) for p in range(n)])
        for step in steps
    ]
    turned, live = pl.pallas_call(
        functools.partial(left_kernel, steps, seqs, rows, width),
        out_shape=(jax.ShapeDtypeStruct((lanes, n * seqs), BF16), jax.ShapeDtypeStruct((rows, n * seqs), BF16)),
        scratch_shapes=[
            pltpu.VMEM((n * seqs, lanes), BF16),
            pltpu.VMEM((n * seqs // LANES, lanes, LANES), F32),
        ],
        compiler_params=pltpu.CompilerParams(vmem_limit_bytes=16 << 20),
        name="turn_left",
    )(*lefts)
    return pl.pallas_call(
        functools.partial(pair_kernel, seqs, rows, rows, width),
        out_shape=jax.ShapeDtypeStruct((rows, rows, outs), BF16),
        scratch_shapes=[
            pltpu.VMEM((rows * rows, width * width), BF16),
            pltpu.VMEM((rows * rows, outs), F32),
        ],
        compiler_params=pltpu.CompilerParams(vmem_limit_bytes=16 << 20),
        name="pair",
    )(*rights, turned, live, w, vectors)


def solution(mesh):
    n = mesh.shape["res"]
    assert n == mesh.shape["seq"] and n & (n - 1) == 0 and n % CORES == 0
    in_specs = (P(("group", "seq"), "res", None), P(("group", "seq"), "res")) + (P(),) * 8
    return jax.shard_map(
        functools.partial(local, n), mesh=mesh, in_specs=in_specs,
        out_specs=P(("group", "res"), "seq", None), check_vma=False,
    )
```

```python
import functools

import jax
import jax.numpy as jnp
from jax import lax
from jax.experimental import pallas as pl
from jax.experimental.pallas import tpu as pltpu
from jax.sharding import PartitionSpec as P

LANES = 128
CORES = 2
F32 = jnp.float32
BF16 = jnp.bfloat16
TN = (((0,), (0,)), ((), ()))
NT = (((1,), (1,)), ((), ()))
NN = (((1,), (0,)), ((), ()))


def dot(a, b, dims=NN):
    return lax.dot_general(a, b, dims, preferred_element_type=F32)


def iota(shape, dim):
    return lax.broadcasted_iota(jnp.int32, shape, dim)


ROUTES = (
    ((2, 0, 3, 1), (1, 0, 2, 3), (1, 3, 0, 2), (1, 3, 0, 2)),
    ((3, 1, 2, 0), (2, 3, 1, 0), (2, 0, 3, 1), (2, 0, 3, 1)),
)


def routes(n):
    if n == 4:
        return ROUTES
    steps = [m for m in range(n) if bin(m).count("1") % 2 == 1]
    return tuple(tuple(tuple(p ^ m for p in range(n)) for a in range(n)) for m in steps)


def sending_chip(step, r, q):
    n = len(step)
    chip = 0
    for bit in range((n // CORES - 1).bit_length()):
        for a in range(n):
            word = sum((step[a].index(to) // CORES >> bit & 1) << to for to in range(n))
            chip = chip | jnp.where(q == a, (jnp.int32(word) >> r & 1) << bit, 0)
    return chip


def project_constants(seqs, rows, width, block, tiles):
    lanes = rows * width
    spreader = (iota((rows, lanes), 1) // width == iota((rows, lanes), 0)).astype(BF16)
    place = iota((seqs, LANES), 1) // width
    mine = [iota((rows, LANES), 1) // seqs + tile * (LANES // seqs) == block for tile in range(tiles)]
    return spreader, place, mine


def project_block(width, x_ref, flag_ref, weight, vectors, constants, left_ref, right_ref, proj_ref):
    seqs, rows, depth = x_ref.shape
    fold = LANES // width
    assert fold == 4
    data = rows * width // LANES * seqs
    spreader, place, mine = constants
    x = x_ref[...].astype(F32).reshape(seqs * rows, depth)
    center = jnp.mean(x, axis=-1, keepdims=True)
    x = x - center
    spread = jnp.mean(x * x, axis=-1, keepdims=True)
    normed = x * lax.rsqrt(spread + 1e-05) * vectors[0:1] + vectors[1:2]
    proj_ref[...] = dot(normed.astype(BF16), weight, NT) + vectors[2:3, :LANES]

    flags = flag_ref[...].astype(F32)
    mask = dot(flags.astype(BF16), spreader, TN)
    flags = jnp.concatenate([flags] * (LANES // seqs), axis=1)
    for tile in range(rows // fold):
        own = [proj_ref[pl.ds(tile * fold + k, seqs, stride=rows), :] for k in range(fold)]
        moved = [pltpu.roll(p, width, 1) for p in own]
        for out_ref, (g0, g1, g2, g3) in (
            (left_ref, (own[0], moved[1], own[2], moved[3])),
            (right_ref, (moved[0], own[1], moved[2], own[3])),
        ):
            merged = jnp.where(place < 2, jnp.where(place == 0, g0, g1), jnp.where(place == 2, g2, g3))
            merged = merged * mask[:, tile * LANES:(tile + 1) * LANES]
            out_ref[tile * seqs:(tile + 1) * seqs, :] = merged.astype(BF16)
    for tile, here in enumerate(mine):
        placed = jnp.where(here, flags, 0.0).astype(BF16)
        for out_ref in (left_ref, right_ref):
            out_ref[data + tile * rows:data + (tile + 1) * rows, :] = placed


def load_kernel(x_hbm, flag_hbm, scale_hbm, shift_hbm, wl_hbm, bl_hbm, wr_hbm, br_hbm, last_hbm,
                x_ref, flag_ref, weight_ref, vector_ref,
                scale_ref, shift_ref, wl_ref, bl_ref, wr_ref, br_ref, last_ref, sems):
    copies = [
        pltpu.make_async_copy(src, dst, sems.at[k])
        for k, (src, dst) in enumerate((
            (x_hbm, x_ref), (flag_hbm, flag_ref), (scale_hbm, scale_ref), (shift_hbm, shift_ref),
            (wl_hbm, wl_ref), (bl_hbm, bl_ref), (wr_hbm, wr_ref), (br_hbm, br_ref), (last_hbm, last_ref),
        ))
    ]
    for copy in copies:
        copy.start()
    for copy in copies[1:]:
        copy.wait()
    width, depth = wl_ref.shape
    fold = LANES // width
    weight_ref[...] = jnp.concatenate([wl_ref[...], wr_ref[...]] * (fold // 2), axis=0)
    bias = [bl_ref[...].reshape(1, width), br_ref[...].reshape(1, width)] * (depth // width // 2)
    vector_ref[...] = jnp.concatenate(
        [
            scale_ref[...].reshape(1, depth),
            shift_ref[...].reshape(1, depth),
            jnp.concatenate(bias, axis=1),
            jnp.concatenate([last_ref[...].reshape(1, LANES)] * (depth // LANES), axis=1),
            jnp.zeros((4, depth), F32),
        ],
        axis=0,
    )
    copies[0].wait()


def project_kernel(width, own_x_ref, own_flag_ref, other_x_ref, other_flag_ref, weight_ref, vector_ref,
                   left_ref, right_ref, own_proj_ref, other_proj_ref):
    seqs, rows, _ = own_x_ref.shape
    block = lax.axis_index("seq")
    core = block % CORES
    other = 1 - core
    tiles = (left_ref.shape[1] - rows * width // LANES * seqs) // rows
    for x_ref, flag_ref, proj_ref, at in (
        (own_x_ref, own_flag_ref, own_proj_ref, core),
        (other_x_ref, other_flag_ref, other_proj_ref, other),
    ):
        project_block(
            width, x_ref, flag_ref, weight_ref[...], vector_ref[...],
            project_constants(seqs, rows, width, block - core + at, tiles),
            left_ref.at[at], right_ref.at[at], proj_ref,
        )


def whole_mask(pieces, rows, data):
    total = functools.reduce(jnp.add, [p[k, data:, :] for p in pieces for k in range(CORES)])
    return jnp.concatenate([total[k:k + rows] for k in range(0, total.shape[0], rows)], axis=1)


def left_kernel(steps, seqs, rows, width, *refs):
    lefts, (out_ref, mask_ref, left_ref, turned_ref) = refs[:-4], refs[-4:]
    data = rows * width // LANES * seqs
    me_res, me_seq = lax.axis_index("res"), lax.axis_index("seq")
    order = [sending_chip(step, me_res, me_seq) for step in steps]
    for k, piece in enumerate(lefts):
        chip = me_seq // CORES ^ k
        slot = sum(jnp.where(there == chip, place, 0) for place, there in enumerate(order))
        for core in range(CORES):
            at = pl.multiple_of((slot * CORES + core) * seqs, seqs)
            for tile in range(data // seqs):
                left_ref[pl.ds(at, seqs), tile * LANES:(tile + 1) * LANES] = (
                    piece[core, tile * seqs:(tile + 1) * seqs, :]
                )
    mask_ref[...] = whole_mask(lefts, rows, data)
    for tile in range(turned_ref.shape[0]):
        turned_ref[tile] = left_ref[tile * LANES:(tile + 1) * LANES, :].astype(F32).T
        for c in range(width):
            out_ref[c * rows:(c + 1) * rows, tile * LANES:(tile + 1) * LANES] = (
                turned_ref[tile, pl.ds(c, rows, stride=width), :].astype(BF16)
            )


def pair_kernel(seqs, rows, columns, width, *refs):
    rights = refs[:-7]
    turned_ref, live_ref, w_ref, vector_ref, out_ref, flat_ref, raw_ref = refs[-7:]
    fold = LANES // width
    assert fold == 4
    data = rows * width // LANES * seqs

    right = jnp.concatenate(
        [
            jnp.concatenate([p[core, t * seqs:(t + 1) * seqs, :] for t in range(data // seqs)], axis=1)
            for p in rights
            for core in range(CORES)
        ],
        axis=0,
    )
    outer = dot(turned_ref[...], right).astype(BF16)

    place = (iota((rows, LANES), 1) // width).astype(BF16)
    even = [None] * fold
    even[1] = (place == 0.0) | (place == 2.0)
    even[2] = (place == 0.0) | (place == 1.0)
    for tile in range(columns // fold):
        for quad in range(width // fold):
            part = [
                outer[(quad * fold + k) * rows:(quad * fold + k + 1) * rows, tile * LANES:(tile + 1) * LANES]
                for k in range(fold)
            ]
            for step in (2, 1):
                new = list(part)
                for k in range(fold):
                    if k & step == 0:
                        x, y = part[k], part[k + step]
                        new[k] = jnp.where(even[step], x, pltpu.roll(y, step * width, 1))
                        new[k + step] = jnp.where(even[step], pltpu.roll(x, LANES - step * width, 1), y)
                part = new
            for k in range(fold):
                j = tile * fold + k
                flat_ref[j * rows:(j + 1) * rows, quad * LANES:(quad + 1) * LANES] = part[k]

    raw = dot(flat_ref[...], w_ref[...]) + vector_ref[3:4, :LANES]
    count = dot(live_ref[...], whole_mask(rights, rows, data), NT)
    scale = 1.0 / (1.0 + count)
    for j in range(columns):
        raw_ref[j * rows:(j + 1) * rows, :] = raw[j * rows:(j + 1) * rows, :] * scale[:, j:j + 1]
    for i in range(rows):
        out_ref[i] = raw_ref[pl.ds(i, columns, stride=rows), :].astype(BF16)


def local(n, x, flags, scale, shift, wl, bl, wr, br, w, bias):
    seqs, rows, depth = x.shape
    width = wl.shape[1]
    outs = w.shape[1]
    lanes = rows * width
    size = lanes // LANES * seqs + rows * pl.cdiv(n * seqs, LANES)
    axes = ("res", "seq")
    flags = flags.T

    swap = [(p, p ^ 1) for p in range(n)]
    other_x, other_flags = lax.ppermute(x, "seq", swap), lax.ppermute(flags, "seq", swap)

    operands = [
        pltpu.with_memory_space_constraint(o, pltpu.HBM) for o in (x, flags, scale, shift, wl.T, bl, wr.T, br, bias)
    ]
    own_x, own_flags, weight, vectors = pl.pallas_call(
        load_kernel,
        out_shape=(
            jax.ShapeDtypeStruct(x.shape, x.dtype),
            jax.ShapeDtypeStruct(flags.shape, flags.dtype),
            jax.ShapeDtypeStruct((LANES, depth), BF16),
            jax.ShapeDtypeStruct((8, depth), F32),
        ),
        in_specs=[pl.BlockSpec(memory_space=pltpu.HBM)] * len(operands),
        scratch_shapes=[pltpu.VMEM(o.shape, o.dtype) for o in operands[2:]]
        + [pltpu.SemaphoreType.DMA((len(operands),))],
        compiler_params=pltpu.CompilerParams(vmem_limit_bytes=16 << 20),
        cost_estimate=pl.CostEstimate(flops=1 << 25, bytes_accessed=x.size * 8, transcendentals=0),
        name="load",
    )(*operands)
    wire = jax.ShapeDtypeStruct((CORES, size, LANES), BF16)
    left, right = pl.pallas_call(
        functools.partial(project_kernel, width),
        out_shape=(wire, wire),
        scratch_shapes=[pltpu.VMEM((seqs * rows, LANES), F32)] * 2,
        compiler_params=pltpu.CompilerParams(vmem_limit_bytes=16 << 20),
        name="project",
    )(own_x, own_flags, other_x, other_flags, weight, vectors)

    steps = routes(n)
    lefts = [left] + [
        lax.ppermute(left, "seq", [(p, p ^ k * CORES) for p in range(n)]) for k in range(1, n // CORES)
    ]
    rights = [
        lax.ppermute(right, axes, [(a * n + p, step[a][p] * n + a) for a in range(n) for p in range(n)])
        for step in steps
    ]
    turned, live = pl.pallas_call(
        functools.partial(left_kernel, steps, seqs, rows, width),
        out_shape=(jax.ShapeDtypeStruct((lanes, n * seqs), BF16), jax.ShapeDtypeStruct((rows, n * seqs), BF16)),
        scratch_shapes=[
            pltpu.VMEM((n * seqs, lanes), BF16),
            pltpu.VMEM((n * seqs // LANES, lanes, LANES), F32),
        ],
        compiler_params=pltpu.CompilerParams(vmem_limit_bytes=16 << 20),
        name="turn_left",
    )(*lefts)
    return pl.pallas_call(
        functools.partial(pair_kernel, seqs, rows, rows, width),
        out_shape=jax.ShapeDtypeStruct((rows, rows, outs), BF16),
        scratch_shapes=[
            pltpu.VMEM((rows * rows, width * width), BF16),
            pltpu.VMEM((rows * rows, outs), F32),
        ],
        compiler_params=pltpu.CompilerParams(vmem_limit_bytes=16 << 20),
        name="pair",
    )(*rights, turned, live, w, vectors)


def solution(mesh):
    n = mesh.shape["res"]
    assert n == mesh.shape["seq"] and n & (n - 1) == 0 and n % CORES == 0
    in_specs = (P(("group", "seq"), "res", None), P(("group", "seq"), "res")) + (P(),) * 8
    return jax.shard_map(
        functools.partial(local, n), mesh=mesh, in_specs=in_specs,
        out_specs=P(("group", "res"), "seq", None), check_vma=False,
    )
```

```python
import functools

import jax
import jax.numpy as jnp
from jax import lax
from jax.experimental import pallas as pl
from jax.experimental.pallas import tpu as pltpu
from jax.sharding import PartitionSpec as P

LANES = 128
CORES = 2
F32 = jnp.float32
BF16 = jnp.bfloat16
TN = (((0,), (0,)), ((), ()))
NT = (((1,), (1,)), ((), ()))
NN = (((1,), (0,)), ((), ()))


def dot(a, b, dims=NN):
    return lax.dot_general(a, b, dims, preferred_element_type=F32)


def iota(shape, dim):
    return lax.broadcasted_iota(jnp.int32, shape, dim)


ROUTES = (
    ((2, 0, 3, 1), (1, 0, 2, 3), (1, 3, 0, 2), (1, 3, 0, 2)),
    ((3, 1, 2, 0), (2, 3, 1, 0), (2, 0, 3, 1), (2, 0, 3, 1)),
)


def routes(n):
    if n == 4:
        return ROUTES
    steps = [m for m in range(n) if bin(m).count("1") % 2 == 1]
    return tuple(tuple(tuple(p ^ m for p in range(n)) for a in range(n)) for m in steps)


def sending_chip(step, r, q):
    n = len(step)
    chip = 0
    for bit in range((n // CORES - 1).bit_length()):
        for a in range(n):
            word = sum((step[a].index(to) // CORES >> bit & 1) << to for to in range(n))
            chip = chip | jnp.where(q == a, (jnp.int32(word) >> r & 1) << bit, 0)
    return chip


def project_constants(seqs, rows, width, block, tiles):
    lanes = rows * width
    spreader = (iota((rows, lanes), 1) // width == iota((rows, lanes), 0)).astype(BF16)
    place = iota((seqs, LANES), 1) // width
    mine = [iota((rows, LANES), 1) // seqs + tile * (LANES // seqs) == block for tile in range(tiles)]
    return spreader, place, mine


def project_block(width, x_ref, flag_ref, weight, vectors, constants, left_ref, right_ref, proj_ref):
    seqs, rows, depth = x_ref.shape
    fold = LANES // width
    lanes = rows * width
    data = lanes // LANES * seqs
    spreader, place, mine = constants
    x = x_ref[...].astype(F32).reshape(seqs * rows, depth)
    center = jnp.mean(x, axis=-1, keepdims=True)
    x = x - center
    spread = jnp.mean(x * x, axis=-1, keepdims=True)
    normed = x * lax.rsqrt(spread + 1e-05) * vectors[0:1] + vectors[1:2]
    both = dot(normed.astype(BF16), weight, NT) + vectors[2:3]
    proj_ref[0] = both[:, :LANES]
    proj_ref[1] = both[:, LANES:]

    flags = flag_ref[...].astype(F32)
    mask = dot(flags.astype(BF16), spreader, TN)
    flags = jnp.concatenate([flags] * (LANES // seqs), axis=1)

    for half, out_ref in ((0, left_ref), (1, right_ref)):
        for tile in range(rows // fold):
            merged = proj_ref[half, pl.ds(tile * fold, seqs, stride=rows), :]
            for k in range(1, fold):
                part = proj_ref[half, pl.ds(tile * fold + k, seqs, stride=rows), :]
                merged = jnp.where(place == k, part, merged)
            merged = merged * mask[:, tile * LANES:(tile + 1) * LANES]
            out_ref[tile * seqs:(tile + 1) * seqs, :] = merged.astype(BF16)
        for tile, here in enumerate(mine):
            out_ref[data + tile * rows:data + (tile + 1) * rows, :] = jnp.where(here, flags, 0.0).astype(BF16)


def load_kernel(x_hbm, flag_hbm, scale_hbm, shift_hbm, wl_hbm, bl_hbm, wr_hbm, br_hbm, last_hbm,
                x_ref, flag_ref, weight_ref, vector_ref,
                scale_ref, shift_ref, wl_ref, bl_ref, wr_ref, br_ref, last_ref, sems):
    copies = [
        pltpu.make_async_copy(src, dst, sems.at[k])
        for k, (src, dst) in enumerate((
            (x_hbm, x_ref), (flag_hbm, flag_ref), (scale_hbm, scale_ref), (shift_hbm, shift_ref),
            (wl_hbm, wl_ref), (bl_hbm, bl_ref), (wr_hbm, wr_ref), (br_hbm, br_ref), (last_hbm, last_ref),
        ))
    ]
    for copy in copies:
        copy.start()
    for copy in copies[1:]:
        copy.wait()
    width, depth = wl_ref.shape
    fold = LANES // width
    weight_ref[...] = jnp.concatenate([wl_ref[...]] * fold + [wr_ref[...]] * fold, axis=0)
    bias = [bl_ref[...].reshape(1, width)] * fold + [br_ref[...].reshape(1, width)] * fold
    vector_ref[...] = jnp.concatenate(
        [
            scale_ref[...].reshape(1, depth),
            shift_ref[...].reshape(1, depth),
            jnp.concatenate(bias, axis=1),
            jnp.concatenate([last_ref[...].reshape(1, LANES)] * (depth // LANES), axis=1),
            jnp.zeros((4, depth), F32),
        ],
        axis=0,
    )
    copies[0].wait()


def project_kernel(width, own_x_ref, own_flag_ref, other_x_ref, other_flag_ref, weight_ref, vector_ref,
                   left_ref, right_ref, own_proj_ref, other_proj_ref):
    seqs, rows, _ = own_x_ref.shape
    block = lax.axis_index("seq")
    core = block % CORES
    other = 1 - core
    tiles = (left_ref.shape[1] - rows * width // LANES * seqs) // rows
    for x_ref, flag_ref, proj_ref, at in (
        (own_x_ref, own_flag_ref, own_proj_ref, core),
        (other_x_ref, other_flag_ref, other_proj_ref, other),
    ):
        project_block(
            width, x_ref, flag_ref, weight_ref[...], vector_ref[...],
            project_constants(seqs, rows, width, block - core + at, tiles),
            left_ref.at[at], right_ref.at[at], proj_ref,
        )


def whole_mask(pieces, rows, data):
    total = functools.reduce(jnp.add, [p[k, data:, :] for p in pieces for k in range(CORES)])
    return jnp.concatenate([total[k:k + rows] for k in range(0, total.shape[0], rows)], axis=1)


def left_kernel(steps, seqs, rows, width, *refs):
    lefts, (out_ref, mask_ref, left_ref, turned_ref) = refs[:-4], refs[-4:]
    data = rows * width // LANES * seqs
    me_res, me_seq = lax.axis_index("res"), lax.axis_index("seq")
    order = [sending_chip(step, me_res, me_seq) for step in steps]
    for k, piece in enumerate(lefts):
        chip = me_seq // CORES ^ k
        slot = sum(jnp.where(there == chip, place, 0) for place, there in enumerate(order))
        for core in range(CORES):
            at = pl.multiple_of((slot * CORES + core) * seqs, seqs)
            for tile in range(data // seqs):
                left_ref[pl.ds(at, seqs), tile * LANES:(tile + 1) * LANES] = (
                    piece[core, tile * seqs:(tile + 1) * seqs, :]
                )
    mask_ref[...] = whole_mask(lefts, rows, data)
    for tile in range(turned_ref.shape[0]):
        turned_ref[tile] = left_ref[tile * LANES:(tile + 1) * LANES, :].astype(F32).T
        for c in range(width):
            out_ref[c * rows:(c + 1) * rows, tile * LANES:(tile + 1) * LANES] = (
                turned_ref[tile, pl.ds(c, rows, stride=width), :].astype(BF16)
            )


def pair_kernel(seqs, rows, columns, width, *refs):
    rights = refs[:-6]
    turned_ref, live_ref, w_ref, vector_ref, out_ref, raw_ref = refs[-6:]
    fold = LANES // width
    assert fold == 4
    data = rows * width // LANES * seqs

    right = jnp.concatenate(
        [
            jnp.concatenate([p[core, t * seqs:(t + 1) * seqs, :] for t in range(data // seqs)], axis=1)
            for p in rights
            for core in range(CORES)
        ],
        axis=0,
    )

    place = (iota((rows, LANES), 1) // width).astype(BF16)
    even = {1: (place == 0.0) | (place == 2.0), 2: (place == 0.0) | (place == 1.0)}
    quads = 2
    passes = width // (fold * quads)
    raw = vector_ref[3:4, :LANES]
    for step_of in range(passes):
        first = step_of * fold * quads * rows
        outer = dot(turned_ref[first:first + fold * quads * rows, :], right).astype(BF16)
        flat = [[] for _ in range(columns)]
        for quad in range(quads):
            for tile in range(columns // fold):
                part = [
                    outer[(quad * fold + k) * rows:(quad * fold + k + 1) * rows, tile * LANES:(tile + 1) * LANES]
                    for k in range(fold)
                ]
                for step in (2, 1):
                    new = list(part)
                    for k in range(fold):
                        if k & step == 0:
                            x, y = part[k], part[k + step]
                            new[k] = jnp.where(even[step], x, pltpu.roll(y, step * width, 1))
                            new[k + step] = jnp.where(even[step], pltpu.roll(x, LANES - step * width, 1), y)
                    part = new
                for k in range(fold):
                    flat[tile * fold + k].append(part[k])
        flat = jnp.concatenate([jnp.concatenate(j, axis=1) for j in flat], axis=0)
        first = step_of * fold * quads * width
        raw = raw + dot(flat, w_ref[first:first + fold * quads * width, :])

    count = dot(live_ref[...], whole_mask(rights, rows, data), NT)
    scale = 1.0 / (1.0 + count)
    for j in range(columns):
        raw_ref[j * rows:(j + 1) * rows, :] = raw[j * rows:(j + 1) * rows, :] * scale[:, j:j + 1]
    for i in range(rows):
        out_ref[i] = raw_ref[pl.ds(i, columns, stride=rows), :].astype(BF16)


def local(n, x, flags, scale, shift, wl, bl, wr, br, w, bias):
    seqs, rows, depth = x.shape
    width = wl.shape[1]
    outs = w.shape[1]
    lanes = rows * width
    size = lanes // LANES * seqs + rows * pl.cdiv(n * seqs, LANES)
    axes = ("res", "seq")
    flags = flags.T

    swap = [(p, p ^ 1) for p in range(n)]
    other_x, other_flags = lax.ppermute(x, "seq", swap), lax.ppermute(flags, "seq", swap)

    operands = [
        pltpu.with_memory_space_constraint(o, pltpu.HBM) for o in (x, flags, scale, shift, wl.T, bl, wr.T, br, bias)
    ]
    own_x, own_flags, weight, vectors = pl.pallas_call(
        load_kernel,
        out_shape=(
            jax.ShapeDtypeStruct(x.shape, x.dtype),
            jax.ShapeDtypeStruct(flags.shape, flags.dtype),
            jax.ShapeDtypeStruct((2 * LANES, depth), BF16),
            jax.ShapeDtypeStruct((8, 2 * LANES), F32),
        ),
        in_specs=[pl.BlockSpec(memory_space=pltpu.HBM)] * len(operands),
        scratch_shapes=[pltpu.VMEM(o.shape, o.dtype) for o in operands[2:]]
        + [pltpu.SemaphoreType.DMA((len(operands),))],
        compiler_params=pltpu.CompilerParams(vmem_limit_bytes=16 << 20),
        cost_estimate=pl.CostEstimate(flops=1 << 25, bytes_accessed=x.size * 8, transcendentals=0),
        name="load",
    )(*operands)
    wire = jax.ShapeDtypeStruct((CORES, size, LANES), BF16)
    left, right = pl.pallas_call(
        functools.partial(project_kernel, width),
        out_shape=(wire, wire),
        scratch_shapes=[pltpu.VMEM((2, seqs * rows, LANES), F32)] * 2,
        compiler_params=pltpu.CompilerParams(vmem_limit_bytes=16 << 20),
        name="project",
    )(own_x, own_flags, other_x, other_flags, weight, vectors)

    steps = routes(n)
    lefts = [left] + [
        lax.ppermute(left, "seq", [(p, p ^ k * CORES) for p in range(n)]) for k in range(1, n // CORES)
    ]
    rights = [
        lax.ppermute(right, axes, [(a * n + p, step[a][p] * n + a) for a in range(n) for p in range(n)])
        for step in steps
    ]
    turned, live = pl.pallas_call(
        functools.partial(left_kernel, steps, seqs, rows, width),
        out_shape=(jax.ShapeDtypeStruct((lanes, n * seqs), BF16), jax.ShapeDtypeStruct((rows, n * seqs), BF16)),
        scratch_shapes=[
            pltpu.VMEM((n * seqs, lanes), BF16),
            pltpu.VMEM((n * seqs // LANES, lanes, LANES), F32),
        ],
        compiler_params=pltpu.CompilerParams(vmem_limit_bytes=16 << 20),
        name="turn_left",
    )(*lefts)
    return pl.pallas_call(
        functools.partial(pair_kernel, seqs, rows, rows, width),
        out_shape=jax.ShapeDtypeStruct((rows, rows, outs), BF16),
        scratch_shapes=[
            pltpu.VMEM((rows * rows, outs), F32),
        ],
        compiler_params=pltpu.CompilerParams(vmem_limit_bytes=16 << 20),
        name="pair",
    )(*rights, turned, live, w, vectors)


def solution(mesh):
    n = mesh.shape["res"]
    assert n == mesh.shape["seq"] and n & (n - 1) == 0 and n % CORES == 0
    in_specs = (P(("group", "seq"), "res", None), P(("group", "seq"), "res")) + (P(),) * 8
    return jax.shard_map(
        functools.partial(local, n), mesh=mesh, in_specs=in_specs,
        out_specs=P(("group", "res"), "seq", None), check_vma=False,
    )
```

```python
import functools

import jax
import jax.numpy as jnp
from jax import lax
from jax.experimental import pallas as pl
from jax.experimental.pallas import tpu as pltpu
from jax.sharding import PartitionSpec as P

LANES = 128
CORES = 2
F32 = jnp.float32
BF16 = jnp.bfloat16
TN = (((0,), (0,)), ((), ()))
NT = (((1,), (1,)), ((), ()))
NN = (((1,), (0,)), ((), ()))


def dot(a, b, dims=NN):
    return lax.dot_general(a, b, dims, preferred_element_type=F32)


def iota(shape, dim):
    return lax.broadcasted_iota(jnp.int32, shape, dim)


RIGHT = (
    ((1, 0, 2, 3), (0, 2, 1, 3), (3, 1, 0, 2), (2, 1, 3, 0)),
    ((3, 2, 1, 0), (1, 3, 2, 0), (0, 2, 3, 1), (3, 0, 2, 1)),
)
LEFT = ((3, 2, 1, 0), (3, 2, 0, 1), (3, 2, 0, 1), (2, 3, 0, 1))


def right_routes(n):
    if n == 4:
        return RIGHT
    steps = [m for m in range(n) if bin(m).count("1") % 2 == 1]
    return tuple(tuple(tuple(p ^ m for p in range(n)) for a in range(n)) for m in steps)


def left_routes(n):
    if n == 4:
        return (LEFT,)
    return tuple(tuple(tuple(p ^ k * CORES for p in range(n)) for a in range(n)) for k in range(1, n // CORES))


def sending_chip(step, r, q):
    n = len(step)
    chip = 0
    for bit in range((n // CORES - 1).bit_length()):
        for a in range(n):
            word = sum((step[a].index(to) // CORES >> bit & 1) << to for to in range(n))
            chip = chip | jnp.where(q == a, (jnp.int32(word) >> r & 1) << bit, 0)
    return chip


def project_constants(seqs, rows, width, block, tiles):
    lanes = rows * width
    spreader = (iota((rows, lanes), 1) // width == iota((rows, lanes), 0)).astype(BF16)
    place = iota((seqs, LANES), 1) // width
    mine = [iota((rows, LANES), 1) // seqs + tile * (LANES // seqs) == block for tile in range(tiles)]
    return spreader, place, mine


def project_block(width, x_ref, flag_ref, weight, vectors, constants, left_ref, right_ref, proj_ref):
    seqs, rows, depth = x_ref.shape
    fold = LANES // width
    lanes = rows * width
    data = lanes // LANES * seqs
    spreader, place, mine = constants
    x = x_ref[...].reshape(seqs * rows, depth)
    center = dot(x, jnp.full((depth, LANES), 1.0 / depth, BF16))
    x = x.astype(F32) - jnp.concatenate([center] * (depth // LANES), axis=1)
    spread = jnp.mean(x * x, axis=-1, keepdims=True)
    normed = x * lax.rsqrt(spread + 1e-05) * vectors[0:1] + vectors[1:2]
    both = dot(normed.astype(BF16), weight, NT) + vectors[2:3]
    proj_ref[0] = both[:, :LANES]
    proj_ref[1] = both[:, LANES:]

    flags = flag_ref[...].astype(F32)
    mask = dot(flags.astype(BF16), spreader, TN)
    flags = jnp.concatenate([flags] * (LANES // seqs), axis=1)

    for half, out_ref in ((0, left_ref), (1, right_ref)):
        for tile in range(rows // fold):
            merged = proj_ref[half, pl.ds(tile * fold, seqs, stride=rows), :]
            for k in range(1, fold):
                part = proj_ref[half, pl.ds(tile * fold + k, seqs, stride=rows), :]
                merged = jnp.where(place == k, part, merged)
            merged = merged * mask[:, tile * LANES:(tile + 1) * LANES]
            out_ref[tile * seqs:(tile + 1) * seqs, :] = merged.astype(BF16)
        for tile, here in enumerate(mine):
            out_ref[data + tile * rows:data + (tile + 1) * rows, :] = jnp.where(here, flags, 0.0).astype(BF16)


def load_kernel(x_hbm, flag_hbm, scale_hbm, shift_hbm, wl_hbm, bl_hbm, wr_hbm, br_hbm, last_hbm,
                x_ref, flag_ref, weight_ref, vector_ref,
                scale_ref, shift_ref, wl_ref, bl_ref, wr_ref, br_ref, last_ref, sems):
    copies = [
        pltpu.make_async_copy(src, dst, sems.at[k])
        for k, (src, dst) in enumerate((
            (x_hbm, x_ref), (flag_hbm, flag_ref), (scale_hbm, scale_ref), (shift_hbm, shift_ref),
            (wl_hbm, wl_ref), (bl_hbm, bl_ref), (wr_hbm, wr_ref), (br_hbm, br_ref), (last_hbm, last_ref),
        ))
    ]
    for copy in copies:
        copy.start()
    for copy in copies[1:]:
        copy.wait()
    width, depth = wl_ref.shape
    fold = LANES // width
    weight_ref[...] = jnp.concatenate([wl_ref[...]] * fold + [wr_ref[...]] * fold, axis=0)
    bias = [bl_ref[...].reshape(1, width)] * fold + [br_ref[...].reshape(1, width)] * fold
    vector_ref[...] = jnp.concatenate(
        [
            scale_ref[...].reshape(1, depth),
            shift_ref[...].reshape(1, depth),
            jnp.concatenate(bias, axis=1),
            jnp.concatenate([last_ref[...].reshape(1, LANES)] * (depth // LANES), axis=1),
            jnp.zeros((4, depth), F32),
        ],
        axis=0,
    )
    copies[0].wait()


def project_kernel(width, own_x_ref, own_flag_ref, other_x_ref, other_flag_ref, weight_ref, vector_ref,
                   left_ref, right_ref, own_proj_ref, other_proj_ref):
    seqs, rows, _ = own_x_ref.shape
    block = lax.axis_index("seq")
    core = block % CORES
    other = 1 - core
    tiles = (left_ref.shape[1] - rows * width // LANES * seqs) // rows
    for x_ref, flag_ref, proj_ref, at in (
        (own_x_ref, own_flag_ref, own_proj_ref, core),
        (other_x_ref, other_flag_ref, other_proj_ref, other),
    ):
        project_block(
            width, x_ref, flag_ref, weight_ref[...], vector_ref[...],
            project_constants(seqs, rows, width, block - core + at, tiles),
            left_ref.at[at], right_ref.at[at], proj_ref,
        )


def whole_mask(pieces, rows, data):
    total = functools.reduce(jnp.add, [p[k, data:, :] for p in pieces for k in range(CORES)])
    return jnp.concatenate([total[k:k + rows] for k in range(0, total.shape[0], rows)], axis=1)


def left_kernel(steps, seqs, rows, width, *refs):
    lefts, (out_ref, mask_ref, left_ref, turned_ref) = refs[:-4], refs[-4:]
    data = rows * width // LANES * seqs
    me_res, me_seq = lax.axis_index("res"), lax.axis_index("seq")
    order = [sending_chip(step, me_res, me_seq) for step in steps]
    for k, piece in enumerate(lefts):
        chip = me_seq // CORES ^ k
        slot = sum(jnp.where(there == chip, place, 0) for place, there in enumerate(order))
        for core in range(CORES):
            at = pl.multiple_of((slot * CORES + core) * seqs, seqs)
            for tile in range(data // seqs):
                left_ref[pl.ds(at, seqs), tile * LANES:(tile + 1) * LANES] = (
                    piece[core, tile * seqs:(tile + 1) * seqs, :]
                )
    mask_ref[...] = whole_mask(lefts, rows, data)
    for tile in range(turned_ref.shape[0]):
        turned_ref[tile] = left_ref[tile * LANES:(tile + 1) * LANES, :].astype(F32).T
        for c in range(width):
            out_ref[c * rows:(c + 1) * rows, tile * LANES:(tile + 1) * LANES] = (
                turned_ref[tile, pl.ds(c, rows, stride=width), :].astype(BF16)
            )


def pair_kernel(seqs, rows, columns, width, *refs):
    rights = refs[:-7]
    turned_ref, live_ref, w_ref, vector_ref, out_ref, flat_ref, raw_ref = refs[-7:]
    fold = LANES // width
    assert fold == 4
    data = rows * width // LANES * seqs

    right = jnp.concatenate(
        [
            jnp.concatenate([p[core, t * seqs:(t + 1) * seqs, :] for t in range(data // seqs)], axis=1)
            for p in rights
            for core in range(CORES)
        ],
        axis=0,
    )
    outer = dot(turned_ref[...], right).astype(BF16)

    place = (iota((rows, LANES), 1) // width).astype(BF16)
    even = [None] * fold
    even[1] = (place == 0.0) | (place == 2.0)
    even[2] = (place == 0.0) | (place == 1.0)
    for tile in range(columns // fold):
        for quad in range(width // fold):
            part = [
                outer[(quad * fold + k) * rows:(quad * fold + k + 1) * rows, tile * LANES:(tile + 1) * LANES]
                for k in range(fold)
            ]
            for step in (2, 1):
                new = list(part)
                for k in range(fold):
                    if k & step == 0:
                        x, y = part[k], part[k + step]
                        new[k] = jnp.where(even[step], x, pltpu.roll(y, step * width, 1))
                        new[k + step] = jnp.where(even[step], pltpu.roll(x, LANES - step * width, 1), y)
                part = new
            for k in range(fold):
                j = tile * fold + k
                flat_ref[j * rows:(j + 1) * rows, quad * LANES:(quad + 1) * LANES] = part[k]

    raw = dot(flat_ref[...], w_ref[...]) + vector_ref[3:4, :LANES]
    count = dot(live_ref[...], whole_mask(rights, rows, data), NT)
    scale = 1.0 / (1.0 + count)
    for j in range(columns):
        raw_ref[j * rows:(j + 1) * rows, :] = raw[j * rows:(j + 1) * rows, :] * scale[:, j:j + 1]
    for i in range(rows):
        out_ref[i] = raw_ref[pl.ds(i, columns, stride=rows), :].astype(BF16)


def local(n, x, flags, scale, shift, wl, bl, wr, br, w, bias):
    seqs, rows, depth = x.shape
    width = wl.shape[1]
    outs = w.shape[1]
    lanes = rows * width
    size = lanes // LANES * seqs + rows * pl.cdiv(n * seqs, LANES)
    axes = ("res", "seq")
    flags = flags.T

    swap = [(p, p ^ 1) for p in range(n)]
    other_x, other_flags = lax.ppermute(x, "seq", swap), lax.ppermute(flags, "seq", swap)

    operands = [
        pltpu.with_memory_space_constraint(o, pltpu.HBM) for o in (x, flags, scale, shift, wl.T, bl, wr.T, br, bias)
    ]
    own_x, own_flags, weight, vectors = pl.pallas_call(
        load_kernel,
        out_shape=(
            jax.ShapeDtypeStruct(x.shape, x.dtype),
            jax.ShapeDtypeStruct(flags.shape, flags.dtype),
            jax.ShapeDtypeStruct((2 * LANES, depth), BF16),
            jax.ShapeDtypeStruct((8, 2 * LANES), F32),
        ),
        in_specs=[pl.BlockSpec(memory_space=pltpu.HBM)] * len(operands),
        scratch_shapes=[pltpu.VMEM(o.shape, o.dtype) for o in operands[2:]]
        + [pltpu.SemaphoreType.DMA((len(operands),))],
        compiler_params=pltpu.CompilerParams(vmem_limit_bytes=16 << 20),
        cost_estimate=pl.CostEstimate(flops=1 << 25, bytes_accessed=x.size * 8, transcendentals=0),
        name="load",
    )(*operands)
    wire = jax.ShapeDtypeStruct((CORES, size, LANES), BF16)
    left, right = pl.pallas_call(
        functools.partial(project_kernel, width),
        out_shape=(wire, wire),
        scratch_shapes=[pltpu.VMEM((2, seqs * rows, LANES), F32)] * 2,
        compiler_params=pltpu.CompilerParams(vmem_limit_bytes=16 << 20),
        name="project",
    )(own_x, own_flags, other_x, other_flags, weight, vectors)

    steps = right_routes(n)
    lefts = [left] + [
        lax.ppermute(left, axes, [(a * n + p, a * n + step[a][p]) for a in range(n) for p in range(n)])
        for step in left_routes(n)
    ]
    rights = [
        lax.ppermute(right, axes, [(a * n + p, step[a][p] * n + a) for a in range(n) for p in range(n)])
        for step in steps
    ]
    turned, live = pl.pallas_call(
        functools.partial(left_kernel, steps, seqs, rows, width),
        out_shape=(jax.ShapeDtypeStruct((lanes, n * seqs), BF16), jax.ShapeDtypeStruct((rows, n * seqs), BF16)),
        scratch_shapes=[
            pltpu.VMEM((n * seqs, lanes), BF16),
            pltpu.VMEM((n * seqs // LANES, lanes, LANES), F32),
        ],
        compiler_params=pltpu.CompilerParams(vmem_limit_bytes=16 << 20),
        name="turn_left",
    )(*lefts)
    return pl.pallas_call(
        functools.partial(pair_kernel, seqs, rows, rows, width),
        out_shape=jax.ShapeDtypeStruct((rows, rows, outs), BF16),
        scratch_shapes=[
            pltpu.VMEM((rows * rows, width * width), BF16),
            pltpu.VMEM((rows * rows, outs), F32),
        ],
        compiler_params=pltpu.CompilerParams(vmem_limit_bytes=16 << 20),
        name="pair",
    )(*rights, turned, live, w, vectors)


def solution(mesh):
    n = mesh.shape["res"]
    assert n == mesh.shape["seq"] and n & (n - 1) == 0 and n % CORES == 0
    in_specs = (P(("group", "seq"), "res", None), P(("group", "seq"), "res")) + (P(),) * 8
    return jax.shard_map(
        functools.partial(local, n), mesh=mesh, in_specs=in_specs,
        out_specs=P(("group", "res"), "seq", None), check_vma=False,
    )
```

```python
import functools

import jax
import jax.numpy as jnp
from jax import lax
from jax.experimental import pallas as pl
from jax.experimental.pallas import tpu as pltpu
from jax.sharding import PartitionSpec as P

LANES = 128
CORES = 2
F32 = jnp.float32
BF16 = jnp.bfloat16
TN = (((0,), (0,)), ((), ()))
NT = (((1,), (1,)), ((), ()))
NN = (((1,), (0,)), ((), ()))


def dot(a, b, dims=NN):
    return lax.dot_general(a, b, dims, preferred_element_type=F32)


def iota(shape, dim):
    return lax.broadcasted_iota(jnp.int32, shape, dim)


RIGHT = (
    ((1, 0, 2, 3), (0, 2, 1, 3), (3, 1, 0, 2), (2, 1, 3, 0)),
    ((3, 2, 1, 0), (1, 3, 2, 0), (0, 2, 3, 1), (3, 0, 2, 1)),
)
LEFT = ((3, 2, 1, 0), (3, 2, 0, 1), (3, 2, 0, 1), (2, 3, 0, 1))


def right_routes(n):
    if n == 4:
        return RIGHT
    steps = [m for m in range(n) if bin(m).count("1") % 2 == 1]
    return tuple(tuple(tuple(p ^ m for p in range(n)) for a in range(n)) for m in steps)


def left_routes(n):
    if n == 4:
        return (LEFT,)
    return tuple(tuple(tuple(p ^ k * CORES for p in range(n)) for a in range(n)) for k in range(1, n // CORES))


def sending_chip(step, r, q):
    n = len(step)
    chip = 0
    for bit in range((n // CORES - 1).bit_length()):
        for a in range(n):
            word = sum((step[a].index(to) // CORES >> bit & 1) << to for to in range(n))
            chip = chip | jnp.where(q == a, (jnp.int32(word) >> r & 1) << bit, 0)
    return chip


def project_constants(seqs, rows, width, block, tiles):
    lanes = rows * width
    spreader = (iota((rows, lanes), 1) // width == iota((rows, lanes), 0)).astype(BF16)
    place = iota((seqs, LANES), 1) // width
    mine = [iota((rows, LANES), 1) // seqs + tile * (LANES // seqs) == block for tile in range(tiles)]
    return spreader, place, mine


def project_block(width, x_ref, flag_ref, weight, vectors, constants, left_ref, right_ref, proj_ref):
    seqs, rows, depth = x_ref.shape
    fold = LANES // width
    lanes = rows * width
    data = lanes // LANES * seqs
    spreader, place, mine = constants
    x = x_ref[...].astype(F32).reshape(seqs * rows, depth)
    center = jnp.mean(x, axis=-1, keepdims=True)
    x = x - center
    spread = jnp.mean(x * x, axis=-1, keepdims=True)
    normed = x * lax.rsqrt(spread + 1e-05) * vectors[0:1] + vectors[1:2]
    both = dot(normed.astype(BF16), weight, NT) + vectors[2:3]
    proj_ref[0] = both[:, :LANES]
    proj_ref[1] = both[:, LANES:]

    flags = flag_ref[...].astype(F32)
    mask = dot(flags.astype(BF16), spreader, TN)
    flags = jnp.concatenate([flags] * (LANES // seqs), axis=1)

    for half, out_ref in ((0, left_ref), (1, right_ref)):
        for tile in range(rows // fold):
            merged = proj_ref[half, pl.ds(tile * fold, seqs, stride=rows), :]
            for k in range(1, fold):
                part = proj_ref[half, pl.ds(tile * fold + k, seqs, stride=rows), :]
                merged = jnp.where(place == k, part, merged)
            merged = merged * mask[:, tile * LANES:(tile + 1) * LANES]
            out_ref[tile * seqs:(tile + 1) * seqs, :] = merged.astype(BF16)
        for tile, here in enumerate(mine):
            out_ref[data + tile * rows:data + (tile + 1) * rows, :] = jnp.where(here, flags, 0.0).astype(BF16)


def load_kernel(x_hbm, flag_hbm, scale_hbm, shift_hbm, wl_hbm, bl_hbm, wr_hbm, br_hbm, last_hbm,
                x_ref, flag_ref, weight_ref, vector_ref,
                scale_ref, shift_ref, wl_ref, bl_ref, wr_ref, br_ref, last_ref, sems):
    copies = [
        pltpu.make_async_copy(src, dst, sems.at[k])
        for k, (src, dst) in enumerate((
            (x_hbm, x_ref), (flag_hbm, flag_ref), (scale_hbm, scale_ref), (shift_hbm, shift_ref),
            (wl_hbm, wl_ref), (bl_hbm, bl_ref), (wr_hbm, wr_ref), (br_hbm, br_ref), (last_hbm, last_ref),
        ))
    ]
    for copy in copies:
        copy.start()
    for copy in copies[1:]:
        copy.wait()
    width, depth = wl_ref.shape
    fold = LANES // width
    weight_ref[...] = jnp.concatenate([wl_ref[...]] * fold + [wr_ref[...]] * fold, axis=0)
    bias = [bl_ref[...].reshape(1, width)] * fold + [br_ref[...].reshape(1, width)] * fold
    vector_ref[...] = jnp.concatenate(
        [
            scale_ref[...].reshape(1, depth),
            shift_ref[...].reshape(1, depth),
            jnp.concatenate(bias, axis=1),
            jnp.concatenate([last_ref[...].reshape(1, LANES)] * (depth // LANES), axis=1),
            jnp.zeros((4, depth), F32),
        ],
        axis=0,
    )
    copies[0].wait()


def project_kernel(width, own_x_ref, own_flag_ref, other_x_ref, other_flag_ref, weight_ref, vector_ref,
                   left_ref, right_ref, own_proj_ref, other_proj_ref):
    seqs, rows, _ = own_x_ref.shape
    block = lax.axis_index("seq")
    core = block % CORES
    other = 1 - core
    tiles = (left_ref.shape[1] - rows * width // LANES * seqs) // rows
    for x_ref, flag_ref, proj_ref, at in (
        (own_x_ref, own_flag_ref, own_proj_ref, core),
        (other_x_ref, other_flag_ref, other_proj_ref, other),
    ):
        project_block(
            width, x_ref, flag_ref, weight_ref[...], vector_ref[...],
            project_constants(seqs, rows, width, block - core + at, tiles),
            left_ref.at[at], right_ref.at[at], proj_ref,
        )


def whole_mask(pieces, rows, data):
    total = functools.reduce(jnp.add, [p[k, data:, :] for p in pieces for k in range(CORES)])
    return jnp.concatenate([total[k:k + rows] for k in range(0, total.shape[0], rows)], axis=1)


def left_kernel(steps, seqs, rows, width, *refs):
    lefts, (out_ref, mask_ref, left_ref, turned_ref) = refs[:-4], refs[-4:]
    data = rows * width // LANES * seqs
    me_res, me_seq = lax.axis_index("res"), lax.axis_index("seq")
    order = [sending_chip(step, me_res, me_seq) for step in steps]
    for k, piece in enumerate(lefts):
        chip = me_seq // CORES ^ k
        slot = sum(jnp.where(there == chip, place, 0) for place, there in enumerate(order))
        for core in range(CORES):
            at = pl.multiple_of((slot * CORES + core) * seqs, seqs)
            for tile in range(data // seqs):
                left_ref[pl.ds(at, seqs), tile * LANES:(tile + 1) * LANES] = (
                    piece[core, tile * seqs:(tile + 1) * seqs, :]
                )
    mask_ref[...] = whole_mask(lefts, rows, data)
    for tile in range(turned_ref.shape[0]):
        turned_ref[tile] = left_ref[tile * LANES:(tile + 1) * LANES, :].astype(F32).T
        for c in range(width):
            out_ref[c * rows:(c + 1) * rows, tile * LANES:(tile + 1) * LANES] = (
                turned_ref[tile, pl.ds(c, rows, stride=width), :].astype(BF16)
            )


def pair_kernel(seqs, rows, columns, width, *refs):
    rights = refs[:-7]
    turned_ref, live_ref, w_ref, vector_ref, out_ref, flat_ref, raw_ref = refs[-7:]
    fold = LANES // width
    assert fold == 4
    data = rows * width // LANES * seqs

    right = jnp.concatenate(
        [
            jnp.concatenate([p[core, t * seqs:(t + 1) * seqs, :] for t in range(data // seqs)], axis=1)
            for p in rights
            for core in range(CORES)
        ],
        axis=0,
    )
    outer = dot(turned_ref[...], right).astype(BF16)

    place = (iota((rows, LANES), 1) // width).astype(BF16)
    even = [None] * fold
    even[1] = (place == 0.0) | (place == 2.0)
    even[2] = (place == 0.0) | (place == 1.0)
    for tile in range(columns // fold):
        for quad in range(width // fold):
            part = [
                outer[(quad * fold + k) * rows:(quad * fold + k + 1) * rows, tile * LANES:(tile + 1) * LANES]
                for k in range(fold)
            ]
            for step in (2, 1):
                new = list(part)
                for k in range(fold):
                    if k & step == 0:
                        x, y = part[k], part[k + step]
                        new[k] = jnp.where(even[step], x, pltpu.roll(y, step * width, 1))
                        new[k + step] = jnp.where(even[step], pltpu.roll(x, LANES - step * width, 1), y)
                part = new
            for k in range(fold):
                j = tile * fold + k
                flat_ref[j * rows:(j + 1) * rows, quad * LANES:(quad + 1) * LANES] = part[k]

    raw = dot(flat_ref[...], w_ref[...]) + vector_ref[3:4, :LANES]
    count = dot(live_ref[...], whole_mask(rights, rows, data), NT)
    scale = 1.0 / (1.0 + count)
    for j in range(columns):
        raw_ref[j * rows:(j + 1) * rows, :] = raw[j * rows:(j + 1) * rows, :] * scale[:, j:j + 1]
    for i in range(rows):
        out_ref[i] = raw_ref[pl.ds(i, columns, stride=rows), :].astype(BF16)


def local(n, x, flags, scale, shift, wl, bl, wr, br, w, bias):
    seqs, rows, depth = x.shape
    width = wl.shape[1]
    outs = w.shape[1]
    lanes = rows * width
    size = lanes // LANES * seqs + rows * pl.cdiv(n * seqs, LANES)
    axes = ("res", "seq")
    flags = flags.T

    swap = [(p, p ^ 1) for p in range(n)]
    other_x, other_flags = lax.ppermute(x, "seq", swap), lax.ppermute(flags, "seq", swap)

    operands = [
        pltpu.with_memory_space_constraint(o, pltpu.HBM) for o in (x, flags, scale, shift, wl.T, bl, wr.T, br, bias)
    ]
    own_x, own_flags, weight, vectors = pl.pallas_call(
        load_kernel,
        out_shape=(
            jax.ShapeDtypeStruct(x.shape, x.dtype),
            jax.ShapeDtypeStruct(flags.shape, flags.dtype),
            jax.ShapeDtypeStruct((2 * LANES, depth), BF16),
            jax.ShapeDtypeStruct((8, 2 * LANES), F32),
        ),
        in_specs=[pl.BlockSpec(memory_space=pltpu.HBM)] * len(operands),
        scratch_shapes=[pltpu.VMEM(o.shape, o.dtype) for o in operands[2:]]
        + [pltpu.SemaphoreType.DMA((len(operands),))],
        compiler_params=pltpu.CompilerParams(vmem_limit_bytes=16 << 20),
        cost_estimate=pl.CostEstimate(flops=1 << 25, bytes_accessed=x.size * 8, transcendentals=0),
        name="load",
    )(*operands)
    wire = jax.ShapeDtypeStruct((CORES, size, LANES), BF16)
    left, right = pl.pallas_call(
        functools.partial(project_kernel, width),
        out_shape=(wire, wire),
        scratch_shapes=[pltpu.VMEM((2, seqs * rows, LANES), F32)] * 2,
        compiler_params=pltpu.CompilerParams(vmem_limit_bytes=16 << 20),
        name="project",
    )(own_x, own_flags, other_x, other_flags, weight, vectors)

    steps = right_routes(n)
    lefts = [left] + [
        lax.ppermute(left, axes, [(a * n + p, a * n + step[a][p]) for a in range(n) for p in range(n)])
        for step in left_routes(n)
    ]
    rights = [
        lax.ppermute(right, axes, [(a * n + p, step[a][p] * n + a) for a in range(n) for p in range(n)])
        for step in steps
    ]
    turned, live = pl.pallas_call(
        functools.partial(left_kernel, steps, seqs, rows, width),
        out_shape=(jax.ShapeDtypeStruct((lanes, n * seqs), BF16), jax.ShapeDtypeStruct((rows, n * seqs), BF16)),
        scratch_shapes=[
            pltpu.VMEM((n * seqs, lanes), BF16),
            pltpu.VMEM((n * seqs // LANES, lanes, LANES), F32),
        ],
        compiler_params=pltpu.CompilerParams(vmem_limit_bytes=16 << 20),
        name="turn_left",
    )(*lefts)
    return pl.pallas_call(
        functools.partial(pair_kernel, seqs, rows, rows, width),
        out_shape=jax.ShapeDtypeStruct((rows, rows, outs), BF16),
        scratch_shapes=[
            pltpu.VMEM((rows * rows, width * width), BF16),
            pltpu.VMEM((rows * rows, outs), F32),
        ],
        compiler_params=pltpu.CompilerParams(vmem_limit_bytes=16 << 20),
        name="pair",
    )(*rights, turned, live, w, vectors)


def solution(mesh):
    n = mesh.shape["res"]
    assert n == mesh.shape["seq"] and n & (n - 1) == 0 and n % CORES == 0
    in_specs = (P(("group", "seq"), "res", None), P(("group", "seq"), "res")) + (P(),) * 8
    return jax.shard_map(
        functools.partial(local, n), mesh=mesh, in_specs=in_specs,
        out_specs=P(("group", "res"), "seq", None), check_vma=False,
    )
```

```python
import functools

import jax
import jax.numpy as jnp
from jax import lax
from jax.experimental import pallas as pl
from jax.experimental.pallas import tpu as pltpu
from jax.sharding import PartitionSpec as P

LANES = 128
CORES = 2
F32 = jnp.float32
BF16 = jnp.bfloat16
TN = (((0,), (0,)), ((), ()))
NT = (((1,), (1,)), ((), ()))
NN = (((1,), (0,)), ((), ()))


def dot(a, b, dims=NN):
    return lax.dot_general(a, b, dims, preferred_element_type=F32)


def iota(shape, dim):
    return lax.broadcasted_iota(jnp.int32, shape, dim)


RIGHT = (
    ((1, 0, 2, 3), (1, 0, 2, 3), (2, 3, 1, 0), (3, 1, 0, 2)),
    ((3, 2, 1, 0), (2, 3, 1, 0), (0, 1, 3, 2), (2, 0, 3, 1)),
)
LEFT = ((3, 2, 1, 0), (2, 3, 1, 0), (3, 2, 0, 1), (3, 2, 1, 0))


def right_routes(n):
    if n == 4:
        return RIGHT
    steps = [m for m in range(n) if bin(m).count("1") % 2 == 1]
    return tuple(tuple(tuple(p ^ m for p in range(n)) for a in range(n)) for m in steps)


def left_routes(n):
    if n == 4:
        return (LEFT,)
    return tuple(tuple(tuple(p ^ k * CORES for p in range(n)) for a in range(n)) for k in range(1, n // CORES))


def sending_chip(step, r, q):
    n = len(step)
    chip = 0
    for bit in range((n // CORES - 1).bit_length()):
        for a in range(n):
            word = sum((step[a].index(to) // CORES >> bit & 1) << to for to in range(n))
            chip = chip | jnp.where(q == a, (jnp.int32(word) >> r & 1) << bit, 0)
    return chip


def project_constants(seqs, rows, width, block, tiles):
    lanes = rows * width
    spreader = (iota((rows, lanes), 1) // width == iota((rows, lanes), 0)).astype(BF16)
    place = iota((seqs, LANES), 1) // width
    mine = [iota((rows, LANES), 1) // seqs + tile * (LANES // seqs) == block for tile in range(tiles)]
    return spreader, place, mine


def project_block(width, x_ref, flag_ref, weight, vectors, constants, left_ref, right_ref, proj_ref):
    seqs, rows, depth = x_ref.shape
    fold = LANES // width
    lanes = rows * width
    data = lanes // LANES * seqs
    spreader, place, mine = constants
    x = x_ref[...].astype(F32).reshape(seqs * rows, depth)
    center = jnp.mean(x, axis=-1, keepdims=True)
    x = x - center
    spread = jnp.mean(x * x, axis=-1, keepdims=True)
    normed = x * lax.rsqrt(spread + 1e-05) * vectors[0:1] + vectors[1:2]
    both = dot(normed.astype(BF16), weight, NT) + vectors[2:3]
    proj_ref[0] = both[:, :LANES]
    proj_ref[1] = both[:, LANES:]

    flags = flag_ref[...].astype(F32)
    mask = dot(flags.astype(BF16), spreader, TN)
    flags = jnp.concatenate([flags] * (LANES // seqs), axis=1)

    for half, out_ref in ((0, left_ref), (1, right_ref)):
        for tile in range(rows // fold):
            merged = proj_ref[half, pl.ds(tile * fold, seqs, stride=rows), :]
            for k in range(1, fold):
                part = proj_ref[half, pl.ds(tile * fold + k, seqs, stride=rows), :]
                merged = jnp.where(place == k, part, merged)
            merged = merged * mask[:, tile * LANES:(tile + 1) * LANES]
            out_ref[tile * seqs:(tile + 1) * seqs, :] = merged.astype(BF16)
        for tile, here in enumerate(mine):
            out_ref[data + tile * rows:data + (tile + 1) * rows, :] = jnp.where(here, flags, 0.0).astype(BF16)


def load_kernel(x_hbm, flag_hbm, scale_hbm, shift_hbm, wl_hbm, bl_hbm, wr_hbm, br_hbm, last_hbm,
                x_ref, flag_ref, weight_ref, vector_ref,
                scale_ref, shift_ref, wl_ref, bl_ref, wr_ref, br_ref, last_ref, sems):
    copies = [
        pltpu.make_async_copy(src, dst, sems.at[k])
        for k, (src, dst) in enumerate((
            (x_hbm, x_ref), (flag_hbm, flag_ref), (scale_hbm, scale_ref), (shift_hbm, shift_ref),
            (wl_hbm, wl_ref), (bl_hbm, bl_ref), (wr_hbm, wr_ref), (br_hbm, br_ref), (last_hbm, last_ref),
        ))
    ]
    for copy in copies:
        copy.start()
    for copy in copies[1:]:
        copy.wait()
    width, depth = wl_ref.shape
    fold = LANES // width
    weight_ref[...] = jnp.concatenate([wl_ref[...]] * fold + [wr_ref[...]] * fold, axis=0)
    bias = [bl_ref[...].reshape(1, width)] * fold + [br_ref[...].reshape(1, width)] * fold
    vector_ref[...] = jnp.concatenate(
        [
            scale_ref[...].reshape(1, depth),
            shift_ref[...].reshape(1, depth),
            jnp.concatenate(bias, axis=1),
            jnp.concatenate([last_ref[...].reshape(1, LANES)] * (depth // LANES), axis=1),
            jnp.zeros((4, depth), F32),
        ],
        axis=0,
    )
    copies[0].wait()


def project_kernel(width, own_x_ref, own_flag_ref, other_x_ref, other_flag_ref, weight_ref, vector_ref,
                   left_ref, right_ref, own_proj_ref, other_proj_ref):
    seqs, rows, _ = own_x_ref.shape
    block = lax.axis_index("seq")
    core = block % CORES
    other = 1 - core
    tiles = (left_ref.shape[1] - rows * width // LANES * seqs) // rows
    for x_ref, flag_ref, proj_ref, at in (
        (own_x_ref, own_flag_ref, own_proj_ref, core),
        (other_x_ref, other_flag_ref, other_proj_ref, other),
    ):
        project_block(
            width, x_ref, flag_ref, weight_ref[...], vector_ref[...],
            project_constants(seqs, rows, width, block - core + at, tiles),
            left_ref.at[at], right_ref.at[at], proj_ref,
        )


def whole_mask(pieces, rows, data):
    total = functools.reduce(jnp.add, [p[k, data:, :] for p in pieces for k in range(CORES)])
    return jnp.concatenate([total[k:k + rows] for k in range(0, total.shape[0], rows)], axis=1)


def left_kernel(steps, seqs, rows, width, *refs):
    lefts, (out_ref, mask_ref, left_ref, turned_ref) = refs[:-4], refs[-4:]
    data = rows * width // LANES * seqs
    me_res, me_seq = lax.axis_index("res"), lax.axis_index("seq")
    order = [sending_chip(step, me_res, me_seq) for step in steps]
    for k, piece in enumerate(lefts):
        chip = me_seq // CORES ^ k
        slot = sum(jnp.where(there == chip, place, 0) for place, there in enumerate(order))
        for core in range(CORES):
            at = pl.multiple_of((slot * CORES + core) * seqs, seqs)
            for tile in range(data // seqs):
                left_ref[pl.ds(at, seqs), tile * LANES:(tile + 1) * LANES] = (
                    piece[core, tile * seqs:(tile + 1) * seqs, :]
                )
    mask_ref[...] = whole_mask(lefts, rows, data)
    for tile in range(turned_ref.shape[0]):
        turned_ref[tile] = left_ref[tile * LANES:(tile + 1) * LANES, :].astype(F32).T
        for c in range(width):
            out_ref[c * rows:(c + 1) * rows, tile * LANES:(tile + 1) * LANES] = (
                turned_ref[tile, pl.ds(c, rows, stride=width), :].astype(BF16)
            )


def pair_kernel(seqs, rows, columns, width, *refs):
    rights = refs[:-7]
    turned_ref, live_ref, w_ref, vector_ref, out_ref, flat_ref, raw_ref = refs[-7:]
    fold = LANES // width
    assert fold == 4
    data = rows * width // LANES * seqs

    right = jnp.concatenate(
        [
            jnp.concatenate([p[core, t * seqs:(t + 1) * seqs, :] for t in range(data // seqs)], axis=1)
            for p in rights
            for core in range(CORES)
        ],
        axis=0,
    )
    outer = dot(turned_ref[...], right).astype(BF16)

    place = (iota((rows, LANES), 1) // width).astype(BF16)
    even = [None] * fold
    even[1] = (place == 0.0) | (place == 2.0)
    even[2] = (place == 0.0) | (place == 1.0)
    for tile in range(columns // fold):
        for quad in range(width // fold):
            part = [
                outer[(quad * fold + k) * rows:(quad * fold + k + 1) * rows, tile * LANES:(tile + 1) * LANES]
                for k in range(fold)
            ]
            for step in (2, 1):
                new = list(part)
                for k in range(fold):
                    if k & step == 0:
                        x, y = part[k], part[k + step]
                        new[k] = jnp.where(even[step], x, pltpu.roll(y, step * width, 1))
                        new[k + step] = jnp.where(even[step], pltpu.roll(x, LANES - step * width, 1), y)
                part = new
            for k in range(fold):
                j = tile * fold + k
                flat_ref[j * rows:(j + 1) * rows, quad * LANES:(quad + 1) * LANES] = part[k]

    raw = dot(flat_ref[...], w_ref[...]) + vector_ref[3:4, :LANES]
    count = dot(live_ref[...], whole_mask(rights, rows, data), NT)
    scale = 1.0 / (1.0 + count)
    for j in range(columns):
        raw_ref[j * rows:(j + 1) * rows, :] = raw[j * rows:(j + 1) * rows, :] * scale[:, j:j + 1]
    for i in range(rows):
        out_ref[i] = raw_ref[pl.ds(i, columns, stride=rows), :].astype(BF16)


def local(n, x, flags, scale, shift, wl, bl, wr, br, w, bias):
    seqs, rows, depth = x.shape
    width = wl.shape[1]
    outs = w.shape[1]
    lanes = rows * width
    size = lanes // LANES * seqs + rows * pl.cdiv(n * seqs, LANES)
    axes = ("res", "seq")
    flags = flags.T

    swap = [(p, p ^ 1) for p in range(n)]
    other_x, other_flags = lax.ppermute(x, "seq", swap), lax.ppermute(flags, "seq", swap)

    operands = [
        pltpu.with_memory_space_constraint(o, pltpu.HBM) for o in (x, flags, scale, shift, wl.T, bl, wr.T, br, bias)
    ]
    own_x, own_flags, weight, vectors = pl.pallas_call(
        load_kernel,
        out_shape=(
            jax.ShapeDtypeStruct(x.shape, x.dtype),
            jax.ShapeDtypeStruct(flags.shape, flags.dtype),
            jax.ShapeDtypeStruct((2 * LANES, depth), BF16),
            jax.ShapeDtypeStruct((8, 2 * LANES), F32),
        ),
        in_specs=[pl.BlockSpec(memory_space=pltpu.HBM)] * len(operands),
        scratch_shapes=[pltpu.VMEM(o.shape, o.dtype) for o in operands[2:]]
        + [pltpu.SemaphoreType.DMA((len(operands),))],
        compiler_params=pltpu.CompilerParams(vmem_limit_bytes=16 << 20),
        cost_estimate=pl.CostEstimate(flops=1 << 25, bytes_accessed=x.size * 8, transcendentals=0),
        name="load",
    )(*operands)
    wire = jax.ShapeDtypeStruct((CORES, size, LANES), BF16)
    left, right = pl.pallas_call(
        functools.partial(project_kernel, width),
        out_shape=(wire, wire),
        scratch_shapes=[pltpu.VMEM((2, seqs * rows, LANES), F32)] * 2,
        compiler_params=pltpu.CompilerParams(vmem_limit_bytes=16 << 20),
        name="project",
    )(own_x, own_flags, other_x, other_flags, weight, vectors)

    steps = right_routes(n)
    lefts = [left] + [
        lax.ppermute(left, axes, [(a * n + p, a * n + step[a][p]) for a in range(n) for p in range(n)])
        for step in left_routes(n)
    ]
    rights = [
        lax.ppermute(right, axes, [(a * n + p, step[a][p] * n + a) for a in range(n) for p in range(n)])
        for step in steps
    ]
    turned, live = pl.pallas_call(
        functools.partial(left_kernel, steps, seqs, rows, width),
        out_shape=(jax.ShapeDtypeStruct((lanes, n * seqs), BF16), jax.ShapeDtypeStruct((rows, n * seqs), BF16)),
        scratch_shapes=[
            pltpu.VMEM((n * seqs, lanes), BF16),
            pltpu.VMEM((n * seqs // LANES, lanes, LANES), F32),
        ],
        compiler_params=pltpu.CompilerParams(vmem_limit_bytes=16 << 20),
        name="turn_left",
    )(*lefts)
    return pl.pallas_call(
        functools.partial(pair_kernel, seqs, rows, rows, width),
        out_shape=jax.ShapeDtypeStruct((rows, rows, outs), BF16),
        scratch_shapes=[
            pltpu.VMEM((rows * rows, width * width), BF16),
            pltpu.VMEM((rows * rows, outs), F32),
        ],
        compiler_params=pltpu.CompilerParams(vmem_limit_bytes=16 << 20),
        name="pair",
    )(*rights, turned, live, w, vectors)


def solution(mesh):
    n = mesh.shape["res"]
    assert n == mesh.shape["seq"] and n & (n - 1) == 0 and n % CORES == 0
    in_specs = (P(("group", "seq"), "res", None), P(("group", "seq"), "res")) + (P(),) * 8
    return jax.shard_map(
        functools.partial(local, n), mesh=mesh, in_specs=in_specs,
        out_specs=P(("group", "res"), "seq", None), check_vma=False,
    )
```

```python
import functools

import jax
import jax.numpy as jnp
from jax import lax
from jax.experimental import pallas as pl
from jax.experimental.pallas import tpu as pltpu
from jax.sharding import PartitionSpec as P

LANES = 128
CORES = 2
F32 = jnp.float32
BF16 = jnp.bfloat16
TN = (((0,), (0,)), ((), ()))
NT = (((1,), (1,)), ((), ()))
NN = (((1,), (0,)), ((), ()))


def dot(a, b, dims=NN):
    return lax.dot_general(a, b, dims, preferred_element_type=F32)


def iota(shape, dim):
    return lax.broadcasted_iota(jnp.int32, shape, dim)


RIGHT = (
    ((1, 0, 2, 3), (1, 0, 2, 3), (3, 1, 0, 2), (2, 1, 3, 0)),
    ((3, 2, 0, 1), (2, 3, 0, 1), (0, 2, 3, 1), (3, 0, 1, 2)),
)
LEFT = ((3, 2, 1, 0), (3, 2, 0, 1), (3, 2, 1, 0), (3, 2, 0, 1))


def right_routes(n):
    if n == 4:
        return RIGHT
    steps = [m for m in range(n) if bin(m).count("1") % 2 == 1]
    return tuple(tuple(tuple(p ^ m for p in range(n)) for a in range(n)) for m in steps)


def left_routes(n):
    if n == 4:
        return (LEFT,)
    return tuple(tuple(tuple(p ^ k * CORES for p in range(n)) for a in range(n)) for k in range(1, n // CORES))


def sending_chip(step, r, q):
    n = len(step)
    chip = 0
    for bit in range((n // CORES - 1).bit_length()):
        for a in range(n):
            word = sum((step[a].index(to) // CORES >> bit & 1) << to for to in range(n))
            chip = chip | jnp.where(q == a, (jnp.int32(word) >> r & 1) << bit, 0)
    return chip


def project_kernel(width, own_x_ref, own_flag_ref, other_x_ref, other_flag_ref, weight_ref, vector_ref,
                   left_ref, right_ref, proj_ref):
    seqs, rows, depth = own_x_ref.shape
    fold = LANES // width
    lanes = rows * width
    data = lanes // LANES * seqs
    block = lax.axis_index("seq")
    core = block % CORES

    x = jnp.concatenate([ref[...].reshape(seqs * rows, depth) for ref in (own_x_ref, other_x_ref)], axis=0).astype(F32)
    center = jnp.mean(x, axis=-1, keepdims=True)
    x = x - center
    spread = jnp.mean(x * x, axis=-1, keepdims=True)
    normed = x * lax.rsqrt(spread + 1e-05) * vector_ref[0:1] + vector_ref[1:2]
    both = dot(normed.astype(BF16), weight_ref[...], NT) + vector_ref[2:3]
    proj_ref[0] = both[:, :LANES]
    proj_ref[1] = both[:, LANES:]

    spreader = (iota((rows, lanes), 1) // width == iota((rows, lanes), 0)).astype(BF16)
    place = iota((seqs, LANES), 1) // width
    lane_block = iota((rows, LANES), 1) // seqs
    for which, (flag_ref, at) in enumerate(((own_flag_ref, core), (other_flag_ref, 1 - core))):
        flags = flag_ref[...].astype(F32)
        mask = dot(flags.astype(BF16), spreader, TN)
        flags = jnp.concatenate([flags] * (LANES // seqs), axis=1)
        for half, out_ref in ((0, left_ref.at[at]), (1, right_ref.at[at])):
            for tile in range(rows // fold):
                first = which * seqs * rows + tile * fold
                merged = proj_ref[half, pl.ds(first, seqs, stride=rows), :]
                for k in range(1, fold):
                    merged = jnp.where(place == k, proj_ref[half, pl.ds(first + k, seqs, stride=rows), :], merged)
                merged = merged * mask[:, tile * LANES:(tile + 1) * LANES]
                out_ref[tile * seqs:(tile + 1) * seqs, :] = merged.astype(BF16)
            for tile in range((out_ref.shape[0] - data) // rows):
                here = lane_block + tile * (LANES // seqs) == block - core + at
                out_ref[data + tile * rows:data + (tile + 1) * rows, :] = jnp.where(here, flags, 0.0).astype(BF16)


def load_kernel(x_hbm, flag_hbm, scale_hbm, shift_hbm, wl_hbm, bl_hbm, wr_hbm, br_hbm, last_hbm,
                x_ref, flag_ref, weight_ref, vector_ref,
                scale_ref, shift_ref, wl_ref, bl_ref, wr_ref, br_ref, last_ref, sems):
    copies = [
        pltpu.make_async_copy(src, dst, sems.at[k])
        for k, (src, dst) in enumerate((
            (x_hbm, x_ref), (flag_hbm, flag_ref), (scale_hbm, scale_ref), (shift_hbm, shift_ref),
            (wl_hbm, wl_ref), (bl_hbm, bl_ref), (wr_hbm, wr_ref), (br_hbm, br_ref), (last_hbm, last_ref),
        ))
    ]
    for copy in copies:
        copy.start()
    for copy in copies[1:]:
        copy.wait()
    width, depth = wl_ref.shape
    fold = LANES // width
    weight_ref[...] = jnp.concatenate([wl_ref[...]] * fold + [wr_ref[...]] * fold, axis=0)
    bias = [bl_ref[...].reshape(1, width)] * fold + [br_ref[...].reshape(1, width)] * fold
    vector_ref[...] = jnp.concatenate(
        [
            scale_ref[...].reshape(1, depth),
            shift_ref[...].reshape(1, depth),
            jnp.concatenate(bias, axis=1),
            jnp.concatenate([last_ref[...].reshape(1, LANES)] * (depth // LANES), axis=1),
            jnp.zeros((4, depth), F32),
        ],
        axis=0,
    )
    copies[0].wait()


def whole_mask(pieces, rows, data):
    total = functools.reduce(jnp.add, [p[k, data:, :] for p in pieces for k in range(CORES)])
    return jnp.concatenate([total[k:k + rows] for k in range(0, total.shape[0], rows)], axis=1)


def left_kernel(steps, seqs, rows, width, *refs):
    lefts, (out_ref, mask_ref, left_ref, turned_ref) = refs[:-4], refs[-4:]
    data = rows * width // LANES * seqs
    me_res, me_seq = lax.axis_index("res"), lax.axis_index("seq")
    order = [sending_chip(step, me_res, me_seq) for step in steps]
    for k, piece in enumerate(lefts):
        chip = me_seq // CORES ^ k
        slot = sum(jnp.where(there == chip, place, 0) for place, there in enumerate(order))
        for core in range(CORES):
            at = pl.multiple_of((slot * CORES + core) * seqs, seqs)
            for tile in range(data // seqs):
                left_ref[pl.ds(at, seqs), tile * LANES:(tile + 1) * LANES] = (
                    piece[core, tile * seqs:(tile + 1) * seqs, :]
                )
    mask_ref[...] = whole_mask(lefts, rows, data)
    for tile in range(turned_ref.shape[0]):
        turned_ref[tile] = left_ref[tile * LANES:(tile + 1) * LANES, :].astype(F32).T
        for c in range(width):
            out_ref[c * rows:(c + 1) * rows, tile * LANES:(tile + 1) * LANES] = (
                turned_ref[tile, pl.ds(c, rows, stride=width), :].astype(BF16)
            )


def pair_kernel(seqs, rows, columns, width, *refs):
    rights = refs[:-9]
    turned_ref, live_ref, w_ref, vector_ref, out_hbm, out_ref, flat_ref, raw_ref, sems = refs[-9:]
    fold = LANES // width
    assert fold == 4
    data = rows * width // LANES * seqs

    right = jnp.concatenate(
        [
            jnp.concatenate([p[core, t * seqs:(t + 1) * seqs, :] for t in range(data // seqs)], axis=1)
            for p in rights
            for core in range(CORES)
        ],
        axis=0,
    )
    outer = dot(turned_ref[...], right).astype(BF16)

    place = (iota((rows, LANES), 1) // width).astype(BF16)
    even = [None] * fold
    even[1] = (place == 0.0) | (place == 2.0)
    even[2] = (place == 0.0) | (place == 1.0)
    for tile in range(columns // fold):
        for quad in range(width // fold):
            part = [
                outer[(quad * fold + k) * rows:(quad * fold + k + 1) * rows, tile * LANES:(tile + 1) * LANES]
                for k in range(fold)
            ]
            for step in (2, 1):
                new = list(part)
                for k in range(fold):
                    if k & step == 0:
                        x, y = part[k], part[k + step]
                        new[k] = jnp.where(even[step], x, pltpu.roll(y, step * width, 1))
                        new[k + step] = jnp.where(even[step], pltpu.roll(x, LANES - step * width, 1), y)
                part = new
            for k in range(fold):
                j = tile * fold + k
                flat_ref[j * rows:(j + 1) * rows, quad * LANES:(quad + 1) * LANES] = part[k]

    raw = dot(flat_ref[...], w_ref[...]) + vector_ref[3:4, :LANES]
    count = dot(live_ref[...], whole_mask(rights, rows, data), NT)
    scale = 1.0 / (1.0 + count)
    for j in range(columns):
        raw_ref[j * rows:(j + 1) * rows, :] = raw[j * rows:(j + 1) * rows, :] * scale[:, j:j + 1]
    parts = sems.shape[0]
    copies = []
    for part in range(parts):
        where = slice(part * rows // parts, (part + 1) * rows // parts)
        for i in range(where.start, where.stop):
            out_ref[i] = raw_ref[pl.ds(i, columns, stride=rows), :].astype(BF16)
        copies.append(pltpu.make_async_copy(out_ref.at[where], out_hbm.at[where], sems.at[part]))
        copies[-1].start()
    for copy in copies:
        copy.wait()


def local(n, x, flags, scale, shift, wl, bl, wr, br, w, bias):
    seqs, rows, depth = x.shape
    width = wl.shape[1]
    outs = w.shape[1]
    lanes = rows * width
    size = lanes // LANES * seqs + rows * pl.cdiv(n * seqs, LANES)
    axes = ("res", "seq")
    flags = flags.T

    swap = [(p, p ^ 1) for p in range(n)]
    other_x, other_flags = lax.ppermute(x, "seq", swap), lax.ppermute(flags, "seq", swap)

    operands = [
        pltpu.with_memory_space_constraint(o, pltpu.HBM) for o in (x, flags, scale, shift, wl.T, bl, wr.T, br, bias)
    ]
    own_x, own_flags, weight, vectors = pl.pallas_call(
        load_kernel,
        out_shape=(
            jax.ShapeDtypeStruct(x.shape, x.dtype),
            jax.ShapeDtypeStruct(flags.shape, flags.dtype),
            jax.ShapeDtypeStruct((2 * LANES, depth), BF16),
            jax.ShapeDtypeStruct((8, 2 * LANES), F32),
        ),
        in_specs=[pl.BlockSpec(memory_space=pltpu.HBM)] * len(operands),
        scratch_shapes=[pltpu.VMEM(o.shape, o.dtype) for o in operands[2:]]
        + [pltpu.SemaphoreType.DMA((len(operands),))],
        compiler_params=pltpu.CompilerParams(vmem_limit_bytes=16 << 20),
        cost_estimate=pl.CostEstimate(flops=1 << 25, bytes_accessed=x.size * 8, transcendentals=0),
        name="load",
    )(*operands)
    wire = jax.ShapeDtypeStruct((CORES, size, LANES), BF16)
    left, right = pl.pallas_call(
        functools.partial(project_kernel, width),
        out_shape=(wire, wire),
        scratch_shapes=[pltpu.VMEM((2, CORES * seqs * rows, LANES), F32)],
        compiler_params=pltpu.CompilerParams(vmem_limit_bytes=16 << 20),
        name="project",
    )(own_x, own_flags, other_x, other_flags, weight, vectors)

    steps = right_routes(n)
    lefts = [left] + [
        lax.ppermute(left, axes, [(a * n + p, a * n + step[a][p]) for a in range(n) for p in range(n)])
        for step in left_routes(n)
    ]
    rights = [
        lax.ppermute(right, axes, [(a * n + p, step[a][p] * n + a) for a in range(n) for p in range(n)])
        for step in steps
    ]
    turned, live = pl.pallas_call(
        functools.partial(left_kernel, steps, seqs, rows, width),
        out_shape=(jax.ShapeDtypeStruct((lanes, n * seqs), BF16), jax.ShapeDtypeStruct((rows, n * seqs), BF16)),
        scratch_shapes=[
            pltpu.VMEM((n * seqs, lanes), BF16),
            pltpu.VMEM((n * seqs // LANES, lanes, LANES), F32),
        ],
        compiler_params=pltpu.CompilerParams(vmem_limit_bytes=16 << 20),
        name="turn_left",
    )(*lefts)
    return pl.pallas_call(
        functools.partial(pair_kernel, seqs, rows, rows, width),
        out_shape=jax.ShapeDtypeStruct((rows, rows, outs), BF16),
        out_specs=pl.BlockSpec(memory_space=pltpu.HBM),
        scratch_shapes=[
            pltpu.VMEM((rows, rows, outs), BF16),
            pltpu.VMEM((rows * rows, width * width), BF16),
            pltpu.VMEM((rows * rows, outs), F32),
            pltpu.SemaphoreType.DMA((4,)),
        ],
        compiler_params=pltpu.CompilerParams(vmem_limit_bytes=16 << 20),
        name="pair",
    )(*rights, turned, live, w, vectors)


def solution(mesh):
    n = mesh.shape["res"]
    assert n == mesh.shape["seq"] and n & (n - 1) == 0 and n % CORES == 0
    in_specs = (P(("group", "seq"), "res", None), P(("group", "seq"), "res")) + (P(),) * 8
    return jax.shard_map(
        functools.partial(local, n), mesh=mesh, in_specs=in_specs,
        out_specs=P(("group", "res"), "seq", None), check_vma=False,
    )
```

```python
import functools

import jax
import jax.numpy as jnp
from jax import lax
from jax.experimental import pallas as pl
from jax.experimental.pallas import tpu as pltpu
from jax.sharding import PartitionSpec as P

LANES = 128
CORES = 2
F32 = jnp.float32
BF16 = jnp.bfloat16
TN = (((0,), (0,)), ((), ()))
NT = (((1,), (1,)), ((), ()))
NN = (((1,), (0,)), ((), ()))


def dot(a, b, dims=NN):
    return lax.dot_general(a, b, dims, preferred_element_type=F32)


def iota(shape, dim):
    return lax.broadcasted_iota(jnp.int32, shape, dim)


RIGHT = (
    ((1, 0, 2, 3), (1, 0, 2, 3), (2, 3, 1, 0), (3, 1, 0, 2)),
    ((3, 2, 1, 0), (2, 3, 1, 0), (0, 1, 3, 2), (2, 0, 3, 1)),
)
LEFT = ((3, 2, 1, 0), (2, 3, 1, 0), (3, 2, 0, 1), (3, 2, 1, 0))


def right_routes(n):
    if n == 4:
        return RIGHT
    steps = [m for m in range(n) if bin(m).count("1") % 2 == 1]
    return tuple(tuple(tuple(p ^ m for p in range(n)) for a in range(n)) for m in steps)


def left_routes(n):
    if n == 4:
        return (LEFT,)
    return tuple(tuple(tuple(p ^ k * CORES for p in range(n)) for a in range(n)) for k in range(1, n // CORES))


def sending_chip(step, r, q):
    n = len(step)
    chip = 0
    for bit in range((n // CORES - 1).bit_length()):
        for a in range(n):
            word = sum((step[a].index(to) // CORES >> bit & 1) << to for to in range(n))
            chip = chip | jnp.where(q == a, (jnp.int32(word) >> r & 1) << bit, 0)
    return chip


def project_constants(seqs, rows, width, block, tiles):
    lanes = rows * width
    spreader = (iota((rows, lanes), 1) // width == iota((rows, lanes), 0)).astype(BF16)
    place = iota((seqs, LANES), 1) // width
    mine = [iota((rows, LANES), 1) // seqs + tile * (LANES // seqs) == block for tile in range(tiles)]
    return spreader, place, mine


def project_block(width, x_ref, flag_ref, weight, vectors, constants, left_ref, right_ref, proj_ref):
    seqs, rows, depth = x_ref.shape
    fold = LANES // width
    lanes = rows * width
    data = lanes // LANES * seqs
    spreader, place, mine = constants
    x = x_ref[...].astype(F32).reshape(seqs * rows, depth)
    center = jnp.mean(x, axis=-1, keepdims=True)
    x = x - center
    spread = jnp.mean(x * x, axis=-1, keepdims=True)
    normed = x * lax.rsqrt(spread + 1e-05) * vectors[0:1] + vectors[1:2]
    both = dot(normed.astype(BF16), weight, NT) + vectors[2:3]
    proj_ref[0] = both[:, :LANES]
    proj_ref[1] = both[:, LANES:]

    flags = flag_ref[...].astype(F32)
    mask = dot(flags.astype(BF16), spreader, TN)
    flags = jnp.concatenate([flags] * (LANES // seqs), axis=1)

    for half, out_ref in ((0, left_ref), (1, right_ref)):
        for tile in range(rows // fold):
            merged = proj_ref[half, pl.ds(tile * fold, seqs, stride=rows), :]
            for k in range(1, fold):
                part = proj_ref[half, pl.ds(tile * fold + k, seqs, stride=rows), :]
                merged = jnp.where(place == k, part, merged)
            merged = merged * mask[:, tile * LANES:(tile + 1) * LANES]
            out_ref[tile * seqs:(tile + 1) * seqs, :] = merged.astype(BF16)
        for tile, here in enumerate(mine):
            out_ref[data + tile * rows:data + (tile + 1) * rows, :] = jnp.where(here, flags, 0.0).astype(BF16)


def load_kernel(x_hbm, flag_hbm, scale_hbm, shift_hbm, wl_hbm, bl_hbm, wr_hbm, br_hbm, last_hbm,
                x_ref, flag_ref, weight_ref, vector_ref,
                scale_ref, shift_ref, wl_ref, bl_ref, wr_ref, br_ref, last_ref, sems):
    copies = [
        pltpu.make_async_copy(src, dst, sems.at[k])
        for k, (src, dst) in enumerate((
            (x_hbm, x_ref), (flag_hbm, flag_ref), (scale_hbm, scale_ref), (shift_hbm, shift_ref),
            (wl_hbm, wl_ref), (bl_hbm, bl_ref), (wr_hbm, wr_ref), (br_hbm, br_ref), (last_hbm, last_ref),
        ))
    ]
    for copy in copies:
        copy.start()
    for copy in copies[1:]:
        copy.wait()
    width, depth = wl_ref.shape
    fold = LANES // width
    weight_ref[...] = jnp.concatenate([wl_ref[...]] * fold + [wr_ref[...]] * fold, axis=0)
    bias = [bl_ref[...].reshape(1, width)] * fold + [br_ref[...].reshape(1, width)] * fold
    vector_ref[...] = jnp.concatenate(
        [
            scale_ref[...].reshape(1, depth),
            shift_ref[...].reshape(1, depth),
            jnp.concatenate(bias, axis=1),
            jnp.concatenate([last_ref[...].reshape(1, LANES)] * (depth // LANES), axis=1),
            jnp.zeros((4, depth), F32),
        ],
        axis=0,
    )
    copies[0].wait()


def project_kernel(width, own_x_ref, own_flag_ref, other_x_ref, other_flag_ref, weight_ref, vector_ref,
                   left_ref, right_ref, own_proj_ref, other_proj_ref):
    seqs, rows, _ = own_x_ref.shape
    block = lax.axis_index("seq")
    core = block % CORES
    other = 1 - core
    tiles = (left_ref.shape[1] - rows * width // LANES * seqs) // rows
    for x_ref, flag_ref, proj_ref, at in (
        (own_x_ref, own_flag_ref, own_proj_ref, core),
        (other_x_ref, other_flag_ref, other_proj_ref, other),
    ):
        project_block(
            width, x_ref, flag_ref, weight_ref[...], vector_ref[...],
            project_constants(seqs, rows, width, block - core + at, tiles),
            left_ref.at[at], right_ref.at[at], proj_ref,
        )


def whole_mask(pieces, rows, data):
    total = functools.reduce(jnp.add, [p[k, data:, :] for p in pieces for k in range(CORES)])
    return jnp.concatenate([total[k:k + rows] for k in range(0, total.shape[0], rows)], axis=1)


def left_kernel(steps, seqs, rows, width, *refs):
    lefts, (out_ref, mask_ref, left_ref, turned_ref) = refs[:-4], refs[-4:]
    data = rows * width // LANES * seqs
    me_res, me_seq = lax.axis_index("res"), lax.axis_index("seq")
    order = [sending_chip(step, me_res, me_seq) for step in steps]
    for k, piece in enumerate(lefts):
        chip = me_seq // CORES ^ k
        slot = sum(jnp.where(there == chip, place, 0) for place, there in enumerate(order))
        for core in range(CORES):
            at = pl.multiple_of((slot * CORES + core) * seqs, seqs)
            for tile in range(data // seqs):
                left_ref[pl.ds(at, seqs), tile * LANES:(tile + 1) * LANES] = (
                    piece[core, tile * seqs:(tile + 1) * seqs, :]
                )
    mask_ref[...] = whole_mask(lefts, rows, data)
    for tile in range(turned_ref.shape[0]):
        turned_ref[tile] = left_ref[tile * LANES:(tile + 1) * LANES, :].astype(F32).T
        for c in range(width):
            out_ref[c * rows:(c + 1) * rows, tile * LANES:(tile + 1) * LANES] = (
                turned_ref[tile, pl.ds(c, rows, stride=width), :].astype(BF16)
            )


def pair_kernel(seqs, rows, columns, width, *refs):
    rights = refs[:-7]
    turned_ref, live_ref, w_ref, vector_ref, out_ref, flat_ref, raw_ref = refs[-7:]
    fold = LANES // width
    assert fold == 4
    data = rows * width // LANES * seqs

    right = jnp.concatenate(
        [
            jnp.concatenate([p[core, t * seqs:(t + 1) * seqs, :] for t in range(data // seqs)], axis=1)
            for p in rights
            for core in range(CORES)
        ],
        axis=0,
    )
    half = width // 2 * rows
    outer = jnp.concatenate(
        [dot(turned_ref[k:k + half, :], right).astype(BF16) for k in (0, half)], axis=0
    )

    place = (iota((rows, LANES), 1) // width).astype(BF16)
    even = [None] * fold
    even[1] = (place == 0.0) | (place == 2.0)
    even[2] = (place == 0.0) | (place == 1.0)
    for tile in range(columns // fold):
        for quad in range(width // fold):
            part = [
                outer[(quad * fold + k) * rows:(quad * fold + k + 1) * rows, tile * LANES:(tile + 1) * LANES]
                for k in range(fold)
            ]
            for step in (2, 1):
                new = list(part)
                for k in range(fold):
                    if k & step == 0:
                        x, y = part[k], part[k + step]
                        new[k] = jnp.where(even[step], x, pltpu.roll(y, step * width, 1))
                        new[k + step] = jnp.where(even[step], pltpu.roll(x, LANES - step * width, 1), y)
                part = new
            for k in range(fold):
                j = tile * fold + k
                flat_ref[j * rows:(j + 1) * rows, quad * LANES:(quad + 1) * LANES] = part[k]

    half = width // 2 * width
    raw = dot(flat_ref[:, :half], w_ref[:half, :]) + dot(flat_ref[:, half:], w_ref[half:, :]) + vector_ref[3:4, :LANES]
    count = dot(live_ref[...], whole_mask(rights, rows, data), NT)
    scale = 1.0 / (1.0 + count)
    for j in range(columns):
        raw_ref[j * rows:(j + 1) * rows, :] = raw[j * rows:(j + 1) * rows, :] * scale[:, j:j + 1]
    for i in range(rows):
        out_ref[i] = raw_ref[pl.ds(i, columns, stride=rows), :].astype(BF16)


def local(n, x, flags, scale, shift, wl, bl, wr, br, w, bias):
    seqs, rows, depth = x.shape
    width = wl.shape[1]
    outs = w.shape[1]
    lanes = rows * width
    size = lanes // LANES * seqs + rows * pl.cdiv(n * seqs, LANES)
    axes = ("res", "seq")
    flags = flags.T

    swap = [(p, p ^ 1) for p in range(n)]
    other_x, other_flags = lax.ppermute(x, "seq", swap), lax.ppermute(flags, "seq", swap)

    operands = [
        pltpu.with_memory_space_constraint(o, pltpu.HBM) for o in (x, flags, scale, shift, wl.T, bl, wr.T, br, bias)
    ]
    own_x, own_flags, weight, vectors = pl.pallas_call(
        load_kernel,
        out_shape=(
            jax.ShapeDtypeStruct(x.shape, x.dtype),
            jax.ShapeDtypeStruct(flags.shape, flags.dtype),
            jax.ShapeDtypeStruct((2 * LANES, depth), BF16),
            jax.ShapeDtypeStruct((8, 2 * LANES), F32),
        ),
        in_specs=[pl.BlockSpec(memory_space=pltpu.HBM)] * len(operands),
        scratch_shapes=[pltpu.VMEM(o.shape, o.dtype) for o in operands[2:]]
        + [pltpu.SemaphoreType.DMA((len(operands),))],
        compiler_params=pltpu.CompilerParams(vmem_limit_bytes=16 << 20),
        cost_estimate=pl.CostEstimate(flops=1 << 25, bytes_accessed=x.size * 8, transcendentals=0),
        name="load",
    )(*operands)
    wire = jax.ShapeDtypeStruct((CORES, size, LANES), BF16)
    left, right = pl.pallas_call(
        functools.partial(project_kernel, width),
        out_shape=(wire, wire),
        scratch_shapes=[pltpu.VMEM((2, seqs * rows, LANES), F32)] * 2,
        compiler_params=pltpu.CompilerParams(vmem_limit_bytes=16 << 20),
        name="project",
    )(own_x, own_flags, other_x, other_flags, weight, vectors)

    steps = right_routes(n)
    lefts = [left] + [
        lax.ppermute(left, axes, [(a * n + p, a * n + step[a][p]) for a in range(n) for p in range(n)])
        for step in left_routes(n)
    ]
    rights = [
        lax.ppermute(right, axes, [(a * n + p, step[a][p] * n + a) for a in range(n) for p in range(n)])
        for step in steps
    ]
    turned, live = pl.pallas_call(
        functools.partial(left_kernel, steps, seqs, rows, width),
        out_shape=(jax.ShapeDtypeStruct((lanes, n * seqs), BF16), jax.ShapeDtypeStruct((rows, n * seqs), BF16)),
        scratch_shapes=[
            pltpu.VMEM((n * seqs, lanes), BF16),
            pltpu.VMEM((n * seqs // LANES, lanes, LANES), F32),
        ],
        compiler_params=pltpu.CompilerParams(vmem_limit_bytes=16 << 20),
        name="turn_left",
    )(*lefts)
    return pl.pallas_call(
        functools.partial(pair_kernel, seqs, rows, rows, width),
        out_shape=jax.ShapeDtypeStruct((rows, rows, outs), BF16),
        scratch_shapes=[
            pltpu.VMEM((rows * rows, width * width), BF16),
            pltpu.VMEM((rows * rows, outs), F32),
        ],
        compiler_params=pltpu.CompilerParams(vmem_limit_bytes=16 << 20),
        name="pair",
    )(*rights, turned, live, w, vectors)


def solution(mesh):
    n = mesh.shape["res"]
    assert n == mesh.shape["seq"] and n & (n - 1) == 0 and n % CORES == 0
    in_specs = (P(("group", "seq"), "res", None), P(("group", "seq"), "res")) + (P(),) * 8
    return jax.shard_map(
        functools.partial(local, n), mesh=mesh, in_specs=in_specs,
        out_specs=P(("group", "res"), "seq", None), check_vma=False,
    )
```

```python
import functools

import jax
import jax.numpy as jnp
from jax import lax
from jax.experimental import pallas as pl
from jax.experimental.pallas import tpu as pltpu
from jax.sharding import PartitionSpec as P

LANES = 128
CORES = 2
F32 = jnp.float32
BF16 = jnp.bfloat16
TN = (((0,), (0,)), ((), ()))
NT = (((1,), (1,)), ((), ()))
NN = (((1,), (0,)), ((), ()))


def dot(a, b, dims=NN):
    return lax.dot_general(a, b, dims, preferred_element_type=F32)


def iota(shape, dim):
    return lax.broadcasted_iota(jnp.int32, shape, dim)


RIGHT = (
    ((1, 0, 2, 3), (1, 0, 2, 3), (2, 3, 1, 0), (3, 1, 0, 2)),
    ((3, 2, 1, 0), (2, 3, 1, 0), (0, 1, 3, 2), (2, 0, 3, 1)),
)
LEFT = ((3, 2, 1, 0), (2, 3, 1, 0), (3, 2, 0, 1), (3, 2, 1, 0))


def right_routes(n):
    if n == 4:
        return RIGHT
    steps = [m for m in range(n) if bin(m).count("1") % 2 == 1]
    return tuple(tuple(tuple(p ^ m for p in range(n)) for a in range(n)) for m in steps)


def left_routes(n):
    if n == 4:
        return (LEFT,)
    return tuple(tuple(tuple(p ^ k * CORES for p in range(n)) for a in range(n)) for k in range(1, n // CORES))


def sending_chip(step, r, q):
    n = len(step)
    chip = 0
    for bit in range((n // CORES - 1).bit_length()):
        for a in range(n):
            word = sum((step[a].index(to) // CORES >> bit & 1) << to for to in range(n))
            chip = chip | jnp.where(q == a, (jnp.int32(word) >> r & 1) << bit, 0)
    return chip


def project_block(width, x_ref, flag_ref, weight, vectors, spreader, place, left_ref, right_ref, proj_ref):
    seqs, rows, depth = x_ref.shape
    fold = LANES // width
    lanes = rows * width
    data = lanes // LANES * seqs
    x = x_ref[...].astype(F32).reshape(seqs * rows, depth)
    center = jnp.mean(x, axis=-1, keepdims=True)
    x = x - center
    spread = jnp.mean(x * x, axis=-1, keepdims=True)
    normed = x * lax.rsqrt(spread + 1e-05) * vectors[0:1] + vectors[1:2]
    both = dot(normed.astype(BF16), weight, NT) + vectors[2:3]
    proj_ref[0] = both[:, :LANES]
    proj_ref[1] = both[:, LANES:]

    mask = dot(flag_ref[...].astype(F32).astype(BF16), spreader, TN)
    for half, out_ref in ((0, left_ref), (1, right_ref)):
        for tile in range(rows // fold):
            merged = proj_ref[half, pl.ds(tile * fold, seqs, stride=rows), :]
            for k in range(1, fold):
                part = proj_ref[half, pl.ds(tile * fold + k, seqs, stride=rows), :]
                merged = jnp.where(place == k, part, merged)
            merged = merged * mask[:, tile * LANES:(tile + 1) * LANES]
            out_ref[tile * seqs:(tile + 1) * seqs, :] = merged.astype(BF16)


def load_kernel(x_hbm, flag_hbm, scale_hbm, shift_hbm, wl_hbm, bl_hbm, wr_hbm, br_hbm, last_hbm,
                x_ref, flag_ref, weight_ref, vector_ref,
                scale_ref, shift_ref, wl_ref, bl_ref, wr_ref, br_ref, last_ref, sems):
    copies = [
        pltpu.make_async_copy(src, dst, sems.at[k])
        for k, (src, dst) in enumerate((
            (x_hbm, x_ref), (flag_hbm, flag_ref), (scale_hbm, scale_ref), (shift_hbm, shift_ref),
            (wl_hbm, wl_ref), (bl_hbm, bl_ref), (wr_hbm, wr_ref), (br_hbm, br_ref), (last_hbm, last_ref),
        ))
    ]
    for copy in copies:
        copy.start()
    for copy in copies[1:]:
        copy.wait()
    width, depth = wl_ref.shape
    fold = LANES // width
    weight_ref[...] = jnp.concatenate([wl_ref[...]] * fold + [wr_ref[...]] * fold, axis=0)
    bias = [bl_ref[...].reshape(1, width)] * fold + [br_ref[...].reshape(1, width)] * fold
    vector_ref[...] = jnp.concatenate(
        [
            scale_ref[...].reshape(1, depth),
            shift_ref[...].reshape(1, depth),
            jnp.concatenate(bias, axis=1),
            jnp.concatenate([last_ref[...].reshape(1, LANES)] * (depth // LANES), axis=1),
            jnp.zeros((4, depth), F32),
        ],
        axis=0,
    )
    copies[0].wait()


def project_kernel(width, own_x_ref, own_flag_ref, other_x_ref, other_flag_ref, weight_ref, vector_ref,
                   left_ref, right_ref, own_proj_ref, other_proj_ref):
    seqs, rows, _ = own_x_ref.shape
    lanes = rows * width
    data = lanes // LANES * seqs
    block = lax.axis_index("seq")
    core = block % CORES
    spreader = (iota((rows, lanes), 1) // width == iota((rows, lanes), 0)).astype(BF16)
    place = iota((seqs, LANES), 1) // width
    for x_ref, flag_ref, proj_ref, at in (
        (own_x_ref, own_flag_ref, own_proj_ref, core),
        (other_x_ref, other_flag_ref, other_proj_ref, 1 - core),
    ):
        here = pl.ds(pl.multiple_of(at * data, data), data)
        project_block(
            width, x_ref, flag_ref, weight_ref[...], vector_ref[...], spreader, place,
            left_ref.at[here], right_ref.at[here], proj_ref,
        )
    own, other = (
        jnp.concatenate([ref[...].astype(F32)] * (LANES // seqs), axis=1) for ref in (own_flag_ref, other_flag_ref)
    )
    for tile in range((left_ref.shape[0] - CORES * data) // rows):
        lane_block = iota((rows, LANES), 1) // seqs + tile * (LANES // seqs)
        placed = jnp.where(lane_block == block, own, jnp.where(lane_block == block + 1 - 2 * core, other, 0.0)).astype(BF16)
        first = CORES * data + tile * rows
        for out_ref in (left_ref, right_ref):
            out_ref[first:first + rows, :] = placed


def whole_mask(pieces, rows, data):
    total = functools.reduce(jnp.add, [p[CORES * data:, :] for p in pieces])
    return jnp.concatenate([total[k:k + rows] for k in range(0, total.shape[0], rows)], axis=1)


def left_kernel(steps, seqs, rows, width, *refs):
    lefts, (out_ref, mask_ref, left_ref, turned_ref) = refs[:-4], refs[-4:]
    data = rows * width // LANES * seqs
    me_res, me_seq = lax.axis_index("res"), lax.axis_index("seq")
    order = [sending_chip(step, me_res, me_seq) for step in steps]
    for k, piece in enumerate(lefts):
        chip = me_seq // CORES ^ k
        slot = sum(jnp.where(there == chip, place, 0) for place, there in enumerate(order))
        for core in range(CORES):
            at = pl.multiple_of((slot * CORES + core) * seqs, seqs)
            for tile in range(data // seqs):
                left_ref[pl.ds(at, seqs), tile * LANES:(tile + 1) * LANES] = (
                    piece[core * data + tile * seqs:core * data + (tile + 1) * seqs, :]
                )
    mask_ref[...] = whole_mask(lefts, rows, data)
    for tile in range(turned_ref.shape[0]):
        turned_ref[tile] = left_ref[tile * LANES:(tile + 1) * LANES, :].astype(F32).T
        for c in range(width):
            out_ref[c * rows:(c + 1) * rows, tile * LANES:(tile + 1) * LANES] = (
                turned_ref[tile, pl.ds(c, rows, stride=width), :].astype(BF16)
            )


def pair_kernel(seqs, rows, columns, width, *refs):
    rights = refs[:-7]
    turned_ref, live_ref, w_ref, vector_ref, out_ref, flat_ref, raw_ref = refs[-7:]
    fold = LANES // width
    assert fold == 4
    data = rows * width // LANES * seqs

    right = jnp.concatenate(
        [
            jnp.concatenate(
                [p[core * data + t * seqs:core * data + (t + 1) * seqs, :] for t in range(data // seqs)], axis=1
            )
            for p in rights
            for core in range(CORES)
        ],
        axis=0,
    )
    outer = dot(turned_ref[...], right).astype(BF16)

    place = (iota((rows, LANES), 1) // width).astype(BF16)
    even = [None] * fold
    even[1] = (place == 0.0) | (place == 2.0)
    even[2] = (place == 0.0) | (place == 1.0)
    for tile in range(columns // fold):
        for quad in range(width // fold):
            part = [
                outer[(quad * fold + k) * rows:(quad * fold + k + 1) * rows, tile * LANES:(tile + 1) * LANES]
                for k in range(fold)
            ]
            for step in (2, 1):
                new = list(part)
                for k in range(fold):
                    if k & step == 0:
                        x, y = part[k], part[k + step]
                        new[k] = jnp.where(even[step], x, pltpu.roll(y, step * width, 1))
                        new[k + step] = jnp.where(even[step], pltpu.roll(x, LANES - step * width, 1), y)
                part = new
            for k in range(fold):
                j = tile * fold + k
                flat_ref[j * rows:(j + 1) * rows, quad * LANES:(quad + 1) * LANES] = part[k]

    raw = dot(flat_ref[...], w_ref[...]) + vector_ref[3:4, :LANES]
    count = dot(live_ref[...], whole_mask(rights, rows, data), NT)
    scale = 1.0 / (1.0 + count)
    for j in range(columns):
        raw_ref[j * rows:(j + 1) * rows, :] = raw[j * rows:(j + 1) * rows, :] * scale[:, j:j + 1]
    for i in range(rows):
        out_ref[i] = raw_ref[pl.ds(i, columns, stride=rows), :].astype(BF16)


def local(n, x, flags, scale, shift, wl, bl, wr, br, w, bias):
    seqs, rows, depth = x.shape
    width = wl.shape[1]
    outs = w.shape[1]
    lanes = rows * width
    size = CORES * lanes // LANES * seqs + rows * pl.cdiv(n * seqs, LANES)
    axes = ("res", "seq")
    flags = flags.T

    swap = [(p, p ^ 1) for p in range(n)]
    other_x, other_flags = lax.ppermute(x, "seq", swap), lax.ppermute(flags, "seq", swap)

    operands = [
        pltpu.with_memory_space_constraint(o, pltpu.HBM) for o in (x, flags, scale, shift, wl.T, bl, wr.T, br, bias)
    ]
    own_x, own_flags, weight, vectors = pl.pallas_call(
        load_kernel,
        out_shape=(
            jax.ShapeDtypeStruct(x.shape, x.dtype),
            jax.ShapeDtypeStruct(flags.shape, flags.dtype),
            jax.ShapeDtypeStruct((2 * LANES, depth), BF16),
            jax.ShapeDtypeStruct((8, 2 * LANES), F32),
        ),
        in_specs=[pl.BlockSpec(memory_space=pltpu.HBM)] * len(operands),
        scratch_shapes=[pltpu.VMEM(o.shape, o.dtype) for o in operands[2:]]
        + [pltpu.SemaphoreType.DMA((len(operands),))],
        compiler_params=pltpu.CompilerParams(vmem_limit_bytes=16 << 20),
        cost_estimate=pl.CostEstimate(flops=1 << 25, bytes_accessed=x.size * 8, transcendentals=0),
        name="load",
    )(*operands)
    wire = jax.ShapeDtypeStruct((size, LANES), BF16)
    left, right = pl.pallas_call(
        functools.partial(project_kernel, width),
        out_shape=(wire, wire),
        scratch_shapes=[pltpu.VMEM((2, seqs * rows, LANES), F32)] * 2,
        compiler_params=pltpu.CompilerParams(vmem_limit_bytes=16 << 20),
        name="project",
    )(own_x, own_flags, other_x, other_flags, weight, vectors)

    steps = right_routes(n)
    lefts = [left] + [
        lax.ppermute(left, axes, [(a * n + p, a * n + step[a][p]) for a in range(n) for p in range(n)])
        for step in left_routes(n)
    ]
    rights = [
        lax.ppermute(right, axes, [(a * n + p, step[a][p] * n + a) for a in range(n) for p in range(n)])
        for step in steps
    ]
    turned, live = pl.pallas_call(
        functools.partial(left_kernel, steps, seqs, rows, width),
        out_shape=(jax.ShapeDtypeStruct((lanes, n * seqs), BF16), jax.ShapeDtypeStruct((rows, n * seqs), BF16)),
        scratch_shapes=[
            pltpu.VMEM((n * seqs, lanes), BF16),
            pltpu.VMEM((n * seqs // LANES, lanes, LANES), F32),
        ],
        compiler_params=pltpu.CompilerParams(vmem_limit_bytes=16 << 20),
        name="turn_left",
    )(*lefts)
    return pl.pallas_call(
        functools.partial(pair_kernel, seqs, rows, rows, width),
        out_shape=jax.ShapeDtypeStruct((rows, rows, outs), BF16),
        scratch_shapes=[
            pltpu.VMEM((rows * rows, width * width), BF16),
            pltpu.VMEM((rows * rows, outs), F32),
        ],
        compiler_params=pltpu.CompilerParams(vmem_limit_bytes=16 << 20),
        name="pair",
    )(*rights, turned, live, w, vectors)


def solution(mesh):
    n = mesh.shape["res"]
    assert n == mesh.shape["seq"] and n & (n - 1) == 0 and n % CORES == 0
    in_specs = (P(("group", "seq"), "res", None), P(("group", "seq"), "res")) + (P(),) * 8
    return jax.shard_map(
        functools.partial(local, n), mesh=mesh, in_specs=in_specs,
        out_specs=P(("group", "res"), "seq", None), check_vma=False,
    )
```

```python
import functools

import jax
import jax.numpy as jnp
from jax import lax
from jax.experimental import pallas as pl
from jax.experimental.pallas import tpu as pltpu
from jax.sharding import PartitionSpec as P

LANES = 128
CORES = 2
F32 = jnp.float32
BF16 = jnp.bfloat16
TN = (((0,), (0,)), ((), ()))
NT = (((1,), (1,)), ((), ()))
NN = (((1,), (0,)), ((), ()))


def dot(a, b, dims=NN):
    return lax.dot_general(a, b, dims, preferred_element_type=F32)


def iota(shape, dim):
    return lax.broadcasted_iota(jnp.int32, shape, dim)


RIGHT = (
    ((1, 0, 2, 3), (1, 0, 2, 3), (2, 3, 1, 0), (3, 1, 0, 2)),
    ((3, 2, 1, 0), (2, 3, 1, 0), (0, 1, 3, 2), (2, 0, 3, 1)),
)
LEFT = ((3, 2, 1, 0), (2, 3, 1, 0), (3, 2, 0, 1), (3, 2, 1, 0))


def right_routes(n):
    if n == 4:
        return RIGHT
    steps = [m for m in range(n) if bin(m).count("1") % 2 == 1]
    return tuple(tuple(tuple(p ^ m for p in range(n)) for a in range(n)) for m in steps)


def left_routes(n):
    if n == 4:
        return (LEFT,)
    return tuple(tuple(tuple(p ^ k * CORES for p in range(n)) for a in range(n)) for k in range(1, n // CORES))


def sending_chip(step, r, q):
    n = len(step)
    chip = 0
    for bit in range((n // CORES - 1).bit_length()):
        for a in range(n):
            word = sum((step[a].index(to) // CORES >> bit & 1) << to for to in range(n))
            chip = chip | jnp.where(q == a, (jnp.int32(word) >> r & 1) << bit, 0)
    return chip


def norm_project(x_ref, weight, vectors):
    seqs, rows, depth = x_ref.shape
    x = x_ref[...].astype(F32).reshape(seqs * rows, depth)
    center = jnp.mean(x, axis=-1, keepdims=True)
    x = x - center
    spread = jnp.mean(x * x, axis=-1, keepdims=True)
    normed = x * lax.rsqrt(spread + 1e-05) * vectors[0:1] + vectors[1:2]
    return dot(normed.astype(BF16), weight, NT) + vectors[2:3]


def merge(width, seqs, rows, proj_ref, mask, place, left_ref, right_ref):
    fold = LANES // width
    for half, out_ref in ((0, left_ref), (1, right_ref)):
        for tile in range(rows // fold):
            merged = proj_ref[half, pl.ds(tile * fold, seqs, stride=rows), :]
            for k in range(1, fold):
                part = proj_ref[half, pl.ds(tile * fold + k, seqs, stride=rows), :]
                merged = jnp.where(place == k, part, merged)
            merged = merged * mask[:, tile * LANES:(tile + 1) * LANES]
            out_ref[tile * seqs:(tile + 1) * seqs, :] = merged.astype(BF16)


def load_kernel(x_hbm, flag_hbm, scale_hbm, shift_hbm, wl_hbm, bl_hbm, wr_hbm, br_hbm, last_hbm,
                x_ref, flag_ref, weight_ref, vector_ref,
                scale_ref, shift_ref, wl_ref, bl_ref, wr_ref, br_ref, last_ref, sems):
    copies = [
        pltpu.make_async_copy(src, dst, sems.at[k])
        for k, (src, dst) in enumerate((
            (x_hbm, x_ref), (flag_hbm, flag_ref), (scale_hbm, scale_ref), (shift_hbm, shift_ref),
            (wl_hbm, wl_ref), (bl_hbm, bl_ref), (wr_hbm, wr_ref), (br_hbm, br_ref), (last_hbm, last_ref),
        ))
    ]
    for copy in copies:
        copy.start()
    for copy in copies[1:]:
        copy.wait()
    width, depth = wl_ref.shape
    fold = LANES // width
    weight_ref[...] = jnp.concatenate([wl_ref[...]] * fold + [wr_ref[...]] * fold, axis=0)
    bias = [bl_ref[...].reshape(1, width)] * fold + [br_ref[...].reshape(1, width)] * fold
    vector_ref[...] = jnp.concatenate(
        [
            scale_ref[...].reshape(1, depth),
            shift_ref[...].reshape(1, depth),
            jnp.concatenate(bias, axis=1),
            jnp.concatenate([last_ref[...].reshape(1, LANES)] * (depth // LANES), axis=1),
            jnp.zeros((4, depth), F32),
        ],
        axis=0,
    )
    copies[0].wait()


def project_kernel(width, own_x_ref, own_flag_ref, other_x_ref, other_flag_ref, weight_ref, vector_ref,
                   left_ref, right_ref, own_proj_ref, other_proj_ref):
    seqs, rows, _ = own_x_ref.shape
    lanes = rows * width
    data = lanes // LANES * seqs
    block = lax.axis_index("seq")
    core = block % CORES
    spreader = (iota((rows, lanes), 1) // width == iota((rows, lanes), 0)).astype(BF16)
    place = iota((seqs, LANES), 1) // width
    flags = [ref[...].astype(F32) for ref in (own_flag_ref, other_flag_ref)]
    masks = [dot(f.astype(BF16), spreader, TN) for f in flags]
    own, other = (jnp.concatenate([f] * (LANES // seqs), axis=1) for f in flags)
    for tile in range((left_ref.shape[0] - CORES * data) // rows):
        lane_block = iota((rows, LANES), 1) // seqs + tile * (LANES // seqs)
        placed = jnp.where(lane_block == block, own, jnp.where(lane_block == block + 1 - 2 * core, other, 0.0)).astype(BF16)
        first = CORES * data + tile * rows
        for out_ref in (left_ref, right_ref):
            out_ref[first:first + rows, :] = placed

    for x_ref, proj_ref in ((own_x_ref, own_proj_ref), (other_x_ref, other_proj_ref)):
        both = norm_project(x_ref, weight_ref[...], vector_ref[...])
        proj_ref[0] = both[:, :LANES]
        proj_ref[1] = both[:, LANES:]
    for proj_ref, mask, at in ((own_proj_ref, masks[0], core), (other_proj_ref, masks[1], 1 - core)):
        here = pl.ds(pl.multiple_of(at * data, data), data)
        merge(width, seqs, rows, proj_ref, mask, place, left_ref.at[here], right_ref.at[here])


def whole_mask(pieces, rows, data):
    total = functools.reduce(jnp.add, [p[CORES * data:, :] for p in pieces])
    return jnp.concatenate([total[k:k + rows] for k in range(0, total.shape[0], rows)], axis=1)


def left_kernel(steps, seqs, rows, width, *refs):
    lefts, (out_ref, mask_ref, left_ref, turned_ref) = refs[:-4], refs[-4:]
    data = rows * width // LANES * seqs
    me_res, me_seq = lax.axis_index("res"), lax.axis_index("seq")
    order = [sending_chip(step, me_res, me_seq) for step in steps]
    for k, piece in enumerate(lefts):
        chip = me_seq // CORES ^ k
        slot = sum(jnp.where(there == chip, place, 0) for place, there in enumerate(order))
        for core in range(CORES):
            at = pl.multiple_of((slot * CORES + core) * seqs, seqs)
            for tile in range(data // seqs):
                left_ref[pl.ds(at, seqs), tile * LANES:(tile + 1) * LANES] = (
                    piece[core * data + tile * seqs:core * data + (tile + 1) * seqs, :]
                )
    mask_ref[...] = whole_mask(lefts, rows, data)
    for tile in range(turned_ref.shape[0]):
        turned_ref[tile] = left_ref[tile * LANES:(tile + 1) * LANES, :].astype(F32).T
        for c in range(width):
            out_ref[c * rows:(c + 1) * rows, tile * LANES:(tile + 1) * LANES] = (
                turned_ref[tile, pl.ds(c, rows, stride=width), :].astype(BF16)
            )


def pair_kernel(seqs, rows, columns, width, *refs):
    rights = refs[:-7]
    turned_ref, live_ref, w_ref, vector_ref, out_ref, flat_ref, raw_ref = refs[-7:]
    fold = LANES // width
    assert fold == 4
    data = rows * width // LANES * seqs

    count = dot(live_ref[...], whole_mask(rights, rows, data), NT)
    scale = 1.0 / (1.0 + count)
    scales = [jnp.broadcast_to(scale[:, j:j + 1], (rows, w_ref.shape[1])) for j in range(columns)]
    right = jnp.concatenate(
        [
            jnp.concatenate(
                [p[core * data + t * seqs:core * data + (t + 1) * seqs, :] for t in range(data // seqs)], axis=1
            )
            for p in rights
            for core in range(CORES)
        ],
        axis=0,
    )
    outer = dot(turned_ref[...], right).astype(BF16)

    place = (iota((rows, LANES), 1) // width).astype(BF16)
    even = [None] * fold
    even[1] = (place == 0.0) | (place == 2.0)
    even[2] = (place == 0.0) | (place == 1.0)
    for tile in range(columns // fold):
        for quad in range(width // fold):
            part = [
                outer[(quad * fold + k) * rows:(quad * fold + k + 1) * rows, tile * LANES:(tile + 1) * LANES]
                for k in range(fold)
            ]
            for step in (2, 1):
                new = list(part)
                for k in range(fold):
                    if k & step == 0:
                        x, y = part[k], part[k + step]
                        new[k] = jnp.where(even[step], x, pltpu.roll(y, step * width, 1))
                        new[k + step] = jnp.where(even[step], pltpu.roll(x, LANES - step * width, 1), y)
                part = new
            for k in range(fold):
                j = tile * fold + k
                flat_ref[j * rows:(j + 1) * rows, quad * LANES:(quad + 1) * LANES] = part[k]

    raw = dot(flat_ref[...], w_ref[...]) + vector_ref[3:4, :LANES]
    for j in range(columns):
        raw_ref[j * rows:(j + 1) * rows, :] = raw[j * rows:(j + 1) * rows, :] * scales[j]
    for i in range(rows):
        out_ref[i] = raw_ref[pl.ds(i, columns, stride=rows), :].astype(BF16)


def local(n, x, flags, scale, shift, wl, bl, wr, br, w, bias):
    seqs, rows, depth = x.shape
    width = wl.shape[1]
    outs = w.shape[1]
    lanes = rows * width
    size = CORES * lanes // LANES * seqs + rows * pl.cdiv(n * seqs, LANES)
    axes = ("res", "seq")
    flags = flags.T

    swap = [(p, p ^ 1) for p in range(n)]
    other_x, other_flags = lax.ppermute(x, "seq", swap), lax.ppermute(flags, "seq", swap)

    operands = [
        pltpu.with_memory_space_constraint(o, pltpu.HBM) for o in (x, flags, scale, shift, wl.T, bl, wr.T, br, bias)
    ]
    own_x, own_flags, weight, vectors = pl.pallas_call(
        load_kernel,
        out_shape=(
            jax.ShapeDtypeStruct(x.shape, x.dtype),
            jax.ShapeDtypeStruct(flags.shape, flags.dtype),
            jax.ShapeDtypeStruct((2 * LANES, depth), BF16),
            jax.ShapeDtypeStruct((8, 2 * LANES), F32),
        ),
        in_specs=[pl.BlockSpec(memory_space=pltpu.HBM)] * len(operands),
        scratch_shapes=[pltpu.VMEM(o.shape, o.dtype) for o in operands[2:]]
        + [pltpu.SemaphoreType.DMA((len(operands),))],
        compiler_params=pltpu.CompilerParams(vmem_limit_bytes=16 << 20),
        cost_estimate=pl.CostEstimate(flops=1 << 25, bytes_accessed=x.size * 8, transcendentals=0),
        name="load",
    )(*operands)
    wire = jax.ShapeDtypeStruct((size, LANES), BF16)
    left, right = pl.pallas_call(
        functools.partial(project_kernel, width),
        out_shape=(wire, wire),
        scratch_shapes=[pltpu.VMEM((2, seqs * rows, LANES), F32)] * 2,
        compiler_params=pltpu.CompilerParams(vmem_limit_bytes=16 << 20),
        name="project",
    )(own_x, own_flags, other_x, other_flags, weight, vectors)

    steps = right_routes(n)
    lefts = [left] + [
        lax.ppermute(left, axes, [(a * n + p, a * n + step[a][p]) for a in range(n) for p in range(n)])
        for step in left_routes(n)
    ]
    rights = [
        lax.ppermute(right, axes, [(a * n + p, step[a][p] * n + a) for a in range(n) for p in range(n)])
        for step in steps
    ]
    turned, live = pl.pallas_call(
        functools.partial(left_kernel, steps, seqs, rows, width),
        out_shape=(jax.ShapeDtypeStruct((lanes, n * seqs), BF16), jax.ShapeDtypeStruct((rows, n * seqs), BF16)),
        scratch_shapes=[
            pltpu.VMEM((n * seqs, lanes), BF16),
            pltpu.VMEM((n * seqs // LANES, lanes, LANES), F32),
        ],
        compiler_params=pltpu.CompilerParams(vmem_limit_bytes=16 << 20),
        name="turn_left",
    )(*lefts)
    return pl.pallas_call(
        functools.partial(pair_kernel, seqs, rows, rows, width),
        out_shape=jax.ShapeDtypeStruct((rows, rows, outs), BF16),
        scratch_shapes=[
            pltpu.VMEM((rows * rows, width * width), BF16),
            pltpu.VMEM((rows * rows, outs), F32),
        ],
        compiler_params=pltpu.CompilerParams(vmem_limit_bytes=16 << 20),
        name="pair",
    )(*rights, turned, live, w, vectors)


def solution(mesh):
    n = mesh.shape["res"]
    assert n == mesh.shape["seq"] and n & (n - 1) == 0 and n % CORES == 0
    in_specs = (P(("group", "seq"), "res", None), P(("group", "seq"), "res")) + (P(),) * 8
    return jax.shard_map(
        functools.partial(local, n), mesh=mesh, in_specs=in_specs,
        out_specs=P(("group", "res"), "seq", None), check_vma=False,
    )
```

```python
import functools

import jax
import jax.numpy as jnp
from jax import lax
from jax.experimental import pallas as pl
from jax.experimental.pallas import tpu as pltpu
from jax.sharding import PartitionSpec as P

LANES = 128
CORES = 2
F32 = jnp.float32
BF16 = jnp.bfloat16
TN = (((0,), (0,)), ((), ()))
NT = (((1,), (1,)), ((), ()))
NN = (((1,), (0,)), ((), ()))


def dot(a, b, dims=NN):
    return lax.dot_general(a, b, dims, preferred_element_type=F32)


def iota(shape, dim):
    return lax.broadcasted_iota(jnp.int32, shape, dim)


RIGHT = (
    ((1, 0, 2, 3), (1, 0, 2, 3), (2, 3, 1, 0), (3, 1, 0, 2)),
    ((3, 2, 1, 0), (2, 3, 1, 0), (0, 1, 3, 2), (2, 0, 3, 1)),
)
LEFT = ((3, 2, 1, 0), (2, 3, 1, 0), (3, 2, 0, 1), (3, 2, 1, 0))


def right_routes(n):
    if n == 4:
        return RIGHT
    steps = [m for m in range(n) if bin(m).count("1") % 2 == 1]
    return tuple(tuple(tuple(p ^ m for p in range(n)) for a in range(n)) for m in steps)


def left_routes(n):
    if n == 4:
        return (LEFT,)
    return tuple(tuple(tuple(p ^ k * CORES for p in range(n)) for a in range(n)) for k in range(1, n // CORES))


def sending_chip(step, r, q):
    n = len(step)
    chip = 0
    for bit in range((n // CORES - 1).bit_length()):
        for a in range(n):
            word = sum((step[a].index(to) // CORES >> bit & 1) << to for to in range(n))
            chip = chip | jnp.where(q == a, (jnp.int32(word) >> r & 1) << bit, 0)
    return chip


def project_block(width, x_ref, mask_of, weight, vectors, place, left_ref, right_ref, proj_ref):
    seqs, rows, depth = x_ref.shape
    fold = LANES // width
    lanes = rows * width
    data = lanes // LANES * seqs
    x = x_ref[...].astype(F32).reshape(seqs * rows, depth)
    center = jnp.mean(x, axis=-1, keepdims=True)
    x = x - center
    spread = jnp.mean(x * x, axis=-1, keepdims=True)
    normed = x * lax.rsqrt(spread + 1e-05) * vectors[0:1] + vectors[1:2]
    both = dot(normed.astype(BF16), weight, NT) + vectors[2:3]
    proj_ref[0] = both[:, :LANES]
    proj_ref[1] = both[:, LANES:]

    mask = mask_of()
    for half, out_ref in ((0, left_ref), (1, right_ref)):
        for tile in range(rows // fold):
            merged = proj_ref[half, pl.ds(tile * fold, seqs, stride=rows), :]
            for k in range(1, fold):
                part = proj_ref[half, pl.ds(tile * fold + k, seqs, stride=rows), :]
                merged = jnp.where(place == k, part, merged)
            merged = merged * mask[:, tile * LANES:(tile + 1) * LANES]
            out_ref[tile * seqs:(tile + 1) * seqs, :] = merged.astype(BF16)


def load_kernel(x_hbm, flag_hbm, scale_hbm, shift_hbm, wl_hbm, bl_hbm, wr_hbm, br_hbm, last_hbm,
                x_ref, flag_ref, weight_ref, vector_ref, spreader_ref, mask_ref,
                scale_ref, shift_ref, wl_ref, bl_ref, wr_ref, br_ref, last_ref, sems):
    copies = [
        pltpu.make_async_copy(src, dst, sems.at[k])
        for k, (src, dst) in enumerate((
            (x_hbm, x_ref), (flag_hbm, flag_ref), (scale_hbm, scale_ref), (shift_hbm, shift_ref),
            (wl_hbm, wl_ref), (bl_hbm, bl_ref), (wr_hbm, wr_ref), (br_hbm, br_ref), (last_hbm, last_ref),
        ))
    ]
    for copy in copies:
        copy.start()
    for copy in copies[1:]:
        copy.wait()
    width, depth = wl_ref.shape
    fold = LANES // width
    weight_ref[...] = jnp.concatenate([wl_ref[...]] * fold + [wr_ref[...]] * fold, axis=0)
    bias = [bl_ref[...].reshape(1, width)] * fold + [br_ref[...].reshape(1, width)] * fold
    vector_ref[...] = jnp.concatenate(
        [
            scale_ref[...].reshape(1, depth),
            shift_ref[...].reshape(1, depth),
            jnp.concatenate(bias, axis=1),
            jnp.concatenate([last_ref[...].reshape(1, LANES)] * (depth // LANES), axis=1),
            jnp.zeros((4, depth), F32),
        ],
        axis=0,
    )
    shape = spreader_ref.shape
    spreader_ref[...] = (iota(shape, 1) // width == iota(shape, 0)).astype(BF16)
    mask_ref[...] = spread_mask(flag_ref, spreader_ref)
    copies[0].wait()


def spread_mask(flag_ref, spreader_ref):
    return dot(flag_ref[...].astype(F32).astype(BF16), spreader_ref[...], TN)


def project_kernel(width, own_x_ref, own_flag_ref, other_x_ref, other_flag_ref, weight_ref, vector_ref,
                   spreader_ref, own_mask_ref, left_ref, right_ref, own_proj_ref, other_proj_ref):
    seqs, rows, _ = own_x_ref.shape
    lanes = rows * width
    data = lanes // LANES * seqs
    block = lax.axis_index("seq")
    core = block % CORES
    place = iota((seqs, LANES), 1) // width
    for x_ref, mask_of, proj_ref, at in (
        (own_x_ref, lambda: own_mask_ref[...], own_proj_ref, core),
        (other_x_ref, lambda: spread_mask(other_flag_ref, spreader_ref), other_proj_ref, 1 - core),
    ):
        here = pl.ds(pl.multiple_of(at * data, data), data)
        project_block(
            width, x_ref, mask_of, weight_ref[...], vector_ref[...], place,
            left_ref.at[here], right_ref.at[here], proj_ref,
        )
    own, other = (
        jnp.concatenate([ref[...].astype(F32)] * (LANES // seqs), axis=1) for ref in (own_flag_ref, other_flag_ref)
    )
    for tile in range((left_ref.shape[0] - CORES * data) // rows):
        lane_block = iota((rows, LANES), 1) // seqs + tile * (LANES // seqs)
        placed = jnp.where(lane_block == block, own, jnp.where(lane_block == block + 1 - 2 * core, other, 0.0)).astype(BF16)
        first = CORES * data + tile * rows
        for out_ref in (left_ref, right_ref):
            out_ref[first:first + rows, :] = placed


def whole_mask(pieces, rows, data):
    total = functools.reduce(jnp.add, [p[CORES * data:, :] for p in pieces])
    return jnp.concatenate([total[k:k + rows] for k in range(0, total.shape[0], rows)], axis=1)


def left_kernel(steps, seqs, rows, width, *refs):
    lefts, (out_ref, mask_ref, left_ref, turned_ref) = refs[:-4], refs[-4:]
    data = rows * width // LANES * seqs
    me_res, me_seq = lax.axis_index("res"), lax.axis_index("seq")
    order = [sending_chip(step, me_res, me_seq) for step in steps]
    for k, piece in enumerate(lefts):
        chip = me_seq // CORES ^ k
        slot = sum(jnp.where(there == chip, place, 0) for place, there in enumerate(order))
        for core in range(CORES):
            at = pl.multiple_of((slot * CORES + core) * seqs, seqs)
            for tile in range(data // seqs):
                left_ref[pl.ds(at, seqs), tile * LANES:(tile + 1) * LANES] = (
                    piece[core * data + tile * seqs:core * data + (tile + 1) * seqs, :]
                )
    mask_ref[...] = whole_mask(lefts, rows, data)
    for tile in range(turned_ref.shape[0]):
        turned_ref[tile] = left_ref[tile * LANES:(tile + 1) * LANES, :].astype(F32).T
        for c in range(width):
            out_ref[c * rows:(c + 1) * rows, tile * LANES:(tile + 1) * LANES] = (
                turned_ref[tile, pl.ds(c, rows, stride=width), :].astype(BF16)
            )


def pair_kernel(seqs, rows, columns, width, *refs):
    rights = refs[:-7]
    turned_ref, live_ref, w_ref, vector_ref, out_ref, flat_ref, raw_ref = refs[-7:]
    fold = LANES // width
    assert fold == 4
    data = rows * width // LANES * seqs

    count = dot(live_ref[...], whole_mask(rights, rows, data), NT)
    scale = 1.0 / (1.0 + count)
    scales = [jnp.broadcast_to(scale[:, j:j + 1], (rows, w_ref.shape[1])) for j in range(columns)]
    right = jnp.concatenate(
        [
            jnp.concatenate(
                [p[core * data + t * seqs:core * data + (t + 1) * seqs, :] for t in range(data // seqs)], axis=1
            )
            for p in rights
            for core in range(CORES)
        ],
        axis=0,
    )
    outer = dot(turned_ref[...], right).astype(BF16)

    place = (iota((rows, LANES), 1) // width).astype(BF16)
    even = [None] * fold
    even[1] = (place == 0.0) | (place == 2.0)
    even[2] = (place == 0.0) | (place == 1.0)
    for tile in range(columns // fold):
        for quad in range(width // fold):
            part = [
                outer[(quad * fold + k) * rows:(quad * fold + k + 1) * rows, tile * LANES:(tile + 1) * LANES]
                for k in range(fold)
            ]
            for step in (2, 1):
                new = list(part)
                for k in range(fold):
                    if k & step == 0:
                        x, y = part[k], part[k + step]
                        new[k] = jnp.where(even[step], x, pltpu.roll(y, step * width, 1))
                        new[k + step] = jnp.where(even[step], pltpu.roll(x, LANES - step * width, 1), y)
                part = new
            for k in range(fold):
                j = tile * fold + k
                flat_ref[j * rows:(j + 1) * rows, quad * LANES:(quad + 1) * LANES] = part[k]

    raw = dot(flat_ref[...], w_ref[...]) + vector_ref[3:4, :LANES]
    for j in range(columns):
        raw_ref[j * rows:(j + 1) * rows, :] = raw[j * rows:(j + 1) * rows, :] * scales[j]
    for i in range(rows):
        out_ref[i] = raw_ref[pl.ds(i, columns, stride=rows), :].astype(BF16)


def local(n, x, flags, scale, shift, wl, bl, wr, br, w, bias):
    seqs, rows, depth = x.shape
    width = wl.shape[1]
    outs = w.shape[1]
    lanes = rows * width
    size = CORES * lanes // LANES * seqs + rows * pl.cdiv(n * seqs, LANES)
    axes = ("res", "seq")
    flags = flags.T

    swap = [(p, p ^ 1) for p in range(n)]
    other_x, other_flags = lax.ppermute(x, "seq", swap), lax.ppermute(flags, "seq", swap)

    operands = [
        pltpu.with_memory_space_constraint(o, pltpu.HBM) for o in (x, flags, scale, shift, wl.T, bl, wr.T, br, bias)
    ]
    own_x, own_flags, weight, vectors, spreader, own_mask = pl.pallas_call(
        load_kernel,
        out_shape=(
            jax.ShapeDtypeStruct(x.shape, x.dtype),
            jax.ShapeDtypeStruct(flags.shape, flags.dtype),
            jax.ShapeDtypeStruct((2 * LANES, depth), BF16),
            jax.ShapeDtypeStruct((8, 2 * LANES), F32),
            jax.ShapeDtypeStruct((rows, lanes), BF16),
            jax.ShapeDtypeStruct((seqs, lanes), F32),
        ),
        in_specs=[pl.BlockSpec(memory_space=pltpu.HBM)] * len(operands),
        scratch_shapes=[pltpu.VMEM(o.shape, o.dtype) for o in operands[2:]]
        + [pltpu.SemaphoreType.DMA((len(operands),))],
        compiler_params=pltpu.CompilerParams(vmem_limit_bytes=16 << 20),
        cost_estimate=pl.CostEstimate(flops=1 << 25, bytes_accessed=x.size * 8, transcendentals=0),
        name="load",
    )(*operands)
    wire = jax.ShapeDtypeStruct((size, LANES), BF16)
    left, right = pl.pallas_call(
        functools.partial(project_kernel, width),
        out_shape=(wire, wire),
        scratch_shapes=[pltpu.VMEM((2, seqs * rows, LANES), F32)] * 2,
        compiler_params=pltpu.CompilerParams(vmem_limit_bytes=16 << 20),
        name="project",
    )(own_x, own_flags, other_x, other_flags, weight, vectors, spreader, own_mask)

    steps = right_routes(n)
    lefts = [left] + [
        lax.ppermute(left, axes, [(a * n + p, a * n + step[a][p]) for a in range(n) for p in range(n)])
        for step in left_routes(n)
    ]
    rights = [
        lax.ppermute(right, axes, [(a * n + p, step[a][p] * n + a) for a in range(n) for p in range(n)])
        for step in steps
    ]
    turned, live = pl.pallas_call(
        functools.partial(left_kernel, steps, seqs, rows, width),
        out_shape=(jax.ShapeDtypeStruct((lanes, n * seqs), BF16), jax.ShapeDtypeStruct((rows, n * seqs), BF16)),
        scratch_shapes=[
            pltpu.VMEM((n * seqs, lanes), BF16),
            pltpu.VMEM((n * seqs // LANES, lanes, LANES), F32),
        ],
        compiler_params=pltpu.CompilerParams(vmem_limit_bytes=16 << 20),
        name="turn_left",
    )(*lefts)
    return pl.pallas_call(
        functools.partial(pair_kernel, seqs, rows, rows, width),
        out_shape=jax.ShapeDtypeStruct((rows, rows, outs), BF16),
        scratch_shapes=[
            pltpu.VMEM((rows * rows, width * width), BF16),
            pltpu.VMEM((rows * rows, outs), F32),
        ],
        compiler_params=pltpu.CompilerParams(vmem_limit_bytes=16 << 20),
        name="pair",
    )(*rights, turned, live, w, vectors)


def solution(mesh):
    n = mesh.shape["res"]
    assert n == mesh.shape["seq"] and n & (n - 1) == 0 and n % CORES == 0
    in_specs = (P(("group", "seq"), "res", None), P(("group", "seq"), "res")) + (P(),) * 8
    return jax.shard_map(
        functools.partial(local, n), mesh=mesh, in_specs=in_specs,
        out_specs=P(("group", "res"), "seq", None), check_vma=False,
    )
```

```python
import functools

import jax
import jax.numpy as jnp
from jax import lax
from jax.experimental import pallas as pl
from jax.experimental.pallas import tpu as pltpu
from jax.sharding import PartitionSpec as P

LANES = 128
CORES = 2
F32 = jnp.float32
BF16 = jnp.bfloat16
TN = (((0,), (0,)), ((), ()))
NT = (((1,), (1,)), ((), ()))
NN = (((1,), (0,)), ((), ()))


def dot(a, b, dims=NN):
    return lax.dot_general(a, b, dims, preferred_element_type=F32)


def iota(shape, dim):
    return lax.broadcasted_iota(jnp.int32, shape, dim)


RIGHT = (
    ((1, 0, 2, 3), (1, 0, 2, 3), (1, 3, 0, 2), (2, 1, 3, 0)),
    ((3, 2, 0, 1), (2, 3, 0, 1), (0, 2, 3, 1), (3, 0, 1, 2)),
)
LEFT = ((2, 3, 1, 0), (3, 2, 0, 1), (3, 2, 1, 0), (3, 2, 0, 1))


def right_routes(n):
    if n == 4:
        return RIGHT
    steps = [m for m in range(n) if bin(m).count("1") % 2 == 1]
    return tuple(tuple(tuple(p ^ m for p in range(n)) for a in range(n)) for m in steps)


def left_routes(n):
    if n == 4:
        return (LEFT,)
    return tuple(tuple(tuple(p ^ k * CORES for p in range(n)) for a in range(n)) for k in range(1, n // CORES))


def sending_chip(step, r, q):
    n = len(step)
    chip = 0
    for bit in range((n // CORES - 1).bit_length()):
        for a in range(n):
            word = sum((step[a].index(to) // CORES >> bit & 1) << to for to in range(n))
            chip = chip | jnp.where(q == a, (jnp.int32(word) >> r & 1) << bit, 0)
    return chip


def project_block(width, x_ref, mask_of, weight, vectors, place, left_ref, right_ref, proj_ref):
    seqs, rows, depth = x_ref.shape
    fold = LANES // width
    lanes = rows * width
    data = lanes // LANES * seqs
    x = x_ref[...].astype(F32).reshape(seqs * rows, depth)
    center = jnp.mean(x, axis=-1, keepdims=True)
    x = x - center
    spread = jnp.mean(x * x, axis=-1, keepdims=True)
    normed = x * lax.rsqrt(spread + 1e-05) * vectors[0:1] + vectors[1:2]
    both = dot(normed.astype(BF16), weight, NT) + vectors[2:3]
    proj_ref[0] = both[:, :LANES]
    proj_ref[1] = both[:, LANES:]

    mask = mask_of()
    for half, out_ref in ((0, left_ref), (1, right_ref)):
        for tile in range(rows // fold):
            merged = proj_ref[half, pl.ds(tile * fold, seqs, stride=rows), :]
            for k in range(1, fold):
                part = proj_ref[half, pl.ds(tile * fold + k, seqs, stride=rows), :]
                merged = jnp.where(place == k, part, merged)
            merged = merged * mask[:, tile * LANES:(tile + 1) * LANES]
            out_ref[tile * seqs:(tile + 1) * seqs, :] = merged.astype(BF16)


def load_kernel(x_hbm, flag_hbm, scale_hbm, shift_hbm, wl_hbm, bl_hbm, wr_hbm, br_hbm, last_hbm,
                x_ref, flag_ref, weight_ref, vector_ref, spreader_ref, mask_ref,
                scale_ref, shift_ref, wl_ref, bl_ref, wr_ref, br_ref, last_ref, sems):
    copies = [
        pltpu.make_async_copy(src, dst, sems.at[k])
        for k, (src, dst) in enumerate((
            (x_hbm, x_ref), (flag_hbm, flag_ref), (scale_hbm, scale_ref), (shift_hbm, shift_ref),
            (wl_hbm, wl_ref), (bl_hbm, bl_ref), (wr_hbm, wr_ref), (br_hbm, br_ref), (last_hbm, last_ref),
        ))
    ]
    for copy in copies:
        copy.start()
    for copy in copies[1:]:
        copy.wait()
    width, depth = wl_ref.shape
    fold = LANES // width
    weight_ref[...] = jnp.concatenate([wl_ref[...]] * fold + [wr_ref[...]] * fold, axis=0)
    bias = [bl_ref[...].reshape(1, width)] * fold + [br_ref[...].reshape(1, width)] * fold
    vector_ref[...] = jnp.concatenate(
        [
            scale_ref[...].reshape(1, depth),
            shift_ref[...].reshape(1, depth),
            jnp.concatenate(bias, axis=1),
            jnp.concatenate([last_ref[...].reshape(1, LANES)] * (depth // LANES), axis=1),
            jnp.zeros((4, depth), F32),
        ],
        axis=0,
    )
    shape = spreader_ref.shape
    spreader_ref[...] = (iota(shape, 1) // width == iota(shape, 0)).astype(BF16)
    mask_ref[...] = spread_mask(flag_ref, spreader_ref)
    copies[0].wait()


def spread_mask(flag_ref, spreader_ref):
    return dot(flag_ref[...].astype(F32).astype(BF16), spreader_ref[...], TN)


def project_kernel(width, own_x_ref, own_flag_ref, other_x_ref, other_flag_ref, weight_ref, vector_ref,
                   spreader_ref, own_mask_ref, left_ref, right_ref, own_proj_ref, other_proj_ref):
    seqs, rows, _ = own_x_ref.shape
    lanes = rows * width
    data = lanes // LANES * seqs
    block = lax.axis_index("seq")
    core = block % CORES
    place = iota((seqs, LANES), 1) // width
    for x_ref, mask_of, proj_ref, at in (
        (own_x_ref, lambda: own_mask_ref[...], own_proj_ref, core),
        (other_x_ref, lambda: spread_mask(other_flag_ref, spreader_ref), other_proj_ref, 1 - core),
    ):
        here = pl.ds(pl.multiple_of(at * data, data), data)
        project_block(
            width, x_ref, mask_of, weight_ref[...], vector_ref[...], place,
            left_ref.at[here], right_ref.at[here], proj_ref,
        )
    own, other = (
        jnp.concatenate([ref[...].astype(F32)] * (LANES // seqs), axis=1) for ref in (own_flag_ref, other_flag_ref)
    )
    for tile in range((left_ref.shape[0] - CORES * data) // rows):
        lane_block = iota((rows, LANES), 1) // seqs + tile * (LANES // seqs)
        placed = jnp.where(lane_block == block, own, jnp.where(lane_block == block + 1 - 2 * core, other, 0.0)).astype(BF16)
        first = CORES * data + tile * rows
        for out_ref in (left_ref, right_ref):
            out_ref[first:first + rows, :] = placed


def whole_mask(pieces, rows, data):
    total = functools.reduce(jnp.add, [p[CORES * data:, :] for p in pieces])
    return jnp.concatenate([total[k:k + rows] for k in range(0, total.shape[0], rows)], axis=1)


def left_kernel(steps, seqs, rows, width, *refs):
    lefts, (out_ref, mask_ref, left_ref, turned_ref) = refs[:-4], refs[-4:]
    data = rows * width // LANES * seqs
    me_res, me_seq = lax.axis_index("res"), lax.axis_index("seq")
    order = [sending_chip(step, me_res, me_seq) for step in steps]
    for k, piece in enumerate(lefts):
        chip = me_seq // CORES ^ k
        slot = sum(jnp.where(there == chip, place, 0) for place, there in enumerate(order))
        for core in range(CORES):
            at = pl.multiple_of((slot * CORES + core) * seqs, seqs)
            for tile in range(data // seqs):
                left_ref[pl.ds(at, seqs), tile * LANES:(tile + 1) * LANES] = (
                    piece[core * data + tile * seqs:core * data + (tile + 1) * seqs, :]
                )
    mask_ref[...] = whole_mask(lefts, rows, data)
    for tile in range(turned_ref.shape[0]):
        turned_ref[tile] = left_ref[tile * LANES:(tile + 1) * LANES, :].astype(F32).T
        for c in range(width):
            out_ref[c * rows:(c + 1) * rows, tile * LANES:(tile + 1) * LANES] = (
                turned_ref[tile, pl.ds(c, rows, stride=width), :].astype(BF16)
            )


def pair_kernel(seqs, rows, columns, width, *refs):
    rights = refs[:-7]
    turned_ref, live_ref, w_ref, vector_ref, out_ref, flat_ref, raw_ref = refs[-7:]
    fold = LANES // width
    assert fold == 4
    data = rows * width // LANES * seqs

    count = dot(live_ref[...], whole_mask(rights, rows, data), NT)
    scale = 1.0 / (1.0 + count)
    scales = [jnp.broadcast_to(scale[:, j:j + 1], (rows, w_ref.shape[1])) for j in range(columns)]
    right = jnp.concatenate(
        [
            jnp.concatenate(
                [p[core * data + t * seqs:core * data + (t + 1) * seqs, :] for t in range(data // seqs)], axis=1
            )
            for p in rights
            for core in range(CORES)
        ],
        axis=0,
    )
    outer = dot(turned_ref[...], right).astype(BF16)

    place = (iota((rows, LANES), 1) // width).astype(BF16)
    even = [None] * fold
    even[1] = (place == 0.0) | (place == 2.0)
    even[2] = (place == 0.0) | (place == 1.0)
    for quad in range(width // fold):
        for tile in range(columns // fold):
            part = [
                outer[(quad * fold + k) * rows:(quad * fold + k + 1) * rows, tile * LANES:(tile + 1) * LANES]
                for k in range(fold)
            ]
            for step in (2, 1):
                new = list(part)
                for k in range(fold):
                    if k & step == 0:
                        x, y = part[k], part[k + step]
                        new[k] = jnp.where(even[step], x, pltpu.roll(y, step * width, 1))
                        new[k + step] = jnp.where(even[step], pltpu.roll(x, LANES - step * width, 1), y)
                part = new
            for k in range(fold):
                j = tile * fold + k
                flat_ref[j * rows:(j + 1) * rows, quad * LANES:(quad + 1) * LANES] = part[k]

    raw = dot(flat_ref[...], w_ref[...]) + vector_ref[3:4, :LANES]
    for j in range(columns):
        raw_ref[j * rows:(j + 1) * rows, :] = raw[j * rows:(j + 1) * rows, :] * scales[j]
    for i in range(rows):
        out_ref[i] = raw_ref[pl.ds(i, columns, stride=rows), :].astype(BF16)


def local(n, x, flags, scale, shift, wl, bl, wr, br, w, bias):
    seqs, rows, depth = x.shape
    width = wl.shape[1]
    outs = w.shape[1]
    lanes = rows * width
    size = CORES * lanes // LANES * seqs + rows * pl.cdiv(n * seqs, LANES)
    axes = ("res", "seq")
    flags = flags.T

    swap = [(p, p ^ 1) for p in range(n)]
    other_x, other_flags = lax.ppermute(x, "seq", swap), lax.ppermute(flags, "seq", swap)

    operands = [
        pltpu.with_memory_space_constraint(o, pltpu.HBM) for o in (x, flags, scale, shift, wl.T, bl, wr.T, br, bias)
    ]
    own_x, own_flags, weight, vectors, spreader, own_mask = pl.pallas_call(
        load_kernel,
        out_shape=(
            jax.ShapeDtypeStruct(x.shape, x.dtype),
            jax.ShapeDtypeStruct(flags.shape, flags.dtype),
            jax.ShapeDtypeStruct((2 * LANES, depth), BF16),
            jax.ShapeDtypeStruct((8, 2 * LANES), F32),
            jax.ShapeDtypeStruct((rows, lanes), BF16),
            jax.ShapeDtypeStruct((seqs, lanes), F32),
        ),
        in_specs=[pl.BlockSpec(memory_space=pltpu.HBM)] * len(operands),
        scratch_shapes=[pltpu.VMEM(o.shape, o.dtype) for o in operands[2:]]
        + [pltpu.SemaphoreType.DMA((len(operands),))],
        compiler_params=pltpu.CompilerParams(vmem_limit_bytes=16 << 20),
        cost_estimate=pl.CostEstimate(flops=1 << 25, bytes_accessed=x.size * 8, transcendentals=0),
        name="load",
    )(*operands)
    wire = jax.ShapeDtypeStruct((size, LANES), BF16)
    left, right = pl.pallas_call(
        functools.partial(project_kernel, width),
        out_shape=(wire, wire),
        scratch_shapes=[pltpu.VMEM((2, seqs * rows, LANES), F32)] * 2,
        compiler_params=pltpu.CompilerParams(vmem_limit_bytes=16 << 20),
        name="project",
    )(own_x, own_flags, other_x, other_flags, weight, vectors, spreader, own_mask)

    steps = right_routes(n)
    lefts = [left] + [
        lax.ppermute(left, axes, [(a * n + p, a * n + step[a][p]) for a in range(n) for p in range(n)])
        for step in left_routes(n)
    ]
    rights = [
        lax.ppermute(right, axes, [(a * n + p, step[a][p] * n + a) for a in range(n) for p in range(n)])
        for step in steps
    ]
    turned, live = pl.pallas_call(
        functools.partial(left_kernel, steps, seqs, rows, width),
        out_shape=(jax.ShapeDtypeStruct((lanes, n * seqs), BF16), jax.ShapeDtypeStruct((rows, n * seqs), BF16)),
        scratch_shapes=[
            pltpu.VMEM((n * seqs, lanes), BF16),
            pltpu.VMEM((n * seqs // LANES, lanes, LANES), F32),
        ],
        compiler_params=pltpu.CompilerParams(vmem_limit_bytes=16 << 20),
        name="turn_left",
    )(*lefts)
    return pl.pallas_call(
        functools.partial(pair_kernel, seqs, rows, rows, width),
        out_shape=jax.ShapeDtypeStruct((rows, rows, outs), BF16),
        scratch_shapes=[
            pltpu.VMEM((rows * rows, width * width), BF16),
            pltpu.VMEM((rows * rows, outs), F32),
        ],
        compiler_params=pltpu.CompilerParams(vmem_limit_bytes=16 << 20),
        name="pair",
    )(*rights, turned, live, w, vectors)


def solution(mesh):
    n = mesh.shape["res"]
    assert n == mesh.shape["seq"] and n & (n - 1) == 0 and n % CORES == 0
    in_specs = (P(("group", "seq"), "res", None), P(("group", "seq"), "res")) + (P(),) * 8
    return jax.shard_map(
        functools.partial(local, n), mesh=mesh, in_specs=in_specs,
        out_specs=P(("group", "res"), "seq", None), check_vma=False,
    )
```

```python
import functools

import jax
import jax.numpy as jnp
from jax import lax
from jax.experimental import pallas as pl
from jax.experimental.pallas import tpu as pltpu
from jax.sharding import PartitionSpec as P

LANES = 128
CORES = 2
F32 = jnp.float32
BF16 = jnp.bfloat16
TN = (((0,), (0,)), ((), ()))
NT = (((1,), (1,)), ((), ()))
NN = (((1,), (0,)), ((), ()))


def dot(a, b, dims=NN):
    return lax.dot_general(a, b, dims, preferred_element_type=F32)


def iota(shape, dim):
    return lax.broadcasted_iota(jnp.int32, shape, dim)


RIGHT = (
    ((1, 0, 2, 3), (1, 0, 2, 3), (1, 3, 0, 2), (2, 1, 3, 0)),
    ((3, 2, 0, 1), (2, 3, 0, 1), (0, 2, 3, 1), (3, 0, 1, 2)),
)
LEFT = ((2, 3, 1, 0), (3, 2, 0, 1), (3, 2, 1, 0), (3, 2, 0, 1))


def right_routes(n):
    if n == 4:
        return RIGHT
    steps = [m for m in range(n) if bin(m).count("1") % 2 == 1]
    return tuple(tuple(tuple(p ^ m for p in range(n)) for a in range(n)) for m in steps)


def left_routes(n):
    if n == 4:
        return (LEFT,)
    return tuple(tuple(tuple(p ^ k * CORES for p in range(n)) for a in range(n)) for k in range(1, n // CORES))


def sending_chip(step, r, q):
    n = len(step)
    chip = 0
    for bit in range((n // CORES - 1).bit_length()):
        for a in range(n):
            word = sum((step[a].index(to) // CORES >> bit & 1) << to for to in range(n))
            chip = chip | jnp.where(q == a, (jnp.int32(word) >> r & 1) << bit, 0)
    return chip


def norm(x_ref, vectors):
    seqs, rows, depth = x_ref.shape
    x = x_ref[...].astype(F32).reshape(seqs * rows, depth)
    center = jnp.mean(x, axis=-1, keepdims=True)
    x = x - center
    spread = jnp.mean(x * x, axis=-1, keepdims=True)
    return (x * lax.rsqrt(spread + 1e-05) * vectors[0:1] + vectors[1:2]).astype(BF16)


def project_block(width, seqs, rows, normed, mask_of, weight, vectors, place, left_ref, right_ref, proj_ref):
    fold = LANES // width
    both = dot(normed, weight, NT) + vectors[2:3]
    proj_ref[0] = both[:, :LANES]
    proj_ref[1] = both[:, LANES:]

    mask = mask_of()
    for half, out_ref in ((0, left_ref), (1, right_ref)):
        for tile in range(rows // fold):
            merged = proj_ref[half, pl.ds(tile * fold, seqs, stride=rows), :]
            for k in range(1, fold):
                part = proj_ref[half, pl.ds(tile * fold + k, seqs, stride=rows), :]
                merged = jnp.where(place == k, part, merged)
            merged = merged * mask[:, tile * LANES:(tile + 1) * LANES]
            out_ref[tile * seqs:(tile + 1) * seqs, :] = merged.astype(BF16)


def load_kernel(x_hbm, flag_hbm, scale_hbm, shift_hbm, wl_hbm, bl_hbm, wr_hbm, br_hbm, last_hbm,
                normed_ref, flag_ref, weight_ref, vector_ref, spreader_ref, mask_ref,
                x_ref, scale_ref, shift_ref, wl_ref, bl_ref, wr_ref, br_ref, last_ref, sems):
    copies = [
        pltpu.make_async_copy(src, dst, sems.at[k])
        for k, (src, dst) in enumerate((
            (x_hbm, x_ref), (flag_hbm, flag_ref), (scale_hbm, scale_ref), (shift_hbm, shift_ref),
            (wl_hbm, wl_ref), (bl_hbm, bl_ref), (wr_hbm, wr_ref), (br_hbm, br_ref), (last_hbm, last_ref),
        ))
    ]
    for copy in copies:
        copy.start()
    for copy in copies[1:]:
        copy.wait()
    width, depth = wl_ref.shape
    fold = LANES // width
    weight_ref[...] = jnp.concatenate([wl_ref[...]] * fold + [wr_ref[...]] * fold, axis=0)
    bias = [bl_ref[...].reshape(1, width)] * fold + [br_ref[...].reshape(1, width)] * fold
    vector_ref[...] = jnp.concatenate(
        [
            scale_ref[...].reshape(1, depth),
            shift_ref[...].reshape(1, depth),
            jnp.concatenate(bias, axis=1),
            jnp.concatenate([last_ref[...].reshape(1, LANES)] * (depth // LANES), axis=1),
            jnp.zeros((4, depth), F32),
        ],
        axis=0,
    )
    shape = spreader_ref.shape
    spreader_ref[...] = (iota(shape, 1) // width == iota(shape, 0)).astype(BF16)
    mask_ref[...] = spread_mask(flag_ref, spreader_ref)
    copies[0].wait()
    normed_ref[...] = norm(x_ref, vector_ref[...])


def spread_mask(flag_ref, spreader_ref):
    return dot(flag_ref[...].astype(F32).astype(BF16), spreader_ref[...], TN)


def project_kernel(width, own_normed_ref, own_flag_ref, other_x_ref, other_flag_ref, weight_ref, vector_ref,
                   spreader_ref, own_mask_ref, left_ref, right_ref, own_proj_ref, other_proj_ref):
    seqs, rows, _ = other_x_ref.shape
    lanes = rows * width
    data = lanes // LANES * seqs
    block = lax.axis_index("seq")
    core = block % CORES
    place = iota((seqs, LANES), 1) // width
    for normed_of, mask_of, proj_ref, at in (
        (lambda: own_normed_ref[...], lambda: own_mask_ref[...], own_proj_ref, core),
        (
            lambda: norm(other_x_ref, vector_ref[...]), lambda: spread_mask(other_flag_ref, spreader_ref),
            other_proj_ref, 1 - core,
        ),
    ):
        here = pl.ds(pl.multiple_of(at * data, data), data)
        project_block(
            width, seqs, rows, normed_of(), mask_of, weight_ref[...], vector_ref[...], place,
            left_ref.at[here], right_ref.at[here], proj_ref,
        )
    own, other = (
        jnp.concatenate([ref[...].astype(F32)] * (LANES // seqs), axis=1) for ref in (own_flag_ref, other_flag_ref)
    )
    for tile in range((left_ref.shape[0] - CORES * data) // rows):
        lane_block = iota((rows, LANES), 1) // seqs + tile * (LANES // seqs)
        placed = jnp.where(lane_block == block, own, jnp.where(lane_block == block + 1 - 2 * core, other, 0.0)).astype(BF16)
        first = CORES * data + tile * rows
        for out_ref in (left_ref, right_ref):
            out_ref[first:first + rows, :] = placed


def whole_mask(pieces, rows, data):
    total = functools.reduce(jnp.add, [p[CORES * data:, :] for p in pieces])
    return jnp.concatenate([total[k:k + rows] for k in range(0, total.shape[0], rows)], axis=1)


def left_kernel(steps, seqs, rows, width, *refs):
    lefts, (out_ref, mask_ref, left_ref, turned_ref) = refs[:-4], refs[-4:]
    data = rows * width // LANES * seqs
    me_res, me_seq = lax.axis_index("res"), lax.axis_index("seq")
    order = [sending_chip(step, me_res, me_seq) for step in steps]
    for k, piece in enumerate(lefts):
        chip = me_seq // CORES ^ k
        slot = sum(jnp.where(there == chip, place, 0) for place, there in enumerate(order))
        for core in range(CORES):
            at = pl.multiple_of((slot * CORES + core) * seqs, seqs)
            for tile in range(data // seqs):
                left_ref[pl.ds(at, seqs), tile * LANES:(tile + 1) * LANES] = (
                    piece[core * data + tile * seqs:core * data + (tile + 1) * seqs, :]
                )
    mask_ref[...] = whole_mask(lefts, rows, data)
    for tile in range(turned_ref.shape[0]):
        turned_ref[tile] = left_ref[tile * LANES:(tile + 1) * LANES, :].astype(F32).T
        for c in range(width):
            out_ref[c * rows:(c + 1) * rows, tile * LANES:(tile + 1) * LANES] = (
                turned_ref[tile, pl.ds(c, rows, stride=width), :].astype(BF16)
            )


def pair_kernel(seqs, rows, columns, width, *refs):
    rights = refs[:-7]
    turned_ref, live_ref, w_ref, vector_ref, out_ref, flat_ref, raw_ref = refs[-7:]
    fold = LANES // width
    assert fold == 4
    data = rows * width // LANES * seqs

    count = dot(live_ref[...], whole_mask(rights, rows, data), NT)
    scale = 1.0 / (1.0 + count)
    scales = [jnp.broadcast_to(scale[:, j:j + 1], (rows, w_ref.shape[1])) for j in range(columns)]
    right = jnp.concatenate(
        [
            jnp.concatenate(
                [p[core * data + t * seqs:core * data + (t + 1) * seqs, :] for t in range(data // seqs)], axis=1
            )
            for p in rights
            for core in range(CORES)
        ],
        axis=0,
    )
    outer = dot(turned_ref[...], right).astype(BF16)

    place = (iota((rows, LANES), 1) // width).astype(BF16)
    even = [None] * fold
    even[1] = (place == 0.0) | (place == 2.0)
    even[2] = (place == 0.0) | (place == 1.0)
    for quad in range(width // fold):
        for tile in range(columns // fold):
            part = [
                outer[(quad * fold + k) * rows:(quad * fold + k + 1) * rows, tile * LANES:(tile + 1) * LANES]
                for k in range(fold)
            ]
            for step in (2, 1):
                new = list(part)
                for k in range(fold):
                    if k & step == 0:
                        x, y = part[k], part[k + step]
                        new[k] = jnp.where(even[step], x, pltpu.roll(y, step * width, 1))
                        new[k + step] = jnp.where(even[step], pltpu.roll(x, LANES - step * width, 1), y)
                part = new
            for k in range(fold):
                j = tile * fold + k
                flat_ref[j * rows:(j + 1) * rows, quad * LANES:(quad + 1) * LANES] = part[k]

    raw = dot(flat_ref[...], w_ref[...]) + vector_ref[3:4, :LANES]
    for j in range(columns):
        raw_ref[j * rows:(j + 1) * rows, :] = raw[j * rows:(j + 1) * rows, :] * scales[j]
    for i in range(rows):
        out_ref[i] = raw_ref[pl.ds(i, columns, stride=rows), :].astype(BF16)


def local(n, x, flags, scale, shift, wl, bl, wr, br, w, bias):
    seqs, rows, depth = x.shape
    width = wl.shape[1]
    outs = w.shape[1]
    lanes = rows * width
    size = CORES * lanes // LANES * seqs + rows * pl.cdiv(n * seqs, LANES)
    axes = ("res", "seq")
    flags = flags.T

    swap = [(p, p ^ 1) for p in range(n)]
    other_x, other_flags = lax.ppermute(x, "seq", swap), lax.ppermute(flags, "seq", swap)

    operands = [
        pltpu.with_memory_space_constraint(o, pltpu.HBM) for o in (x, flags, scale, shift, wl.T, bl, wr.T, br, bias)
    ]
    own_normed, own_flags, weight, vectors, spreader, own_mask = pl.pallas_call(
        load_kernel,
        out_shape=(
            jax.ShapeDtypeStruct((seqs * rows, depth), BF16),
            jax.ShapeDtypeStruct(flags.shape, flags.dtype),
            jax.ShapeDtypeStruct((2 * LANES, depth), BF16),
            jax.ShapeDtypeStruct((8, 2 * LANES), F32),
            jax.ShapeDtypeStruct((rows, lanes), BF16),
            jax.ShapeDtypeStruct((seqs, lanes), F32),
        ),
        in_specs=[pl.BlockSpec(memory_space=pltpu.HBM)] * len(operands),
        scratch_shapes=[pltpu.VMEM(o.shape, o.dtype) for o in (operands[0], *operands[2:])]
        + [pltpu.SemaphoreType.DMA((len(operands),))],
        compiler_params=pltpu.CompilerParams(vmem_limit_bytes=16 << 20),
        cost_estimate=pl.CostEstimate(flops=1 << 25, bytes_accessed=x.size * 8, transcendentals=0),
        name="load",
    )(*operands)
    wire = jax.ShapeDtypeStruct((size, LANES), BF16)
    left, right = pl.pallas_call(
        functools.partial(project_kernel, width),
        out_shape=(wire, wire),
        scratch_shapes=[pltpu.VMEM((2, seqs * rows, LANES), F32)] * 2,
        compiler_params=pltpu.CompilerParams(vmem_limit_bytes=16 << 20),
        name="project",
    )(own_normed, own_flags, other_x, other_flags, weight, vectors, spreader, own_mask)

    steps = right_routes(n)
    lefts = [left] + [
        lax.ppermute(left, axes, [(a * n + p, a * n + step[a][p]) for a in range(n) for p in range(n)])
        for step in left_routes(n)
    ]
    rights = [
        lax.ppermute(right, axes, [(a * n + p, step[a][p] * n + a) for a in range(n) for p in range(n)])
        for step in steps
    ]
    turned, live = pl.pallas_call(
        functools.partial(left_kernel, steps, seqs, rows, width),
        out_shape=(jax.ShapeDtypeStruct((lanes, n * seqs), BF16), jax.ShapeDtypeStruct((rows, n * seqs), BF16)),
        scratch_shapes=[
            pltpu.VMEM((n * seqs, lanes), BF16),
            pltpu.VMEM((n * seqs // LANES, lanes, LANES), F32),
        ],
        compiler_params=pltpu.CompilerParams(vmem_limit_bytes=16 << 20),
        name="turn_left",
    )(*lefts)
    return pl.pallas_call(
        functools.partial(pair_kernel, seqs, rows, rows, width),
        out_shape=jax.ShapeDtypeStruct((rows, rows, outs), BF16),
        scratch_shapes=[
            pltpu.VMEM((rows * rows, width * width), BF16),
            pltpu.VMEM((rows * rows, outs), F32),
        ],
        compiler_params=pltpu.CompilerParams(vmem_limit_bytes=16 << 20),
        name="pair",
    )(*rights, turned, live, w, vectors)


def solution(mesh):
    n = mesh.shape["res"]
    assert n == mesh.shape["seq"] and n & (n - 1) == 0 and n % CORES == 0
    in_specs = (P(("group", "seq"), "res", None), P(("group", "seq"), "res")) + (P(),) * 8
    return jax.shard_map(
        functools.partial(local, n), mesh=mesh, in_specs=in_specs,
        out_specs=P(("group", "res"), "seq", None), check_vma=False,
    )
```

```python
import functools

import jax
import jax.numpy as jnp
from jax import lax
from jax.experimental import pallas as pl
from jax.experimental.pallas import tpu as pltpu
from jax.sharding import PartitionSpec as P

LANES = 128
CORES = 2
F32 = jnp.float32
BF16 = jnp.bfloat16
TN = (((0,), (0,)), ((), ()))
NT = (((1,), (1,)), ((), ()))
NN = (((1,), (0,)), ((), ()))


def dot(a, b, dims=NN):
    return lax.dot_general(a, b, dims, preferred_element_type=F32)


def iota(shape, dim):
    return lax.broadcasted_iota(jnp.int32, shape, dim)


RIGHT = (
    ((1, 0, 2, 3), (1, 0, 2, 3), (1, 3, 0, 2), (2, 1, 3, 0)),
    ((3, 2, 0, 1), (2, 3, 0, 1), (0, 2, 3, 1), (3, 0, 1, 2)),
)
LEFT = ((2, 3, 1, 0), (3, 2, 0, 1), (3, 2, 1, 0), (3, 2, 0, 1))


def right_routes(n):
    if n == 4:
        return RIGHT
    steps = [m for m in range(n) if bin(m).count("1") % 2 == 1]
    return tuple(tuple(tuple(p ^ m for p in range(n)) for a in range(n)) for m in steps)


def left_routes(n):
    if n == 4:
        return (LEFT,)
    return tuple(tuple(tuple(p ^ k * CORES for p in range(n)) for a in range(n)) for k in range(1, n // CORES))


def sending_chip(step, r, q):
    n = len(step)
    chip = 0
    for bit in range((n // CORES - 1).bit_length()):
        for a in range(n):
            word = sum((step[a].index(to) // CORES >> bit & 1) << to for to in range(n))
            chip = chip | jnp.where(q == a, (jnp.int32(word) >> r & 1) << bit, 0)
    return chip


def project_block(width, x_ref, mask_of, weight, vectors, place, left_ref, right_ref, proj_ref):
    seqs, rows, depth = x_ref.shape
    fold = LANES // width
    lanes = rows * width
    data = lanes // LANES * seqs
    x = x_ref[...].astype(F32).reshape(seqs * rows, depth)
    center = jnp.mean(x, axis=-1, keepdims=True)
    x = x - center
    spread = jnp.mean(x * x, axis=-1, keepdims=True)
    normed = x * lax.rsqrt(spread + 1e-05) * vectors[0:1] + vectors[1:2]
    both = dot(normed.astype(BF16), weight, NT) + vectors[2:3]
    proj_ref[0] = both[:, :LANES]
    proj_ref[1] = both[:, LANES:]

    mask = mask_of()
    for half, out_ref in ((0, left_ref), (1, right_ref)):
        for tile in range(rows // fold):
            merged = proj_ref[half, pl.ds(tile * fold, seqs, stride=rows), :]
            for k in range(1, fold):
                part = proj_ref[half, pl.ds(tile * fold + k, seqs, stride=rows), :]
                merged = jnp.where(place == k, part, merged)
            merged = merged * mask[:, tile * LANES:(tile + 1) * LANES]
            out_ref[tile * seqs:(tile + 1) * seqs, :] = merged.astype(BF16)


def load_kernel(x_hbm, flag_hbm, scale_hbm, shift_hbm, wl_hbm, bl_hbm, wr_hbm, br_hbm, last_hbm,
                x_ref, flag_ref, weight_ref, vector_ref, spreader_ref, mask_ref,
                scale_ref, shift_ref, wl_ref, bl_ref, wr_ref, br_ref, last_ref, sems):
    copies = [
        pltpu.make_async_copy(src, dst, sems.at[k])
        for k, (src, dst) in enumerate((
            (x_hbm, x_ref), (flag_hbm, flag_ref), (scale_hbm, scale_ref), (shift_hbm, shift_ref),
            (wl_hbm, wl_ref), (bl_hbm, bl_ref), (wr_hbm, wr_ref), (br_hbm, br_ref), (last_hbm, last_ref),
        ))
    ]
    for copy in copies:
        copy.start()
    for copy in copies[1:]:
        copy.wait()
    width, depth = wl_ref.shape
    fold = LANES // width
    weight_ref[...] = jnp.concatenate([wl_ref[...]] * fold + [wr_ref[...]] * fold, axis=0)
    bias = [bl_ref[...].reshape(1, width)] * fold + [br_ref[...].reshape(1, width)] * fold
    vector_ref[...] = jnp.concatenate(
        [
            scale_ref[...].reshape(1, depth),
            shift_ref[...].reshape(1, depth),
            jnp.concatenate(bias, axis=1),
            jnp.concatenate([last_ref[...].reshape(1, LANES)] * (depth // LANES), axis=1),
            jnp.zeros((4, depth), F32),
        ],
        axis=0,
    )
    shape = spreader_ref.shape
    spreader_ref[...] = (iota(shape, 1) // width == iota(shape, 0)).astype(BF16)
    mask_ref[...] = spread_mask(flag_ref, spreader_ref)
    copies[0].wait()


def spread_mask(flag_ref, spreader_ref):
    return dot(flag_ref[...].astype(F32).astype(BF16), spreader_ref[...], TN)


def project_kernel(width, own_x_ref, own_flag_ref, other_x_ref, other_flag_ref, weight_ref, vector_ref,
                   spreader_ref, own_mask_ref, left_ref, right_ref, own_proj_ref, other_proj_ref):
    seqs, rows, _ = own_x_ref.shape
    lanes = rows * width
    data = lanes // LANES * seqs
    block = lax.axis_index("seq")
    core = block % CORES
    place = iota((seqs, LANES), 1) // width
    for x_ref, mask_of, proj_ref, at in (
        (own_x_ref, lambda: own_mask_ref[...], own_proj_ref, core),
        (other_x_ref, lambda: spread_mask(other_flag_ref, spreader_ref), other_proj_ref, 1 - core),
    ):
        here = pl.ds(pl.multiple_of(at * data, data), data)
        project_block(
            width, x_ref, mask_of, weight_ref[...], vector_ref[...], place,
            left_ref.at[here], right_ref.at[here], proj_ref,
        )
    own, other = (
        jnp.concatenate([ref[...].astype(F32)] * (LANES // seqs), axis=1) for ref in (own_flag_ref, other_flag_ref)
    )
    for tile in range((left_ref.shape[0] - CORES * data) // rows):
        lane_block = iota((rows, LANES), 1) // seqs + tile * (LANES // seqs)
        placed = jnp.where(lane_block == block, own, jnp.where(lane_block == block + 1 - 2 * core, other, 0.0)).astype(BF16)
        first = CORES * data + tile * rows
        for out_ref in (left_ref, right_ref):
            out_ref[first:first + rows, :] = placed


def whole_mask(pieces, rows, data):
    total = functools.reduce(jnp.add, [p[CORES * data:, :] for p in pieces])
    return jnp.concatenate([total[k:k + rows] for k in range(0, total.shape[0], rows)], axis=1)


def left_kernel(steps, seqs, rows, width, *refs):
    lefts, (out_ref, mask_ref, left_ref, turned_ref) = refs[:-4], refs[-4:]
    data = rows * width // LANES * seqs
    me_res, me_seq = lax.axis_index("res"), lax.axis_index("seq")
    order = [sending_chip(step, me_res, me_seq) for step in steps]
    for k, piece in enumerate(lefts):
        chip = me_seq // CORES ^ k
        slot = sum(jnp.where(there == chip, place, 0) for place, there in enumerate(order))
        for core in range(CORES):
            at = pl.multiple_of((slot * CORES + core) * seqs, seqs)
            for tile in range(data // seqs):
                left_ref[pl.ds(at, seqs), tile * LANES:(tile + 1) * LANES] = (
                    piece[core * data + tile * seqs:core * data + (tile + 1) * seqs, :]
                )
    mask_ref[...] = whole_mask(lefts, rows, data)
    for tile in range(turned_ref.shape[0]):
        turned_ref[tile] = left_ref[tile * LANES:(tile + 1) * LANES, :].astype(F32).T
        for c in range(width):
            out_ref[c * rows:(c + 1) * rows, tile * LANES:(tile + 1) * LANES] = (
                turned_ref[tile, pl.ds(c, rows, stride=width), :].astype(BF16)
            )


def pair_kernel(seqs, rows, columns, width, *refs):
    rights = refs[:-6]
    turned_ref, live_ref, w_ref, vector_ref, out_ref, flat_ref = refs[-6:]
    fold = LANES // width
    assert fold == 4
    data = rows * width // LANES * seqs

    count = dot(live_ref[...], whole_mask(rights, rows, data), NT)
    scale = 1.0 / (1.0 + count)
    scales = [jnp.broadcast_to(scale[:, j:j + 1], (rows, w_ref.shape[1])) for j in range(columns)]
    right = jnp.concatenate(
        [
            jnp.concatenate(
                [p[core * data + t * seqs:core * data + (t + 1) * seqs, :] for t in range(data // seqs)], axis=1
            )
            for p in rights
            for core in range(CORES)
        ],
        axis=0,
    )
    outer = dot(turned_ref[...], right).astype(BF16)

    place = (iota((rows, LANES), 1) // width).astype(BF16)
    even = [None] * fold
    even[1] = (place == 0.0) | (place == 2.0)
    even[2] = (place == 0.0) | (place == 1.0)
    for quad in range(width // fold):
        for tile in range(columns // fold):
            part = [
                outer[(quad * fold + k) * rows:(quad * fold + k + 1) * rows, tile * LANES:(tile + 1) * LANES]
                for k in range(fold)
            ]
            for step in (2, 1):
                new = list(part)
                for k in range(fold):
                    if k & step == 0:
                        x, y = part[k], part[k + step]
                        new[k] = jnp.where(even[step], x, pltpu.roll(y, step * width, 1))
                        new[k + step] = jnp.where(even[step], pltpu.roll(x, LANES - step * width, 1), y)
                part = new
            for k in range(fold):
                j = tile * fold + k
                flat_ref[j * rows:(j + 1) * rows, quad * LANES:(quad + 1) * LANES] = part[k]

    raw = dot(flat_ref[...], w_ref[...]) + vector_ref[3:4, :LANES]
    scaled = [raw[j * rows:(j + 1) * rows, :] * scales[j] for j in range(columns)]
    out_ref[...] = jnp.swapaxes(jnp.stack(scaled, axis=0), 0, 1).astype(BF16)


def local(n, x, flags, scale, shift, wl, bl, wr, br, w, bias):
    seqs, rows, depth = x.shape
    width = wl.shape[1]
    outs = w.shape[1]
    lanes = rows * width
    size = CORES * lanes // LANES * seqs + rows * pl.cdiv(n * seqs, LANES)
    axes = ("res", "seq")
    flags = flags.T

    swap = [(p, p ^ 1) for p in range(n)]
    other_x, other_flags = lax.ppermute(x, "seq", swap), lax.ppermute(flags, "seq", swap)

    operands = [
        pltpu.with_memory_space_constraint(o, pltpu.HBM) for o in (x, flags, scale, shift, wl.T, bl, wr.T, br, bias)
    ]
    own_x, own_flags, weight, vectors, spreader, own_mask = pl.pallas_call(
        load_kernel,
        out_shape=(
            jax.ShapeDtypeStruct(x.shape, x.dtype),
            jax.ShapeDtypeStruct(flags.shape, flags.dtype),
            jax.ShapeDtypeStruct((2 * LANES, depth), BF16),
            jax.ShapeDtypeStruct((8, 2 * LANES), F32),
            jax.ShapeDtypeStruct((rows, lanes), BF16),
            jax.ShapeDtypeStruct((seqs, lanes), F32),
        ),
        in_specs=[pl.BlockSpec(memory_space=pltpu.HBM)] * len(operands),
        scratch_shapes=[pltpu.VMEM(o.shape, o.dtype) for o in operands[2:]]
        + [pltpu.SemaphoreType.DMA((len(operands),))],
        compiler_params=pltpu.CompilerParams(vmem_limit_bytes=16 << 20),
        cost_estimate=pl.CostEstimate(flops=1 << 25, bytes_accessed=x.size * 8, transcendentals=0),
        name="load",
    )(*operands)
    wire = jax.ShapeDtypeStruct((size, LANES), BF16)
    left, right = pl.pallas_call(
        functools.partial(project_kernel, width),
        out_shape=(wire, wire),
        scratch_shapes=[pltpu.VMEM((2, seqs * rows, LANES), F32)] * 2,
        compiler_params=pltpu.CompilerParams(vmem_limit_bytes=16 << 20),
        name="project",
    )(own_x, own_flags, other_x, other_flags, weight, vectors, spreader, own_mask)

    steps = right_routes(n)
    lefts = [left] + [
        lax.ppermute(left, axes, [(a * n + p, a * n + step[a][p]) for a in range(n) for p in range(n)])
        for step in left_routes(n)
    ]
    rights = [
        lax.ppermute(right, axes, [(a * n + p, step[a][p] * n + a) for a in range(n) for p in range(n)])
        for step in steps
    ]
    turned, live = pl.pallas_call(
        functools.partial(left_kernel, steps, seqs, rows, width),
        out_shape=(jax.ShapeDtypeStruct((lanes, n * seqs), BF16), jax.ShapeDtypeStruct((rows, n * seqs), BF16)),
        scratch_shapes=[
            pltpu.VMEM((n * seqs, lanes), BF16),
            pltpu.VMEM((n * seqs // LANES, lanes, LANES), F32),
        ],
        compiler_params=pltpu.CompilerParams(vmem_limit_bytes=16 << 20),
        name="turn_left",
    )(*lefts)
    return pl.pallas_call(
        functools.partial(pair_kernel, seqs, rows, rows, width),
        out_shape=jax.ShapeDtypeStruct((rows, rows, outs), BF16),
        scratch_shapes=[
            pltpu.VMEM((rows * rows, width * width), BF16),
        ],
        compiler_params=pltpu.CompilerParams(vmem_limit_bytes=16 << 20),
        name="pair",
    )(*rights, turned, live, w, vectors)


def solution(mesh):
    n = mesh.shape["res"]
    assert n == mesh.shape["seq"] and n & (n - 1) == 0 and n % CORES == 0
    in_specs = (P(("group", "seq"), "res", None), P(("group", "seq"), "res")) + (P(),) * 8
    return jax.shard_map(
        functools.partial(local, n), mesh=mesh, in_specs=in_specs,
        out_specs=P(("group", "res"), "seq", None), check_vma=False,
    )
```

```python
import functools

import jax
import jax.numpy as jnp
from jax import lax
from jax.experimental import pallas as pl
from jax.experimental.pallas import tpu as pltpu
from jax.sharding import PartitionSpec as P

LANES = 128
CORES = 2
F32 = jnp.float32
BF16 = jnp.bfloat16
TN = (((0,), (0,)), ((), ()))
NT = (((1,), (1,)), ((), ()))
NN = (((1,), (0,)), ((), ()))


def dot(a, b, dims=NN):
    return lax.dot_general(a, b, dims, preferred_element_type=F32)


def iota(shape, dim):
    return lax.broadcasted_iota(jnp.int32, shape, dim)


RIGHT = (
    ((1, 0, 2, 3), (1, 0, 2, 3), (1, 3, 0, 2), (2, 1, 3, 0)),
    ((3, 2, 0, 1), (2, 3, 0, 1), (0, 2, 3, 1), (3, 0, 1, 2)),
)
LEFT = ((2, 3, 1, 0), (3, 2, 0, 1), (3, 2, 1, 0), (3, 2, 0, 1))


def right_routes(n):
    if n == 4:
        return RIGHT
    steps = [m for m in range(n) if bin(m).count("1") % 2 == 1]
    return tuple(tuple(tuple(p ^ m for p in range(n)) for a in range(n)) for m in steps)


def left_routes(n):
    if n == 4:
        return (LEFT,)
    return tuple(tuple(tuple(p ^ k * CORES for p in range(n)) for a in range(n)) for k in range(1, n // CORES))


def sending_chip(step, r, q):
    n = len(step)
    chip = 0
    for bit in range((n // CORES - 1).bit_length()):
        for a in range(n):
            word = sum((step[a].index(to) // CORES >> bit & 1) << to for to in range(n))
            chip = chip | jnp.where(q == a, (jnp.int32(word) >> r & 1) << bit, 0)
    return chip


def project_block(width, x_ref, mask_of, weight, vectors, place, left_ref, right_ref, proj_ref):
    seqs, rows, depth = x_ref.shape
    fold = LANES // width
    lanes = rows * width
    data = lanes // LANES * seqs
    x = x_ref[...].astype(F32).reshape(seqs * rows, depth)
    center = jnp.mean(x, axis=-1, keepdims=True)
    x = x - center
    spread = jnp.mean(x * x, axis=-1, keepdims=True)
    normed = x * lax.rsqrt(spread + 1e-05) * vectors[0:1] + vectors[1:2]
    both = dot(normed.astype(BF16), weight, NT) + vectors[2:3]
    proj_ref[0] = both[:, :LANES]
    proj_ref[1] = both[:, LANES:]

    mask = mask_of()
    for half, out_ref in ((0, left_ref), (1, right_ref)):
        for tile in range(rows // fold):
            merged = proj_ref[half, pl.ds(tile * fold, seqs, stride=rows), :]
            for k in range(1, fold):
                part = proj_ref[half, pl.ds(tile * fold + k, seqs, stride=rows), :]
                merged = jnp.where(place == k, part, merged)
            merged = merged * mask[:, tile * LANES:(tile + 1) * LANES]
            out_ref[tile * seqs:(tile + 1) * seqs, :] = merged.astype(BF16)


def load_kernel(x_hbm, flag_hbm, scale_hbm, shift_hbm, wl_hbm, bl_hbm, wr_hbm, br_hbm, last_hbm,
                x_ref, flag_ref, weight_ref, vector_ref, spreader_ref, mask_ref,
                scale_ref, shift_ref, wl_ref, bl_ref, wr_ref, br_ref, last_ref, sems):
    copies = [
        pltpu.make_async_copy(src, dst, sems.at[k])
        for k, (src, dst) in enumerate((
            (x_hbm, x_ref), (flag_hbm, flag_ref), (scale_hbm, scale_ref), (shift_hbm, shift_ref),
            (wl_hbm, wl_ref), (bl_hbm, bl_ref), (wr_hbm, wr_ref), (br_hbm, br_ref), (last_hbm, last_ref),
        ))
    ]
    for copy in copies:
        copy.start()
    for copy in copies[1:]:
        copy.wait()
    width, depth = wl_ref.shape
    fold = LANES // width
    weight_ref[...] = jnp.concatenate([wl_ref[...]] * fold + [wr_ref[...]] * fold, axis=0)
    bias = [bl_ref[...].reshape(1, width)] * fold + [br_ref[...].reshape(1, width)] * fold
    vector_ref[...] = jnp.concatenate(
        [
            scale_ref[...].reshape(1, depth),
            shift_ref[...].reshape(1, depth),
            jnp.concatenate(bias, axis=1),
            jnp.concatenate([last_ref[...].reshape(1, LANES)] * (depth // LANES), axis=1),
            jnp.zeros((4, depth), F32),
        ],
        axis=0,
    )
    shape = spreader_ref.shape
    spreader_ref[...] = (iota(shape, 1) // width == iota(shape, 0)).astype(BF16)
    mask_ref[...] = spread_mask(flag_ref, spreader_ref)
    copies[0].wait()


def spread_mask(flag_ref, spreader_ref):
    return dot(flag_ref[...].astype(F32).astype(BF16), spreader_ref[...], TN)


def project_kernel(width, own_x_ref, own_flag_ref, other_x_ref, other_flag_ref, weight_ref, vector_ref,
                   spreader_ref, own_mask_ref, left_ref, right_ref, own_proj_ref, other_proj_ref):
    seqs, rows, _ = own_x_ref.shape
    lanes = rows * width
    data = lanes // LANES * seqs
    block = lax.axis_index("seq")
    core = block % CORES
    own, other = (
        jnp.concatenate([ref[...].astype(F32)] * (LANES // seqs), axis=1) for ref in (own_flag_ref, other_flag_ref)
    )
    for tile in range((left_ref.shape[0] - CORES * data) // rows):
        lane_block = iota((rows, LANES), 1) // seqs + tile * (LANES // seqs)
        placed = jnp.where(lane_block == block, own, jnp.where(lane_block == block + 1 - 2 * core, other, 0.0)).astype(BF16)
        first = CORES * data + tile * rows
        for out_ref in (left_ref, right_ref):
            out_ref[first:first + rows, :] = placed

    place = iota((seqs, LANES), 1) // width
    for x_ref, mask_of, proj_ref, at in (
        (own_x_ref, lambda: own_mask_ref[...], own_proj_ref, core),
        (other_x_ref, lambda: spread_mask(other_flag_ref, spreader_ref), other_proj_ref, 1 - core),
    ):
        here = pl.ds(pl.multiple_of(at * data, data), data)
        project_block(
            width, x_ref, mask_of, weight_ref[...], vector_ref[...], place,
            left_ref.at[here], right_ref.at[here], proj_ref,
        )


def whole_mask(pieces, rows, data):
    total = functools.reduce(jnp.add, [p[CORES * data:, :] for p in pieces])
    return jnp.concatenate([total[k:k + rows] for k in range(0, total.shape[0], rows)], axis=1)


def left_kernel(steps, seqs, rows, width, *refs):
    lefts, (out_ref, mask_ref, left_ref, turned_ref) = refs[:-4], refs[-4:]
    data = rows * width // LANES * seqs
    me_res, me_seq = lax.axis_index("res"), lax.axis_index("seq")
    order = [sending_chip(step, me_res, me_seq) for step in steps]
    for k, piece in enumerate(lefts):
        chip = me_seq // CORES ^ k
        slot = sum(jnp.where(there == chip, place, 0) for place, there in enumerate(order))
        for core in range(CORES):
            at = pl.multiple_of((slot * CORES + core) * seqs, seqs)
            for tile in range(data // seqs):
                left_ref[pl.ds(at, seqs), tile * LANES:(tile + 1) * LANES] = (
                    piece[core * data + tile * seqs:core * data + (tile + 1) * seqs, :]
                )
    mask_ref[...] = whole_mask(lefts, rows, data)
    for tile in range(turned_ref.shape[0]):
        turned_ref[tile] = left_ref[tile * LANES:(tile + 1) * LANES, :].astype(F32).T
        for c in range(width):
            out_ref[c * rows:(c + 1) * rows, tile * LANES:(tile + 1) * LANES] = (
                turned_ref[tile, pl.ds(c, rows, stride=width), :].astype(BF16)
            )


def pair_kernel(seqs, rows, columns, width, *refs):
    rights = refs[:-6]
    turned_ref, live_ref, w_ref, vector_ref, out_ref, flat_ref = refs[-6:]
    fold = LANES // width
    assert fold == 4
    data = rows * width // LANES * seqs

    count = dot(live_ref[...], whole_mask(rights, rows, data), NT)
    scale = 1.0 / (1.0 + count)
    scales = [jnp.broadcast_to(scale[:, j:j + 1], (rows, w_ref.shape[1])) for j in range(columns)]
    right = jnp.concatenate(
        [
            jnp.concatenate(
                [p[core * data + t * seqs:core * data + (t + 1) * seqs, :] for t in range(data // seqs)], axis=1
            )
            for p in rights
            for core in range(CORES)
        ],
        axis=0,
    )
    outer = dot(turned_ref[...], right).astype(BF16)

    place = (iota((rows, LANES), 1) // width).astype(BF16)
    even = [None] * fold
    even[1] = (place == 0.0) | (place == 2.0)
    even[2] = (place == 0.0) | (place == 1.0)
    for quad in range(width // fold):
        for tile in range(columns // fold):
            part = [
                outer[(quad * fold + k) * rows:(quad * fold + k + 1) * rows, tile * LANES:(tile + 1) * LANES]
                for k in range(fold)
            ]
            for step in (2, 1):
                new = list(part)
                for k in range(fold):
                    if k & step == 0:
                        x, y = part[k], part[k + step]
                        new[k] = jnp.where(even[step], x, pltpu.roll(y, step * width, 1))
                        new[k + step] = jnp.where(even[step], pltpu.roll(x, LANES - step * width, 1), y)
                part = new
            for k in range(fold):
                j = tile * fold + k
                flat_ref[j * rows:(j + 1) * rows, quad * LANES:(quad + 1) * LANES] = part[k]

    raw = dot(flat_ref[...], w_ref[...]) + vector_ref[3:4, :LANES]
    scaled = [raw[j * rows:(j + 1) * rows, :] * scales[j] for j in range(columns)]
    out_ref[...] = jnp.swapaxes(jnp.stack(scaled, axis=0), 0, 1).astype(BF16)


def local(n, x, flags, scale, shift, wl, bl, wr, br, w, bias):
    seqs, rows, depth = x.shape
    width = wl.shape[1]
    outs = w.shape[1]
    lanes = rows * width
    size = CORES * lanes // LANES * seqs + rows * pl.cdiv(n * seqs, LANES)
    axes = ("res", "seq")
    flags = flags.T

    swap = [(p, p ^ 1) for p in range(n)]
    other_x, other_flags = lax.ppermute(x, "seq", swap), lax.ppermute(flags, "seq", swap)

    operands = [
        pltpu.with_memory_space_constraint(o, pltpu.HBM) for o in (x, flags, scale, shift, wl.T, bl, wr.T, br, bias)
    ]
    own_x, own_flags, weight, vectors, spreader, own_mask = pl.pallas_call(
        load_kernel,
        out_shape=(
            jax.ShapeDtypeStruct(x.shape, x.dtype),
            jax.ShapeDtypeStruct(flags.shape, flags.dtype),
            jax.ShapeDtypeStruct((2 * LANES, depth), BF16),
            jax.ShapeDtypeStruct((8, 2 * LANES), F32),
            jax.ShapeDtypeStruct((rows, lanes), BF16),
            jax.ShapeDtypeStruct((seqs, lanes), F32),
        ),
        in_specs=[pl.BlockSpec(memory_space=pltpu.HBM)] * len(operands),
        scratch_shapes=[pltpu.VMEM(o.shape, o.dtype) for o in operands[2:]]
        + [pltpu.SemaphoreType.DMA((len(operands),))],
        compiler_params=pltpu.CompilerParams(vmem_limit_bytes=16 << 20),
        cost_estimate=pl.CostEstimate(flops=1 << 25, bytes_accessed=x.size * 8, transcendentals=0),
        name="load",
    )(*operands)
    wire = jax.ShapeDtypeStruct((size, LANES), BF16)
    left, right = pl.pallas_call(
        functools.partial(project_kernel, width),
        out_shape=(wire, wire),
        scratch_shapes=[pltpu.VMEM((2, seqs * rows, LANES), F32)] * 2,
        compiler_params=pltpu.CompilerParams(vmem_limit_bytes=16 << 20),
        name="project",
    )(own_x, own_flags, other_x, other_flags, weight, vectors, spreader, own_mask)

    steps = right_routes(n)
    lefts = [left] + [
        lax.ppermute(left, axes, [(a * n + p, a * n + step[a][p]) for a in range(n) for p in range(n)])
        for step in left_routes(n)
    ]
    rights = [
        lax.ppermute(right, axes, [(a * n + p, step[a][p] * n + a) for a in range(n) for p in range(n)])
        for step in steps
    ]
    turned, live = pl.pallas_call(
        functools.partial(left_kernel, steps, seqs, rows, width),
        out_shape=(jax.ShapeDtypeStruct((lanes, n * seqs), BF16), jax.ShapeDtypeStruct((rows, n * seqs), BF16)),
        scratch_shapes=[
            pltpu.VMEM((n * seqs, lanes), BF16),
            pltpu.VMEM((n * seqs // LANES, lanes, LANES), F32),
        ],
        compiler_params=pltpu.CompilerParams(vmem_limit_bytes=16 << 20),
        name="turn_left",
    )(*lefts)
    return pl.pallas_call(
        functools.partial(pair_kernel, seqs, rows, rows, width),
        out_shape=jax.ShapeDtypeStruct((rows, rows, outs), BF16),
        scratch_shapes=[
            pltpu.VMEM((rows * rows, width * width), BF16),
        ],
        compiler_params=pltpu.CompilerParams(vmem_limit_bytes=16 << 20),
        name="pair",
    )(*rights, turned, live, w, vectors)


def solution(mesh):
    n = mesh.shape["res"]
    assert n == mesh.shape["seq"] and n & (n - 1) == 0 and n % CORES == 0
    in_specs = (P(("group", "seq"), "res", None), P(("group", "seq"), "res")) + (P(),) * 8
    return jax.shard_map(
        functools.partial(local, n), mesh=mesh, in_specs=in_specs,
        out_specs=P(("group", "res"), "seq", None), check_vma=False,
    )
```

```python
import functools

import jax
import jax.numpy as jnp
from jax import lax
from jax.experimental import pallas as pl
from jax.experimental.pallas import tpu as pltpu
from jax.sharding import PartitionSpec as P

LANES = 128
CORES = 2
F32 = jnp.float32
BF16 = jnp.bfloat16
TN = (((0,), (0,)), ((), ()))
NT = (((1,), (1,)), ((), ()))
NN = (((1,), (0,)), ((), ()))


def dot(a, b, dims=NN):
    return lax.dot_general(a, b, dims, preferred_element_type=F32)


def iota(shape, dim):
    return lax.broadcasted_iota(jnp.int32, shape, dim)


RIGHT = (
    ((1, 0, 2, 3), (1, 0, 2, 3), (1, 3, 0, 2), (2, 1, 3, 0)),
    ((3, 2, 0, 1), (2, 3, 0, 1), (0, 2, 3, 1), (3, 0, 1, 2)),
)
LEFT = ((2, 3, 1, 0), (3, 2, 0, 1), (3, 2, 1, 0), (3, 2, 0, 1))


def right_routes(n):
    if n == 4:
        return RIGHT
    steps = [m for m in range(n) if bin(m).count("1") % 2 == 1]
    return tuple(tuple(tuple(p ^ m for p in range(n)) for a in range(n)) for m in steps)


def left_routes(n):
    if n == 4:
        return (LEFT,)
    return tuple(tuple(tuple(p ^ k * CORES for p in range(n)) for a in range(n)) for k in range(1, n // CORES))


def sending_chip(step, r, q):
    n = len(step)
    chip = 0
    for bit in range((n // CORES - 1).bit_length()):
        for a in range(n):
            word = sum((step[a].index(to) // CORES >> bit & 1) << to for to in range(n))
            chip = chip | jnp.where(q == a, (jnp.int32(word) >> r & 1) << bit, 0)
    return chip


def project_block(width, x_ref, mask_of, weight, vectors, place, left_ref, right_ref, proj_ref):
    seqs, rows, depth = x_ref.shape
    fold = LANES // width
    lanes = rows * width
    data = lanes // LANES * seqs
    x = x_ref[...].astype(F32).reshape(seqs * rows, depth)
    center = jnp.mean(x, axis=-1, keepdims=True)
    x = x - center
    spread = jnp.mean(x * x, axis=-1, keepdims=True)
    normed = x * lax.rsqrt(spread + 1e-05) * vectors[0:1] + vectors[1:2]
    both = dot(normed.astype(BF16), weight, NT) + vectors[2:3]
    proj_ref[0] = both[:, :LANES]
    proj_ref[1] = both[:, LANES:]

    mask = mask_of()
    for half, out_ref in ((0, left_ref), (1, right_ref)):
        for tile in range(rows // fold):
            merged = proj_ref[half, pl.ds(tile * fold, seqs, stride=rows), :]
            for k in range(1, fold):
                part = proj_ref[half, pl.ds(tile * fold + k, seqs, stride=rows), :]
                merged = jnp.where(place == k, part, merged)
            merged = merged * mask[:, tile * LANES:(tile + 1) * LANES]
            out_ref[tile * seqs:(tile + 1) * seqs, :] = merged.astype(BF16)


def load_kernel(x_hbm, flag_hbm, scale_hbm, shift_hbm, wl_hbm, bl_hbm, wr_hbm, br_hbm, last_hbm,
                x_ref, flag_ref, weight_ref, vector_ref, spreader_ref, mask_ref,
                scale_ref, shift_ref, wl_ref, bl_ref, wr_ref, br_ref, last_ref, sems):
    copies = [
        pltpu.make_async_copy(src, dst, sems.at[k])
        for k, (src, dst) in enumerate((
            (x_hbm, x_ref), (flag_hbm, flag_ref), (scale_hbm, scale_ref), (shift_hbm, shift_ref),
            (wl_hbm, wl_ref), (bl_hbm, bl_ref), (wr_hbm, wr_ref), (br_hbm, br_ref), (last_hbm, last_ref),
        ))
    ]
    for copy in copies:
        copy.start()
    for copy in copies[1:]:
        copy.wait()
    width, depth = wl_ref.shape
    fold = LANES // width
    weight_ref[...] = jnp.concatenate([wl_ref[...]] * fold + [wr_ref[...]] * fold, axis=0)
    bias = [bl_ref[...].reshape(1, width)] * fold + [br_ref[...].reshape(1, width)] * fold
    vector_ref[...] = jnp.concatenate(
        [
            scale_ref[...].reshape(1, depth),
            shift_ref[...].reshape(1, depth),
            jnp.concatenate(bias, axis=1),
            jnp.concatenate([last_ref[...].reshape(1, LANES)] * (depth // LANES), axis=1),
            jnp.zeros((4, depth), F32),
        ],
        axis=0,
    )
    shape = spreader_ref.shape
    spreader_ref[...] = (iota(shape, 1) // width == iota(shape, 0)).astype(BF16)
    mask_ref[...] = spread_mask(flag_ref, spreader_ref)
    copies[0].wait()


def spread_mask(flag_ref, spreader_ref):
    return dot(flag_ref[...].astype(F32).astype(BF16), spreader_ref[...], TN)


def project_kernel(width, own_x_ref, own_flag_ref, other_x_ref, other_flag_ref, weight_ref, vector_ref,
                   spreader_ref, own_mask_ref, left_ref, right_ref, own_proj_ref, other_proj_ref):
    seqs, rows, _ = own_x_ref.shape
    lanes = rows * width
    data = lanes // LANES * seqs
    block = lax.axis_index("seq")
    core = block % CORES
    own, other = (
        jnp.concatenate([ref[...].astype(F32)] * (LANES // seqs), axis=1) for ref in (own_flag_ref, other_flag_ref)
    )
    for tile in range((left_ref.shape[0] - CORES * data) // rows):
        lane_block = iota((rows, LANES), 1) // seqs + tile * (LANES // seqs)
        placed = jnp.where(lane_block == block, own, jnp.where(lane_block == block + 1 - 2 * core, other, 0.0)).astype(BF16)
        first = CORES * data + tile * rows
        for out_ref in (left_ref, right_ref):
            out_ref[first:first + rows, :] = placed

    place = iota((seqs, LANES), 1) // width
    for x_ref, mask_of, proj_ref, at in (
        (other_x_ref, lambda: spread_mask(other_flag_ref, spreader_ref), other_proj_ref, 1 - core),
        (own_x_ref, lambda: own_mask_ref[...], own_proj_ref, core),
    ):
        here = pl.ds(pl.multiple_of(at * data, data), data)
        project_block(
            width, x_ref, mask_of, weight_ref[...], vector_ref[...], place,
            left_ref.at[here], right_ref.at[here], proj_ref,
        )


def whole_mask(pieces, rows, data):
    total = functools.reduce(jnp.add, [p[CORES * data:, :] for p in pieces])
    return jnp.concatenate([total[k:k + rows] for k in range(0, total.shape[0], rows)], axis=1)


def left_kernel(steps, seqs, rows, width, *refs):
    lefts, (out_ref, mask_ref, left_ref, turned_ref) = refs[:-4], refs[-4:]
    data = rows * width // LANES * seqs
    me_res, me_seq = lax.axis_index("res"), lax.axis_index("seq")
    order = [sending_chip(step, me_res, me_seq) for step in steps]
    for k, piece in enumerate(lefts):
        chip = me_seq // CORES ^ k
        slot = sum(jnp.where(there == chip, place, 0) for place, there in enumerate(order))
        for core in range(CORES):
            at = pl.multiple_of((slot * CORES + core) * seqs, seqs)
            for tile in range(data // seqs):
                left_ref[pl.ds(at, seqs), tile * LANES:(tile + 1) * LANES] = (
                    piece[core * data + tile * seqs:core * data + (tile + 1) * seqs, :]
                )
    mask_ref[...] = whole_mask(lefts, rows, data)
    for tile in range(turned_ref.shape[0]):
        turned_ref[tile] = left_ref[tile * LANES:(tile + 1) * LANES, :].astype(F32).T
        for c in range(width):
            out_ref[c * rows:(c + 1) * rows, tile * LANES:(tile + 1) * LANES] = (
                turned_ref[tile, pl.ds(c, rows, stride=width), :].astype(BF16)
            )


def pair_kernel(seqs, rows, columns, width, *refs):
    rights = refs[:-6]
    turned_ref, live_ref, w_ref, vector_ref, out_ref, flat_ref = refs[-6:]
    fold = LANES // width
    assert fold == 4
    data = rows * width // LANES * seqs

    count = dot(live_ref[...], whole_mask(rights, rows, data), NT)
    scale = 1.0 / (1.0 + count)
    scales = [jnp.broadcast_to(scale[:, j:j + 1], (rows, w_ref.shape[1])) for j in range(columns)]
    right = jnp.concatenate(
        [
            jnp.concatenate(
                [p[core * data + t * seqs:core * data + (t + 1) * seqs, :] for t in range(data // seqs)], axis=1
            )
            for p in rights
            for core in range(CORES)
        ],
        axis=0,
    )
    outer = dot(turned_ref[...], right).astype(BF16)

    place = (iota((rows, LANES), 1) // width).astype(BF16)
    even = [None] * fold
    even[1] = (place == 0.0) | (place == 2.0)
    even[2] = (place == 0.0) | (place == 1.0)
    for quad in range(width // fold):
        for tile in range(columns // fold):
            part = [
                outer[(quad * fold + k) * rows:(quad * fold + k + 1) * rows, tile * LANES:(tile + 1) * LANES]
                for k in range(fold)
            ]
            for step in (2, 1):
                new = list(part)
                for k in range(fold):
                    if k & step == 0:
                        x, y = part[k], part[k + step]
                        new[k] = jnp.where(even[step], x, pltpu.roll(y, step * width, 1))
                        new[k + step] = jnp.where(even[step], pltpu.roll(x, LANES - step * width, 1), y)
                part = new
            for k in range(fold):
                j = tile * fold + k
                flat_ref[j * rows:(j + 1) * rows, quad * LANES:(quad + 1) * LANES] = part[k]

    raw = dot(flat_ref[...], w_ref[...]) + vector_ref[3:4, :LANES]
    scaled = [raw[j * rows:(j + 1) * rows, :] * scales[j] for j in range(columns)]
    out_ref[...] = jnp.swapaxes(jnp.stack(scaled, axis=0), 0, 1).astype(BF16)


def local(n, x, flags, scale, shift, wl, bl, wr, br, w, bias):
    seqs, rows, depth = x.shape
    width = wl.shape[1]
    outs = w.shape[1]
    lanes = rows * width
    size = CORES * lanes // LANES * seqs + rows * pl.cdiv(n * seqs, LANES)
    axes = ("res", "seq")
    flags = flags.T

    swap = [(p, p ^ 1) for p in range(n)]
    other_x, other_flags = lax.ppermute(x, "seq", swap), lax.ppermute(flags, "seq", swap)

    operands = [
        pltpu.with_memory_space_constraint(o, pltpu.HBM) for o in (x, flags, scale, shift, wl.T, bl, wr.T, br, bias)
    ]
    own_x, own_flags, weight, vectors, spreader, own_mask = pl.pallas_call(
        load_kernel,
        out_shape=(
            jax.ShapeDtypeStruct(x.shape, x.dtype),
            jax.ShapeDtypeStruct(flags.shape, flags.dtype),
            jax.ShapeDtypeStruct((2 * LANES, depth), BF16),
            jax.ShapeDtypeStruct((8, 2 * LANES), F32),
            jax.ShapeDtypeStruct((rows, lanes), BF16),
            jax.ShapeDtypeStruct((seqs, lanes), F32),
        ),
        in_specs=[pl.BlockSpec(memory_space=pltpu.HBM)] * len(operands),
        scratch_shapes=[pltpu.VMEM(o.shape, o.dtype) for o in operands[2:]]
        + [pltpu.SemaphoreType.DMA((len(operands),))],
        compiler_params=pltpu.CompilerParams(vmem_limit_bytes=16 << 20),
        cost_estimate=pl.CostEstimate(flops=1 << 25, bytes_accessed=x.size * 8, transcendentals=0),
        name="load",
    )(*operands)
    wire = jax.ShapeDtypeStruct((size, LANES), BF16)
    left, right = pl.pallas_call(
        functools.partial(project_kernel, width),
        out_shape=(wire, wire),
        scratch_shapes=[pltpu.VMEM((2, seqs * rows, LANES), F32)] * 2,
        compiler_params=pltpu.CompilerParams(vmem_limit_bytes=16 << 20),
        name="project",
    )(own_x, own_flags, other_x, other_flags, weight, vectors, spreader, own_mask)

    steps = right_routes(n)
    lefts = [left] + [
        lax.ppermute(left, axes, [(a * n + p, a * n + step[a][p]) for a in range(n) for p in range(n)])
        for step in left_routes(n)
    ]
    rights = [
        lax.ppermute(right, axes, [(a * n + p, step[a][p] * n + a) for a in range(n) for p in range(n)])
        for step in steps
    ]
    turned, live = pl.pallas_call(
        functools.partial(left_kernel, steps, seqs, rows, width),
        out_shape=(jax.ShapeDtypeStruct((lanes, n * seqs), BF16), jax.ShapeDtypeStruct((rows, n * seqs), BF16)),
        scratch_shapes=[
            pltpu.VMEM((n * seqs, lanes), BF16),
            pltpu.VMEM((n * seqs // LANES, lanes, LANES), F32),
        ],
        compiler_params=pltpu.CompilerParams(vmem_limit_bytes=16 << 20),
        name="turn_left",
    )(*lefts)
    return pl.pallas_call(
        functools.partial(pair_kernel, seqs, rows, rows, width),
        out_shape=jax.ShapeDtypeStruct((rows, rows, outs), BF16),
        scratch_shapes=[
            pltpu.VMEM((rows * rows, width * width), BF16),
        ],
        compiler_params=pltpu.CompilerParams(vmem_limit_bytes=16 << 20),
        name="pair",
    )(*rights, turned, live, w, vectors)


def solution(mesh):
    n = mesh.shape["res"]
    assert n == mesh.shape["seq"] and n & (n - 1) == 0 and n % CORES == 0
    in_specs = (P(("group", "seq"), "res", None), P(("group", "seq"), "res")) + (P(),) * 8
    return jax.shard_map(
        functools.partial(local, n), mesh=mesh, in_specs=in_specs,
        out_specs=P(("group", "res"), "seq", None), check_vma=False,
    )
```

```python
import functools

import jax
import jax.numpy as jnp
from jax import lax
from jax.experimental import pallas as pl
from jax.experimental.pallas import tpu as pltpu
from jax.sharding import PartitionSpec as P

LANES = 128
CORES = 2
F32 = jnp.float32
BF16 = jnp.bfloat16
TN = (((0,), (0,)), ((), ()))
NT = (((1,), (1,)), ((), ()))
NN = (((1,), (0,)), ((), ()))


def dot(a, b, dims=NN):
    return lax.dot_general(a, b, dims, preferred_element_type=F32)


def iota(shape, dim):
    return lax.broadcasted_iota(jnp.int32, shape, dim)


RIGHT = (
    ((1, 0, 2, 3), (1, 0, 2, 3), (1, 3, 0, 2), (2, 1, 3, 0)),
    ((3, 2, 0, 1), (2, 3, 0, 1), (0, 2, 3, 1), (3, 0, 1, 2)),
)
LEFT = ((2, 3, 1, 0), (3, 2, 0, 1), (3, 2, 1, 0), (3, 2, 0, 1))


def right_routes(n):
    if n == 4:
        return RIGHT
    steps = [m for m in range(n) if bin(m).count("1") % 2 == 1]
    return tuple(tuple(tuple(p ^ m for p in range(n)) for a in range(n)) for m in steps)


def left_routes(n):
    if n == 4:
        return (LEFT,)
    return tuple(tuple(tuple(p ^ k * CORES for p in range(n)) for a in range(n)) for k in range(1, n // CORES))


def sending_chip(step, r, q):
    n = len(step)
    chip = 0
    for bit in range((n // CORES - 1).bit_length()):
        for a in range(n):
            word = sum((step[a].index(to) // CORES >> bit & 1) << to for to in range(n))
            chip = chip | jnp.where(q == a, (jnp.int32(word) >> r & 1) << bit, 0)
    return chip


def project_block(width, x_ref, mask_of, weight, vectors, place, left_ref, right_ref, proj_ref):
    seqs, rows, depth = x_ref.shape
    fold = LANES // width
    lanes = rows * width
    data = lanes // LANES * seqs
    x = x_ref[...].astype(F32).reshape(seqs * rows, depth)
    center = jnp.mean(x, axis=-1, keepdims=True)
    x = x - center
    spread = jnp.mean(x * x, axis=-1, keepdims=True)
    normed = x * lax.rsqrt(spread + 1e-05) * vectors[0:1] + vectors[1:2]
    both = dot(normed.astype(BF16), weight, NT) + vectors[2:3]
    proj_ref[0] = both[:, :LANES]
    proj_ref[1] = both[:, LANES:]

    mask = mask_of()
    for half, out_ref in ((0, left_ref), (1, right_ref)):
        for tile in range(rows // fold):
            merged = proj_ref[half, pl.ds(tile * fold, seqs, stride=rows), :]
            for k in range(1, fold):
                part = proj_ref[half, pl.ds(tile * fold + k, seqs, stride=rows), :]
                merged = jnp.where(place == k, part, merged)
            merged = merged * mask[:, tile * LANES:(tile + 1) * LANES]
            out_ref[tile * seqs:(tile + 1) * seqs, :] = merged.astype(BF16)


def load_kernel(x_hbm, flag_hbm, scale_hbm, shift_hbm, wl_hbm, bl_hbm, wr_hbm, br_hbm, last_hbm,
                x_ref, flag_ref, weight_ref, vector_ref, spreader_ref, mask_ref,
                scale_ref, shift_ref, wl_ref, bl_ref, wr_ref, br_ref, last_ref, sems):
    copies = [
        pltpu.make_async_copy(src, dst, sems.at[k])
        for k, (src, dst) in enumerate((
            (x_hbm, x_ref), (flag_hbm, flag_ref), (scale_hbm, scale_ref), (shift_hbm, shift_ref),
            (wl_hbm, wl_ref), (bl_hbm, bl_ref), (wr_hbm, wr_ref), (br_hbm, br_ref), (last_hbm, last_ref),
        ))
    ]
    for copy in copies:
        copy.start()
    for copy in copies[1:]:
        copy.wait()
    width, depth = wl_ref.shape
    fold = LANES // width
    weight_ref[...] = jnp.concatenate([wl_ref[...]] * fold + [wr_ref[...]] * fold, axis=0)
    bias = [bl_ref[...].reshape(1, width)] * fold + [br_ref[...].reshape(1, width)] * fold
    vector_ref[...] = jnp.concatenate(
        [
            scale_ref[...].reshape(1, depth),
            shift_ref[...].reshape(1, depth),
            jnp.concatenate(bias, axis=1),
            jnp.concatenate([last_ref[...].reshape(1, LANES)] * (depth // LANES), axis=1),
            jnp.zeros((4, depth), F32),
        ],
        axis=0,
    )
    shape = spreader_ref.shape
    spreader_ref[...] = (iota(shape, 1) // width == iota(shape, 0)).astype(BF16)
    mask_ref[...] = spread_mask(flag_ref, spreader_ref)
    copies[0].wait()


def spread_mask(flag_ref, spreader_ref):
    return dot(flag_ref[...].astype(F32).astype(BF16), spreader_ref[...], TN)


def project_kernel(width, own_x_ref, own_flag_ref, other_x_ref, other_flag_ref, weight_ref, vector_ref,
                   spreader_ref, own_mask_ref, left_ref, right_ref, own_proj_ref, other_proj_ref):
    seqs, rows, _ = own_x_ref.shape
    lanes = rows * width
    data = lanes // LANES * seqs
    block = lax.axis_index("seq")
    core = block % CORES
    own, other = (
        jnp.concatenate([ref[...].astype(F32)] * (LANES // seqs), axis=1) for ref in (own_flag_ref, other_flag_ref)
    )
    for tile in range((left_ref.shape[0] - CORES * data) // rows):
        lane_block = iota((rows, LANES), 1) // seqs + tile * (LANES // seqs)
        placed = jnp.where(lane_block == block, own, jnp.where(lane_block == block + 1 - 2 * core, other, 0.0)).astype(BF16)
        first = CORES * data + tile * rows
        for out_ref in (left_ref, right_ref):
            out_ref[first:first + rows, :] = placed

    place = iota((seqs, LANES), 1) // width
    for x_ref, mask_of, proj_ref, at in (
        (own_x_ref, lambda: own_mask_ref[...], own_proj_ref, core),
        (other_x_ref, lambda: spread_mask(other_flag_ref, spreader_ref), other_proj_ref, 1 - core),
    ):
        here = pl.ds(pl.multiple_of(at * data, data), data)
        project_block(
            width, x_ref, mask_of, weight_ref[...], vector_ref[...], place,
            left_ref.at[here], right_ref.at[here], proj_ref,
        )


def whole_mask(pieces, rows, data):
    total = functools.reduce(jnp.add, [p[CORES * data:, :] for p in pieces])
    return jnp.concatenate([total[k:k + rows] for k in range(0, total.shape[0], rows)], axis=1)


def left_kernel(steps, seqs, rows, width, *refs):
    lefts, (out_ref, mask_ref, left_ref, turned_ref) = refs[:-4], refs[-4:]
    data = rows * width // LANES * seqs
    me_res, me_seq = lax.axis_index("res"), lax.axis_index("seq")
    order = [sending_chip(step, me_res, me_seq) for step in steps]
    for k, piece in enumerate(lefts):
        chip = me_seq // CORES ^ k
        slot = sum(jnp.where(there == chip, place, 0) for place, there in enumerate(order))
        for core in range(CORES):
            at = pl.multiple_of((slot * CORES + core) * seqs, seqs)
            for tile in range(data // seqs):
                left_ref[pl.ds(at, seqs), tile * LANES:(tile + 1) * LANES] = (
                    piece[core * data + tile * seqs:core * data + (tile + 1) * seqs, :]
                )
    mask_ref[...] = whole_mask(lefts, rows, data)
    for tile in range(turned_ref.shape[0]):
        turned_ref[tile] = left_ref[tile * LANES:(tile + 1) * LANES, :].astype(F32).T
        for c in range(width):
            out_ref[c * rows:(c + 1) * rows, tile * LANES:(tile + 1) * LANES] = (
                turned_ref[tile, pl.ds(c, rows, stride=width), :].astype(BF16)
            )


def pair_kernel(seqs, rows, columns, width, *refs):
    rights = refs[:-6]
    turned_ref, live_ref, w_ref, vector_ref, out_ref, flat_ref = refs[-6:]
    fold = LANES // width
    assert fold == 4
    data = rows * width // LANES * seqs

    count = dot(live_ref[...], whole_mask(rights, rows, data), NT)
    scale = 1.0 / (1.0 + count)
    scales = [jnp.broadcast_to(scale[:, j:j + 1], (rows, w_ref.shape[1])) for j in range(columns)]
    right = jnp.concatenate(
        [
            jnp.concatenate(
                [p[core * data + t * seqs:core * data + (t + 1) * seqs, :] for t in range(data // seqs)], axis=1
            )
            for p in rights
            for core in range(CORES)
        ],
        axis=0,
    )
    outer = dot(turned_ref[...], right).astype(BF16)

    place = (iota((rows, LANES), 1) // width).astype(BF16)
    even = [None] * fold
    even[1] = (place == 0.0) | (place == 2.0)
    even[2] = (place == 0.0) | (place == 1.0)
    for quad in range(width // fold):
        for tile in range(columns // fold):
            part = [
                outer[(quad * fold + k) * rows:(quad * fold + k + 1) * rows, tile * LANES:(tile + 1) * LANES]
                for k in range(fold)
            ]
            for step in (2, 1):
                new = list(part)
                for k in range(fold):
                    if k & step == 0:
                        x, y = part[k], part[k + step]
                        new[k] = jnp.where(even[step], x, pltpu.roll(y, step * width, 1))
                        new[k + step] = jnp.where(even[step], pltpu.roll(x, LANES - step * width, 1), y)
                part = new
            for k in range(fold):
                j = tile * fold + k
                flat_ref[j * rows:(j + 1) * rows, quad * LANES:(quad + 1) * LANES] = part[k]

    raw = dot(flat_ref[...], w_ref[...]) + vector_ref[3:4, :LANES]
    scaled = [(raw[j * rows:(j + 1) * rows, :] * scales[j]).astype(BF16) for j in range(columns)]
    out_ref[...] = jnp.swapaxes(jnp.stack(scaled, axis=0), 0, 1)


def local(n, x, flags, scale, shift, wl, bl, wr, br, w, bias):
    seqs, rows, depth = x.shape
    width = wl.shape[1]
    outs = w.shape[1]
    lanes = rows * width
    size = CORES * lanes // LANES * seqs + rows * pl.cdiv(n * seqs, LANES)
    axes = ("res", "seq")
    flags = flags.T

    swap = [(p, p ^ 1) for p in range(n)]
    other_x, other_flags = lax.ppermute(x, "seq", swap), lax.ppermute(flags, "seq", swap)

    operands = [
        pltpu.with_memory_space_constraint(o, pltpu.HBM) for o in (x, flags, scale, shift, wl.T, bl, wr.T, br, bias)
    ]
    own_x, own_flags, weight, vectors, spreader, own_mask = pl.pallas_call(
        load_kernel,
        out_shape=(
            jax.ShapeDtypeStruct(x.shape, x.dtype),
            jax.ShapeDtypeStruct(flags.shape, flags.dtype),
            jax.ShapeDtypeStruct((2 * LANES, depth), BF16),
            jax.ShapeDtypeStruct((8, 2 * LANES), F32),
            jax.ShapeDtypeStruct((rows, lanes), BF16),
            jax.ShapeDtypeStruct((seqs, lanes), F32),
        ),
        in_specs=[pl.BlockSpec(memory_space=pltpu.HBM)] * len(operands),
        scratch_shapes=[pltpu.VMEM(o.shape, o.dtype) for o in operands[2:]]
        + [pltpu.SemaphoreType.DMA((len(operands),))],
        compiler_params=pltpu.CompilerParams(vmem_limit_bytes=16 << 20),
        cost_estimate=pl.CostEstimate(flops=1 << 25, bytes_accessed=x.size * 8, transcendentals=0),
        name="load",
    )(*operands)
    wire = jax.ShapeDtypeStruct((size, LANES), BF16)
    left, right = pl.pallas_call(
        functools.partial(project_kernel, width),
        out_shape=(wire, wire),
        scratch_shapes=[pltpu.VMEM((2, seqs * rows, LANES), F32)] * 2,
        compiler_params=pltpu.CompilerParams(vmem_limit_bytes=16 << 20),
        name="project",
    )(own_x, own_flags, other_x, other_flags, weight, vectors, spreader, own_mask)

    steps = right_routes(n)
    lefts = [left] + [
        lax.ppermute(left, axes, [(a * n + p, a * n + step[a][p]) for a in range(n) for p in range(n)])
        for step in left_routes(n)
    ]
    rights = [
        lax.ppermute(right, axes, [(a * n + p, step[a][p] * n + a) for a in range(n) for p in range(n)])
        for step in steps
    ]
    turned, live = pl.pallas_call(
        functools.partial(left_kernel, steps, seqs, rows, width),
        out_shape=(jax.ShapeDtypeStruct((lanes, n * seqs), BF16), jax.ShapeDtypeStruct((rows, n * seqs), BF16)),
        scratch_shapes=[
            pltpu.VMEM((n * seqs, lanes), BF16),
            pltpu.VMEM((n * seqs // LANES, lanes, LANES), F32),
        ],
        compiler_params=pltpu.CompilerParams(vmem_limit_bytes=16 << 20),
        name="turn_left",
    )(*lefts)
    return pl.pallas_call(
        functools.partial(pair_kernel, seqs, rows, rows, width),
        out_shape=jax.ShapeDtypeStruct((rows, rows, outs), BF16),
        scratch_shapes=[
            pltpu.VMEM((rows * rows, width * width), BF16),
        ],
        compiler_params=pltpu.CompilerParams(vmem_limit_bytes=16 << 20),
        name="pair",
    )(*rights, turned, live, w, vectors)


def solution(mesh):
    n = mesh.shape["res"]
    assert n == mesh.shape["seq"] and n & (n - 1) == 0 and n % CORES == 0
    in_specs = (P(("group", "seq"), "res", None), P(("group", "seq"), "res")) + (P(),) * 8
    return jax.shard_map(
        functools.partial(local, n), mesh=mesh, in_specs=in_specs,
        out_specs=P(("group", "res"), "seq", None), check_vma=False,
    )
```
